32 devices in a mesh: blk: 8 (over y, x, core), tp: 4 (over z).
Axes of the slice: x: 2, y: 2, z: 4, core: 2. Of those that a mesh axis runs over, the one named last changes fastest.
Arguments:
- hidden_in: bfloat16 [4096, 1536], P('blk'), may hold values from -6 to 6
- out_grad: bfloat16 [4096, 1536], P('blk'), may hold values from -6 to 6
- lengths: int32 [5], replicated, may hold values from 1 to 2560, as said below
- attn_gain: float32 [1536], replicated, may hold values from 0.5 to 1.5
- w_query: bfloat16 [1536, 1536], P(None, 'tp'), may hold values from -0.15625 to 0.15625
- key_projection_weight: bfloat16 [1536, 768], P(None, 'tp'), may hold values from -0.15625 to 0.15625
- value_projection_weight: bfloat16 [1536, 768], P(None, 'tp'), may hold values from -0.15625 to 0.15625
- w_out: bfloat16 [1536, 1536], P('tp'), may hold values from -6 to 6
- mlp_gain: float32 [1536], replicated, may hold values from 0.5 to 1.5
- w_gate: bfloat16 [1536, 4096], P(None, 'tp'), may hold values from -0.15625 to 0.15625
- w_up: bfloat16 [1536, 4096], P(None, 'tp'), may hold values from -0.15625 to 0.15625
- w_down: bfloat16 [4096, 1536], P('tp'), may hold values from -0.375 to 0.375
Outputs:
- layer_out: bfloat16 [4096, 1536], P('blk')
- input_grad: bfloat16 [4096, 1536], P('blk')
- grad_query: float32 [1536, 1536], P('blk', 'tp')
- grad_key: float32 [1536, 768], P('blk', 'tp')
- grad_value: float32 [1536, 768], P('blk', 'tp')
- grad_out: float32 [1536, 1536], P('tp', 'blk')
- grad_gate: float32 [1536, 4096], P('blk', 'tp')
- grad_up: float32 [1536, 4096], P('blk', 'tp')
- grad_down: float32 [4096, 1536], P('tp', 'blk')
- grad_attn_gain: float32 [1536], P('blk')
- grad_mlp_gain: float32 [1536], P('blk')
The draws below stay inside these ranges and needn't reach their ends.
Inputs may be any that keep to these rules, and one draw needn't show every extreme that they name: The lengths sum to 4096. The first entry is a piece of 1 to min(512, 512) - 1 tokens drawn from the seed and the last entry is 512 minus it; of the entries between, exactly one, at a place drawn from the seed, is 2560 and all others are 512.
All inputs are finite; a program needn't handle non-finite values.
Results may differ from the reference program's by a relative error of at most 0.03.
Values may be sent and summed in bfloat16 or wider, within the bound.
A program may use at most 192 MiB of HBM per device.

```python
import jax
import jax.numpy as jnp
from jax import lax

MODEL_WIDTH = 1536
QUERY_HEADS = 16
KEY_VALUE_HEADS = 8
HEAD_SIZE = 96
FF = 4096
BLOCK_TOKENS = 512
SHORT = 512
STREAM_TOKENS = 4096
LONG_LEN = 2560
NDOC = 5


def draw_lengths(key, part):
    key = jax.random.fold_in(key, 11)
    key_offset, key_place = jax.random.split(key, 2)
    smallest = min(SHORT, BLOCK_TOKENS)
    offset = jax.random.randint(key_offset, (), 1, smallest).astype(jnp.int32)
    middle_count = NDOC - 2
    long_at = jax.random.randint(key_place, (), 1, middle_count + 1).astype(jnp.int32)
    places = jnp.arange(NDOC, dtype=jnp.int32)
    short_fill = jnp.full((NDOC,), SHORT, jnp.int32)
    with_long = jnp.where(places == long_at, LONG_LEN, short_fill)
    with_head = jnp.where(places == 0, offset, with_long)
    return jnp.where(places == NDOC - 1, SHORT - offset, with_head).astype(jnp.int32)


def block_levels(stream_key, shape, cuts, low, high):
    def one(position, blocks):
        heights = jax.random.uniform(jax.random.fold_in(jax.random.fold_in(stream_key, 6), position), (blocks,), jnp.float32, low / len(cuts), high / len(cuts))
        return jnp.repeat(jnp.exp(heights), shape[position] // blocks).reshape((-1,) + (1,) * (len(shape) - position - 1))

    level = one(*cuts[0])
    for cut in cuts[1:]:
        level = level * one(*cut)
    return level


def centred(key, shape, width, most, cuts=(), kind=jnp.bfloat16):
    entries = width * jax.random.normal(key, shape, jnp.float32)
    if cuts:
        entries = entries * block_levels(key, shape, cuts, -0.22, 0.18)
    return jnp.clip(entries, -most, most).astype(kind)


def setup_inputs(seed: int = 0) -> dict:
    key_of = jax.random.split(jax.random.key(seed), 13)
    return {
        "hidden_in": centred(key_of[0], (STREAM_TOKENS, MODEL_WIDTH), 1.0, 6.0, ((0, 8),)),
        "out_grad": centred(key_of[1], (STREAM_TOKENS, MODEL_WIDTH), 1.0, 6.0, ((0, 8),)),
        "lengths": draw_lengths(jax.random.fold_in(key_of[12], 71), 0),
        "attn_gain": jnp.clip(1.0 + 0.1 * jax.random.normal(key_of[3], (MODEL_WIDTH,), jnp.float32), 0.5, 1.5),
        "w_query": centred(key_of[4], (MODEL_WIDTH, QUERY_HEADS * HEAD_SIZE), MODEL_WIDTH ** -0.5, 0.15625, ((1, 4),)),
        "key_projection_weight": centred(key_of[5], (MODEL_WIDTH, KEY_VALUE_HEADS * HEAD_SIZE), MODEL_WIDTH ** -0.5, 0.15625, ((1, 4),)),
        "value_projection_weight": centred(key_of[6], (MODEL_WIDTH, KEY_VALUE_HEADS * HEAD_SIZE), MODEL_WIDTH ** -0.5, 0.15625, ((1, 4),)),
        "w_out": centred(key_of[7], (QUERY_HEADS * HEAD_SIZE, MODEL_WIDTH), 1.0, 6.0, ((0, 4),)),
        "mlp_gain": jnp.clip(1.0 + 0.1 * jax.random.normal(key_of[8], (MODEL_WIDTH,), jnp.float32), 0.5, 1.5),
        "w_gate": centred(key_of[9], (MODEL_WIDTH, FF), MODEL_WIDTH ** -0.5, 0.15625, ((1, 4),)),
        "w_up": centred(key_of[10], (MODEL_WIDTH, FF), MODEL_WIDTH ** -0.5, 0.15625, ((1, 4),)),
        "w_down": centred(key_of[11], (FF, MODEL_WIDTH), (FF // 16) ** -0.5, 0.375, ((0, 4),)),
    }


norm_eps = 1e-05
rope_base = 100000.0
neg_fill = -1e+30

@jax.custom_vjp
def reduced_precision(v):
    return lax.optimization_barrier(v.astype(jnp.bfloat16)).astype(jnp.float32)

@jax.custom_vjp
def reduced_precision_backward(v):
    return v

def low_keep(v):
    return (reduced_precision(v), None)

def low_pass(kept, grad):
    return (grad,)

def back_keep(v):
    return (v, None)

def back_low(kept, grad):
    return (reduced_precision(grad),)
reduced_precision.defvjp(low_keep, low_pass)
reduced_precision_backward.defvjp(back_keep, back_low)

def matrix_multiply(left_side, right_side):
    return jnp.dot(left_side, right_side, precision=lax.Precision.HIGHEST, preferred_element_type=jnp.float32)

def doc_places(lengths, places):
    doc_ends = jnp.cumsum(lengths).astype(jnp.int32)
    passed = (places[:, None] >= doc_ends[None, :]).astype(jnp.int32)
    segment = lax.optimization_barrier(jnp.sum(passed, axis=1)).astype(jnp.int32)
    preceding = lax.optimization_barrier(jnp.sum(passed * lengths[None, :], axis=1)).astype(jnp.int32)
    return (segment, (places - preceding).astype(jnp.int32))

def apply_rotary(values, token_position, heads):
    half_size = HEAD_SIZE // 2
    freqs = rope_base ** (-(2.0 * jnp.arange(half_size, dtype=jnp.float32)) / HEAD_SIZE)
    angle = token_position.astype(jnp.float32)[:, None] * freqs[None, :]
    cosine = jnp.cos(angle)[:, None, :]
    sine = jnp.sin(angle)[:, None, :]
    shaped = values.reshape(values.shape[0], heads, HEAD_SIZE)
    first_half = shaped[..., :half_size]
    second_half = shaped[..., half_size:]
    turned = jnp.concatenate([first_half * cosine - second_half * sine, second_half * cosine + first_half * sine], axis=-1)
    return turned.reshape(values.shape[0], heads * HEAD_SIZE)

def rms_norm(values, gain):
    return values * lax.rsqrt(lax.optimization_barrier(jnp.mean(values * values, axis=-1, keepdims=True)) + norm_eps) * gain

def attention(query_tensor, key, value_tensor, segment, places):
    query_group_size = QUERY_HEADS // KEY_VALUE_HEADS
    score_scale = HEAD_SIZE ** (-0.5)
    gathered_keys = key.reshape(STREAM_TOKENS, KEY_VALUE_HEADS, HEAD_SIZE)
    gathered_values = value_tensor.reshape(STREAM_TOKENS, KEY_VALUE_HEADS, HEAD_SIZE)
    count_of_blocks = STREAM_TOKENS // BLOCK_TOKENS
    query_block_list = query_tensor.reshape(count_of_blocks, BLOCK_TOKENS, KEY_VALUE_HEADS, query_group_size, HEAD_SIZE)
    seg_blocks = segment.reshape(count_of_blocks, BLOCK_TOKENS)
    place_blocks = places.reshape(count_of_blocks, BLOCK_TOKENS)

    def one_block(inputs):
        query_part, query_seg, query_place = inputs
        scores = jnp.einsum('igrd,jgd->grij', query_part, gathered_keys, precision=lax.Precision.HIGHEST) * score_scale
        scores = reduced_precision_backward(scores)
        allowed = (query_seg[:, None] == segment[None, :]) & (places[None, :] <= query_place[:, None])
        scores = jnp.where(allowed[None, None], scores, neg_fill)
        probs = jax.nn.softmax(scores, axis=-1)
        mixed = jnp.einsum('grij,jgd->igrd', reduced_precision(probs), gathered_values, precision=lax.Precision.HIGHEST)
        return mixed.reshape(BLOCK_TOKENS, QUERY_HEADS * HEAD_SIZE)
    outputs = lax.map(jax.checkpoint(one_block), (query_block_list, seg_blocks, place_blocks))
    return outputs.reshape(STREAM_TOKENS, QUERY_HEADS * HEAD_SIZE)

def layer(hidden_in, attn_gain, w_query, key_projection_weight, value_projection_weight, w_out, mlp_gain, w_gate, w_up, w_down, segment, token_position, places):
    first_layer_norm = reduced_precision(rms_norm(hidden_in, attn_gain))
    query_tensor = reduced_precision(apply_rotary(reduced_precision_backward(matrix_multiply(first_layer_norm, w_query)), token_position, QUERY_HEADS))
    key = reduced_precision(apply_rotary(reduced_precision_backward(matrix_multiply(first_layer_norm, key_projection_weight)), token_position, KEY_VALUE_HEADS))
    value_tensor = reduced_precision(reduced_precision_backward(matrix_multiply(first_layer_norm, value_projection_weight)))
    mixed = attention(query_tensor, key, value_tensor, segment, places)
    branch = reduced_precision_backward(matrix_multiply(reduced_precision(reduced_precision_backward(mixed)), w_out))
    middle = hidden_in + branch
    ln_two = reduced_precision(rms_norm(middle, mlp_gain))
    gate = reduced_precision_backward(matrix_multiply(ln_two, w_gate))
    up_proj = reduced_precision_backward(matrix_multiply(ln_two, w_up))
    hidden = reduced_precision(jax.nn.silu(gate) * up_proj)
    return middle + matrix_multiply(hidden, w_down)

def reference(hidden_in, out_grad, lengths, attn_gain, w_query, key_projection_weight, value_projection_weight, w_out, mlp_gain, w_gate, w_up, w_down):
    places = jnp.arange(STREAM_TOKENS, dtype=jnp.int32)
    segment, token_position = doc_places(lengths, places)
    floats = [arg.astype(jnp.float32) for arg in (hidden_in, attn_gain, w_query, key_projection_weight, value_projection_weight, w_out, mlp_gain, w_gate, w_up, w_down)]

    def forward(*weights):
        return layer(*weights, segment, token_position, places)
    layer_out, pull_back = jax.vjp(forward, *floats)
    grads = pull_back(out_grad.astype(jnp.float32))
    return (layer_out.astype(jnp.bfloat16), grads[0].astype(jnp.bfloat16), grads[2], grads[3], grads[4], grads[5], grads[7], grads[8], grads[9], grads[1], grads[6])
```

```python
import functools

import jax
import jax.numpy as jnp
from jax import lax
from jax.experimental import pallas as pl
from jax.experimental.pallas import tpu as pltpu
from jax.sharding import PartitionSpec as P

HEAD_SIZE = 96


norm_eps = 1e-05
rope_base = 100000.0
neg_fill = -1e30


def doc_places(lengths, places):
    doc_ends = jnp.cumsum(lengths)
    passed = (places[:, None] >= doc_ends[None, :]).astype(jnp.int32)
    segment = jnp.sum(passed, axis=1)
    preceding = jnp.sum(passed * lengths[None, :], axis=1)
    return (segment, places - preceding)


def apply_rotary(values, token_position, heads, sign_value):
    half_size = HEAD_SIZE // 2
    freqs = rope_base ** (-(2.0 * jnp.arange(half_size, dtype=jnp.float32)) / HEAD_SIZE)
    angle = token_position.astype(jnp.float32)[:, None] * freqs[None, :]
    cosine = jnp.cos(angle)[:, None, :]
    sine = sign_value * jnp.sin(angle)[:, None, :]
    shaped = values.reshape(values.shape[0], heads, HEAD_SIZE)
    first_half = shaped[..., :half_size]
    second_half = shaped[..., half_size:]
    turned = jnp.concatenate(
        [first_half * cosine - second_half * sine, second_half * cosine + first_half * sine],
        axis=-1,
    )
    return turned.reshape(values.shape[0], heads * HEAD_SIZE)


def rms_parts(values):
    inverse = lax.rsqrt(jnp.mean(values * values, axis=-1, keepdims=True) + norm_eps)
    return (values * inverse, inverse)


def norm_back(grad_in, normed, inverse, gain):
    scaled = grad_in * gain
    grad_values = inverse * (scaled - normed * jnp.mean(scaled * normed, axis=-1, keepdims=True))
    return (grad_values, jnp.sum(grad_in * normed, axis=0))


def left_product(left_side, right_side):
    return lax.dot_general(
        left_side, right_side, (((0,), (0,)), ((), ())), preferred_element_type=jnp.float32
    )


def right_product(left_side, weight):
    return lax.dot_general(
        left_side, weight, (((1,), (1,)), ((), ())), preferred_element_type=jnp.float32
    )


def score_block(query_four, key_rows, query_seg, query_place, key_seg, key_place):
    score_scale = HEAD_SIZE ** (-0.5)
    scores = (
        jnp.einsum("igrd,jgd->grij", query_four, key_rows, preferred_element_type=jnp.float32)
        * score_scale
    )
    allowed = (query_seg[:, None] == key_seg[None, :]) & (
        key_place[None, :] <= query_place[:, None]
    )
    return (jnp.where(allowed[None, None], scores, neg_fill), allowed)


def score_grads(
    query_four,
    grad_four,
    log_sum,
    delta,
    query_seg,
    query_place,
    key_rows,
    value_rows,
    key_seg,
    key_place,
):
    scores, allowed = score_block(query_four, key_rows, query_seg, query_place, key_seg, key_place)
    probs = jnp.where(allowed[None, None], jnp.exp(scores - log_sum[..., None]), 0.0)
    grad_probs = jnp.einsum(
        "igrd,jgd->grij", grad_four, value_rows, preferred_element_type=jnp.float32
    )
    grad_scores = (probs * (grad_probs - delta[..., None])).astype(jnp.bfloat16)
    return (grad_scores, probs.astype(jnp.bfloat16))


def keep_same(running):
    return running


def shards(
    hidden_in,
    out_grad,
    lengths,
    attn_gain,
    w_query,
    key_projection_weight,
    value_projection_weight,
    w_out,
    mlp_gain,
    w_gate,
    w_up,
    w_down,
):
    row_count = hidden_in.shape[0]
    cycle_size = lax.axis_size("blk")
    first_row = lax.axis_index("blk") * row_count
    offsets = jnp.arange(row_count, dtype=jnp.int32)
    places = first_row + offsets
    segment, token_position = doc_places(lengths, places)
    q_heads = w_query.shape[1] // HEAD_SIZE
    kv_heads = key_projection_weight.shape[1] // HEAD_SIZE
    query_group_size = q_heads // kv_heads
    kv_width = kv_heads * HEAD_SIZE
    score_scale = HEAD_SIZE ** (-0.5)
    hidden_f = hidden_in.astype(jnp.float32)
    normed_one, inverse_one = rms_parts(hidden_f)
    first_layer_norm = (normed_one * attn_gain).astype(jnp.bfloat16)
    query_raw = jnp.dot(first_layer_norm, w_query, preferred_element_type=jnp.float32)
    key_raw = jnp.dot(first_layer_norm, key_projection_weight, preferred_element_type=jnp.float32)
    value_raw = jnp.dot(
        first_layer_norm, value_projection_weight, preferred_element_type=jnp.float32
    )
    query_low = apply_rotary(query_raw, token_position, q_heads, 1.0).astype(jnp.bfloat16)
    key_low = apply_rotary(key_raw, token_position, kv_heads, 1.0).astype(jnp.bfloat16)
    value_low = value_raw.astype(jnp.bfloat16)
    kv_rows = jnp.concatenate([key_low, value_low], axis=1)
    query_four = query_low.reshape(row_count, kv_heads, query_group_size, HEAD_SIZE)

    def split_kv(piece, block_step):
        block_rows = lax.dynamic_slice_in_dim(piece, block_step * row_count, row_count, 0)
        key_rows = block_rows[:, :kv_width].reshape(row_count, kv_heads, HEAD_SIZE)
        value_rows = block_rows[:, kv_width:].reshape(row_count, kv_heads, HEAD_SIZE)
        return (key_rows, value_rows)

    start_max = jnp.full((kv_heads, query_group_size, row_count), neg_fill, jnp.float32)
    start_sum = jnp.zeros((kv_heads, query_group_size, row_count), jnp.float32)
    start_acc = jnp.zeros((kv_heads, query_group_size, row_count, HEAD_SIZE), jnp.float32)
    piece = lax.all_gather(kv_rows, "blk", axis=0, tiled=True)

    def forward_one_step(block_step, running):
        key_start = block_step * row_count

        def forward_work(running):
            row_max, row_sum, weighted = running
            key_rows, value_rows = split_kv(piece, block_step)
            key_place = key_start + offsets
            key_seg, _ = doc_places(lengths, key_place)
            scores, allowed = score_block(query_four, key_rows, segment, places, key_seg, key_place)
            new_max = jnp.maximum(row_max, jnp.max(scores, axis=-1))
            exp_scores = jnp.where(allowed[None, None], jnp.exp(scores - new_max[..., None]), 0.0)
            rescale = jnp.exp(row_max - new_max)
            row_sum = row_sum * rescale + jnp.sum(exp_scores, axis=-1)
            weighted = weighted * rescale[..., None] + jnp.einsum(
                "grij,jgd->grid",
                exp_scores.astype(jnp.bfloat16),
                value_rows,
                preferred_element_type=jnp.float32,
            )
            return (new_max, row_sum, weighted)

        return lax.cond(key_start <= first_row, forward_work, keep_same, running)

    row_max, row_sum, weighted = lax.fori_loop(
        0, piece.shape[0] // row_count, forward_one_step, (start_max, start_sum, start_acc)
    )
    attn_four = weighted / row_sum[..., None]
    log_sum = row_max + jnp.log(row_sum)
    attn_rows = jnp.transpose(attn_four, (2, 0, 1, 3)).reshape(row_count, q_heads * HEAD_SIZE)
    attn_low = attn_rows.astype(jnp.bfloat16)
    branch = lax.psum(jnp.dot(attn_low, w_out, preferred_element_type=jnp.float32), "tp")
    middle = hidden_f + branch
    normed_two, inverse_two = rms_parts(middle)
    ln_two = (normed_two * mlp_gain).astype(jnp.bfloat16)
    gate = jnp.dot(ln_two, w_gate, preferred_element_type=jnp.float32)
    up_proj = jnp.dot(ln_two, w_up, preferred_element_type=jnp.float32)
    sig_gate = jax.nn.sigmoid(gate)
    act_gate = gate * sig_gate
    hidden = (act_gate * up_proj).astype(jnp.bfloat16)
    mlp_branch = lax.psum(jnp.dot(hidden, w_down, preferred_element_type=jnp.float32), "tp")
    layer_out = (middle + mlp_branch).astype(jnp.bfloat16)
    grad_down = left_product(hidden, out_grad)
    grad_hidden = right_product(out_grad, w_down)
    grad_gate_act = (grad_hidden * up_proj * sig_gate * (1.0 + gate * (1.0 - sig_gate))).astype(
        jnp.bfloat16
    )
    grad_up_act = (grad_hidden * act_gate).astype(jnp.bfloat16)
    grad_gate = left_product(ln_two, grad_gate_act)
    grad_up = left_product(ln_two, grad_up_act)
    grad_ln_two = lax.psum(
        right_product(grad_gate_act, w_gate) + right_product(grad_up_act, w_up), "tp"
    )
    grad_middle_norm, grad_mlp_gain = norm_back(grad_ln_two, normed_two, inverse_two, mlp_gain)
    grad_middle = out_grad.astype(jnp.float32) + grad_middle_norm
    grad_branch = grad_middle.astype(jnp.bfloat16)
    grad_out = left_product(attn_low, grad_branch)
    grad_attn = right_product(grad_branch, w_out).astype(jnp.bfloat16)
    grad_four = grad_attn.reshape(row_count, kv_heads, query_group_size, HEAD_SIZE)
    delta = jnp.sum(jnp.transpose(grad_four.astype(jnp.float32), (1, 2, 0, 3)) * attn_four, axis=-1)

    def query_grads(grad_scores, key_rows):
        return (
            jnp.einsum("grij,jgd->grid", grad_scores, key_rows, preferred_element_type=jnp.float32)
            * score_scale
        )

    def key_value_grads(grad_scores, probs_low, query_rows, grad_rows):
        grad_keys = (
            jnp.einsum(
                "grij,igrd->jgd", grad_scores, query_rows, preferred_element_type=jnp.float32
            )
            * score_scale
        )
        grad_values = jnp.einsum(
            "grij,igrd->jgd", probs_low, grad_rows, preferred_element_type=jnp.float32
        )
        return jnp.concatenate(
            [grad_keys.reshape(row_count, kv_width), grad_values.reshape(row_count, kv_width)],
            axis=1,
        )

    start_dq = jnp.zeros((kv_heads, query_group_size, row_count, HEAD_SIZE), jnp.float32)
    start_kv = jnp.zeros((row_count * cycle_size, 2 * kv_width), jnp.float32)
    back_piece = lax.all_gather(kv_rows, "blk", axis=0, tiled=True)

    def back_one_step(block_step, running):
        key_start = block_step * row_count

        def back_work(running):
            grad_query_acc, grad_kv_acc = running
            key_rows, value_rows = split_kv(back_piece, block_step)
            key_place = key_start + offsets
            key_seg, _ = doc_places(lengths, key_place)
            grad_scores, probs_low = score_grads(
                query_four,
                grad_four,
                log_sum,
                delta,
                segment,
                places,
                key_rows,
                value_rows,
                key_seg,
                key_place,
            )
            grad_query_acc = grad_query_acc + query_grads(grad_scores, key_rows)
            earlier = lax.dynamic_slice_in_dim(grad_kv_acc, key_start, row_count, 0)
            added = earlier + key_value_grads(grad_scores, probs_low, query_four, grad_four)
            return (
                grad_query_acc,
                lax.dynamic_update_slice_in_dim(grad_kv_acc, added, key_start, 0),
            )

        return lax.cond(key_start <= first_row, back_work, keep_same, running)

    grad_query_four, grad_kv_all = lax.fori_loop(
        0, back_piece.shape[0] // row_count, back_one_step, (start_dq, start_kv)
    )
    grad_kv = lax.psum_scatter(grad_kv_all, "blk", scatter_dimension=0, tiled=True)
    grad_query_rows = jnp.transpose(grad_query_four, (2, 0, 1, 3)).reshape(
        row_count, q_heads * HEAD_SIZE
    )
    grad_query_low = apply_rotary(grad_query_rows, token_position, q_heads, -1.0).astype(
        jnp.bfloat16
    )
    grad_key_low = apply_rotary(grad_kv[:, :kv_width], token_position, kv_heads, -1.0).astype(
        jnp.bfloat16
    )
    grad_value_low = grad_kv[:, kv_width:].astype(jnp.bfloat16)
    grad_query = left_product(first_layer_norm, grad_query_low)
    grad_key = left_product(first_layer_norm, grad_key_low)
    grad_value = left_product(first_layer_norm, grad_value_low)
    grad_ln_part = (
        right_product(grad_query_low, w_query)
        + right_product(grad_key_low, key_projection_weight)
        + right_product(grad_value_low, value_projection_weight)
    )
    grad_ln_one = lax.psum(grad_ln_part, "tp")
    grad_input_norm, grad_attn_gain = norm_back(grad_ln_one, normed_one, inverse_one, attn_gain)
    input_grad = (grad_middle + grad_input_norm).astype(jnp.bfloat16)
    summed = (
        lax.psum_scatter(grad_query, "blk", scatter_dimension=0, tiled=True),
        lax.psum_scatter(grad_key, "blk", scatter_dimension=0, tiled=True),
        lax.psum_scatter(grad_value, "blk", scatter_dimension=0, tiled=True),
        lax.psum_scatter(grad_out, "blk", scatter_dimension=1, tiled=True),
        lax.psum_scatter(grad_gate, "blk", scatter_dimension=0, tiled=True),
        lax.psum_scatter(grad_up, "blk", scatter_dimension=0, tiled=True),
        lax.psum_scatter(grad_down, "blk", scatter_dimension=1, tiled=True),
        lax.psum_scatter(grad_attn_gain, "blk", scatter_dimension=0, tiled=True),
        lax.psum_scatter(grad_mlp_gain, "blk", scatter_dimension=0, tiled=True),
    )
    return (
        layer_out,
        input_grad,
        summed[0],
        summed[1],
        summed[2],
        summed[3],
        summed[4],
        summed[5],
        summed[6],
        summed[7],
        summed[8],
    )


MESH = pl.DeviceIdType.MESH
F32, BF16 = jnp.float32, jnp.bfloat16
LOG2E = 1.4426950408889634
SCORE_SCALE = HEAD_SIZE**-0.5
VMEM_BYTES = 62 * 2**20
HALF = HEAD_SIZE // 2


def dot_nn(a, b):
    return lax.dot_general(a, b, (((1,), (0,)), ((), ())), preferred_element_type=F32)


def dot_nt(a, b):
    return lax.dot_general(a, b, (((1,), (1,)), ((), ())), preferred_element_type=F32)


def dot_tn(a, b):
    return lax.dot_general(a, b, (((0,), (0,)), ((), ())), preferred_element_type=F32)


class Place:
    def __init__(self):
        self.b = lax.axis_index("blk")
        self.t = lax.axis_index("tp")
        self.core = self.b % 2
        self.chip = self.b // 2
        self.x = self.chip % 2
        self.y = self.b // 4
        self.mate = self.b + 1 - 2 * self.core
        self.inner = jnp.logical_or(self.t == 1, self.t == 2)
        self.outer = jnp.logical_not(self.inner)
        self.pair = self.t + 1 - 2 * (self.t % 2)
        self.across = 3 - self.t

    def slot(self, s):
        core = (self.core + s % 2) % 2
        x = (self.x + (s // 2) % 2) % 2
        y = (self.y + s // 4) % 2
        return (y * 2 + x) * 2 + core

    def chip_at(self, k):
        x = (self.x + (k + 1) % 2) % 2
        y = (self.y + 1 - k // 2) % 2
        return y * 2 + x


def remote(src, dst, ssem, rsem, b, t):
    return pltpu.make_async_remote_copy(
        src_ref=src, dst_ref=dst, send_sem=ssem, recv_sem=rsem, device_id=(b, t), device_id_type=MESH
    )


def enter(me, blk_steps):
    barrier = pltpu.get_barrier_semaphore()
    for s in blk_steps:
        pl.semaphore_signal(barrier, inc=1, device_id=(me.slot(s), me.t), device_id_type=MESH)
    for z in (me.pair, me.across):
        pl.semaphore_signal(barrier, inc=1, device_id=(me.b, z), device_id_type=MESH)
    pl.semaphore_wait(barrier, len(blk_steps) + 2)


class LineSum:
    def __init__(self, me, part, first, second, sems, rows):
        self.me, self.part, self.first, self.second, self.sems, self.rows = (
            me, part, first, second, sems, rows,
        )

    def at(self, ref, p):
        return ref.at[pl.ds(pl.multiple_of(p * self.rows, self.rows), self.rows), :]

    def copy(self, stage, p):
        me = self.me
        src = (self.part, self.part, self.first)[stage]
        dst = (self.first, self.second, self.first)[stage]
        target = (me.pair, me.across, me.pair)[stage]
        return remote(
            self.at(src, p), self.at(dst, p),
            self.sems.at[2 * stage, p], self.sems.at[2 * stage + 1, p], me.b, target,
        )

    def give(self, p):
        @pl.when(self.me.outer)
        def _():
            self.copy(0, p).start()

    def fold(self, p):
        @pl.when(self.me.inner)
        def _():
            self.copy(0, p).wait_recv()
            mine, got = self.at(self.part, p), self.at(self.first, p)
            mine[...] = (mine[...].astype(F32) + got[...].astype(F32)).astype(BF16)
            self.copy(1, p).start()

    def unfold(self, p):
        @pl.when(self.me.inner)
        def _():
            self.copy(1, p).wait_recv()
            mine, got, out = self.at(self.part, p), self.at(self.second, p), self.at(self.first, p)
            out[...] = (mine[...].astype(F32) + got[...].astype(F32)).astype(BF16)
            self.copy(2, p).start()

    def take(self, p):
        @pl.when(self.me.outer)
        def _():
            self.copy(2, p).wait_recv()

    def drain(self, pieces):
        def one(p, carry):
            @pl.when(self.me.outer)
            def _():
                self.copy(0, p).wait_send()

            @pl.when(self.me.inner)
            def _():
                self.copy(1, p).wait_send()
                self.copy(2, p).wait_send()

            return carry

        lax.fori_loop(0, pieces, one, 0)


class BlockSum:
    def __init__(self, me, make, out, held, mates, chips, sems):
        self.me, self.make, self.out = me, make, out
        self.held, self.mates, self.chips, self.sems = held, mates, chips, sems

    def to_mate(self, k):
        me = self.me
        return remote(
            self.held.at[k % 2], self.mates.at[k], self.sems.at[0, k], self.sems.at[1, k], me.mate, me.t
        )

    def to_chip(self, k):
        me = self.me
        return remote(
            self.mates.at[k], self.chips.at[k], self.sems.at[2, k], self.sems.at[3, k],
            me.chip_at(k) * 2 + me.core, me.t,
        )

    def lend(self, k):
        me = self.me
        if k >= 2:
            self.to_mate(k - 2).wait_send()
        for lo, hi, value in self.make(me.chip_at(k) * 2 + 1 - me.core):
            self.held[k % 2, :, lo:hi] = value.astype(BF16)
        self.to_mate(k).start()

    def step(self, k):
        me = self.me
        if k == 0:
            self.lend(0)
        if k < 3:
            self.lend(k + 1)
        own = self.make(me.chip_at(k) * 2 + me.core)
        first = True
        for lo, hi, value in own:
            if first:
                self.to_mate(k).wait_recv()
                first = False
            total = value + self.mates[k, :, lo:hi].astype(F32)
            if k < 3:
                self.mates[k, :, lo:hi] = total.astype(BF16)
            else:
                self.out[:, lo:hi] = total
        if k < 3:
            self.to_chip(k).start()

    def finish(self):
        for k in range(3):
            self.to_chip(k).wait_recv()
            self.out[...] += self.chips[k].astype(F32)
        for k in (2, 3):
            self.to_mate(k).wait_send()
        for k in range(3):
            self.to_chip(k).wait_send()


def norm_rows(values):
    inverse = lax.rsqrt(jnp.mean(values * values, axis=-1, keepdims=True) + norm_eps)
    return values * inverse, inverse


def turn(values, cs_ref, sign):
    cosine, sine = cs_ref[0:HALF, :], cs_ref[HALF:HEAD_SIZE, :] * sign
    pieces = []
    for h in range(values.shape[0] // HEAD_SIZE):
        low = values[h * HEAD_SIZE : h * HEAD_SIZE + HALF]
        high = values[h * HEAD_SIZE + HALF : (h + 1) * HEAD_SIZE]
        pieces.append(low * cosine - high * sine)
        pieces.append(high * cosine + low * sine)
    return jnp.concatenate(pieces, axis=0)


def fill_bias(bias, st_ref, key_start, query_start):
    key_place = lax.broadcasted_iota(jnp.int32, bias.shape, 0) + key_start
    query_place = lax.broadcasted_iota(jnp.int32, bias.shape, 1) + query_start
    allowed = jnp.logical_and(key_place >= st_ref[0:1, :], key_place <= query_place)
    bias[...] = jnp.where(allowed, 0.0, neg_fill)


def heads_of(h, group):
    g = h // group
    return slice(h * HEAD_SIZE, (h + 1) * HEAD_SIZE), slice(g * HEAD_SIZE, (g + 1) * HEAD_SIZE), g


def forward_kernel(
    dims,
    hid_ref, og_ref, st_ref, cs_ref, ag_ref, mg_ref, wq_ref, wk_ref, wv_ref, wo_ref,
    wg_hbm, wu_hbm, wd_hbm,
    q_ref, kv_out, ot_ref, lse_ref, br_out, dl_out, mlp_out, act_out, gg_ref, gu_ref,
    wg, wu, wd, kv, norm, norm_t, og_t, m_ref, l_ref, bias, dh, act, dg, du, mlp,
    p1, a1, b1, p2, a2, b2, held, mates, chips, total,
    load_sem, kv_ssem, kv_rsem, sem1, sem2, rs_sem, out_sem,
):
    rows, piece, chunk = dims["rows"], dims["piece"], dims["chunk"]
    q_heads, group, kv_width = dims["q_heads"], dims["group"], dims["kv_width"]
    n_pieces, n_chunks = rows // piece, rows // chunk
    per = chunk // piece
    hidden_units = wg.shape[1]
    width = hid_ref.shape[1]
    me = Place()
    loads = [
        pltpu.make_async_copy(src, dst, load_sem.at[i])
        for i, (src, dst) in enumerate(((wd_hbm, wd), (wg_hbm, wg), (wu_hbm, wu)))
    ]
    for load in loads:
        load.start()

    def first_norm(c, carry):
        r = pl.ds(pl.multiple_of(c * chunk, chunk), chunk)
        normed, _ = norm_rows(hid_ref[r, :].astype(F32))
        norm[r, :] = (normed * ag_ref[...]).astype(BF16)
        return carry

    lax.fori_loop(0, n_chunks, first_norm, 0)
    key_t = dot_nn(norm[...], wk_ref[...]).T
    kv[me.b, 0:kv_width, :] = turn(key_t, cs_ref, 1.0).astype(BF16)
    kv[me.b, kv_width : 2 * kv_width, :] = dot_nn(norm[...], wv_ref[...]).T.astype(BF16)
    enter(me, (1, 2, 4, 6))

    def kv_copy(s, target):
        return remote(kv.at[s], kv.at[s], kv_ssem, kv_rsem, target, me.t)

    def send_kv(slot, target, n):
        return remote(kv.at[slot], kv.at[slot], kv_ssem.at[n], kv_rsem.at[n], target, me.t)

    for s in (6, 4, 2, 1):
        send_kv(me.b, me.slot(s), s).start()
    q_ref[...] = turn(dot_nn(norm[...], wq_ref[...]).T, cs_ref, 1.0).astype(BF16)
    og_t[...] = og_ref[...].T

    m_ref[...] = jnp.full(m_ref.shape, neg_fill, F32)
    l_ref[...] = jnp.zeros(l_ref.shape, F32)
    ot_ref[...] = jnp.zeros(ot_ref.shape, F32)
    loads[0].wait()
    dh[...] = dot_nt(og_ref[...], wd[...])

    def attend(s, carry):
        slot = me.slot(s)

        @pl.when(s > 0)
        def _():
            send_kv(slot, me.mate, s).wait_recv()

        @pl.when(jnp.logical_and(s > 0, s % 2 == 0))
        def _():
            send_kv(slot, me.mate, s + 1).start()

        @pl.when(slot <= me.b)
        def _():
            fill_bias(bias, st_ref, slot * rows, me.b * rows)
            for h in range(q_heads):
                qs, ks, g = heads_of(h, group)
                vs = slice(kv_width + g * HEAD_SIZE, kv_width + (g + 1) * HEAD_SIZE)
                scores = dot_tn(kv[slot, ks, :], q_ref[qs, :]) + bias[...]
                old = m_ref[h : h + 1, :]
                new = jnp.maximum(old, jnp.max(scores, axis=0, keepdims=True))
                probs = jnp.exp2((scores - new) * (SCORE_SCALE * LOG2E))
                keep = jnp.exp2((old - new) * (SCORE_SCALE * LOG2E))
                m_ref[h : h + 1, :] = new
                l_ref[h : h + 1, :] = l_ref[h : h + 1, :] * keep + jnp.sum(probs, axis=0, keepdims=True)
                ot_ref[qs, :] = ot_ref[qs, :] * keep + dot_nn(kv[slot, vs, :], probs.astype(BF16))

        return carry

    lax.fori_loop(0, 8, attend, 0)
    for h in range(q_heads):
        qs, _, _ = heads_of(h, group)
        ot_ref[qs, :] = ot_ref[qs, :] / l_ref[h : h + 1, :]
    lse_ref[...] = jnp.zeros(lse_ref.shape, F32)
    lse_ref[0:q_heads, :] = m_ref[0:q_heads, :] * (SCORE_SCALE * LOG2E) + jnp.log2(l_ref[0:q_heads, :])
    kv_save = pltpu.make_async_copy(kv, kv_out, out_sem.at[0])
    kv_save.start()

    branch = LineSum(me, p1, a1, b1, sem1, piece)
    attn_low = ot_ref[...].T.astype(BF16)
    for n in range(0, width, 512):
        p1[:, n : n + 512] = dot_nn(attn_low, wo_ref[:, n : n + 512]).astype(BF16)

    def each(f, lo, hi):
        def one(p, carry):
            f(p)
            return carry

        lax.fori_loop(lo, hi, one, 0)

    each(branch.give, 0, n_pieces)
    each(branch.fold, 0, per)
    loads[1].wait()
    loads[2].wait()
    back = LineSum(me, p2, a2, b2, sem2, piece)

    def feed(c, carry):
        @pl.when(c < n_chunks - 1)
        def _():
            each(branch.fold, (c + 1) * per, (c + 2) * per)

        each(branch.unfold, c * per, (c + 1) * per)
        each(branch.take, c * per, (c + 1) * per)
        r = pl.ds(pl.multiple_of(c * chunk, chunk), chunk)
        middle = hid_ref[r, :].astype(F32) + a1[r, :].astype(F32)
        normed, _ = norm_rows(middle)
        norm[r, :] = (normed * mg_ref[...]).astype(BF16)
        for n in range(0, hidden_units, 512):
            ns = slice(n, n + 512)
            gate = dot_nn(norm[r, :], wg[:, ns])
            up = dot_nn(norm[r, :], wu[:, ns])
            sig = 1.0 / (1.0 + jnp.exp(-gate))
            silu = gate * sig
            act[r, ns] = (silu * up).astype(BF16)
            grad = dh[r, ns]
            dg[r, ns] = (grad * up * sig * (1.0 + gate * (1.0 - sig))).astype(BF16)
            du[r, ns] = (grad * silu).astype(BF16)
        for n in range(0, width, 512):
            ns = slice(n, n + 512)
            p2[r, ns] = (dot_nt(dg[r, :], wg[ns, :]) + dot_nt(du[r, :], wu[ns, :])).astype(BF16)
        each(back.give, c * per, (c + 1) * per)

        @pl.when(c >= 1)
        def _():
            each(back.fold, (c - 1) * per, c * per)

        @pl.when(c >= 2)
        def _():
            each(back.unfold, (c - 2) * per, (c - 1) * per)

        return carry

    lax.fori_loop(0, n_chunks, feed, 0)
    br_save = pltpu.make_async_copy(a1, br_out, out_sem.at[1])
    br_save.start()
    act_save = pltpu.make_async_copy(act, act_out, out_sem.at[2])
    act_save.start()
    each(back.fold, n_pieces - per, n_pieces)
    each(back.unfold, n_pieces - 2 * per, n_pieces - per)
    norm_t[...] = norm[...].T

    def products(j):
        js = pl.ds(pl.multiple_of(j * dims["share"], dims["share"]), dims["share"])
        yield 0, hidden_units, dot_nn(norm_t[js, :], dg[...])
        yield hidden_units, 2 * hidden_units, dot_nn(norm_t[js, :], du[...])

    weight_sum = BlockSum(me, products, total, held, mates, chips, rs_sem)
    weight_sum.step(0)
    each(back.unfold, n_pieces - per, n_pieces)
    for k in range(1, 4):
        weight_sum.step(k)
    for n in range(0, width, 512):
        mlp[:, n : n + 512] = dot_nn(act[...], wd[:, n : n + 512]).astype(BF16)
    mlp_save = pltpu.make_async_copy(mlp, mlp_out, out_sem.at[3])
    mlp_save.start()
    each(back.take, 0, n_pieces)
    dl_save = pltpu.make_async_copy(a2, dl_out, out_sem.at[4])
    dl_save.start()
    weight_sum.finish()
    gg_ref[...] = total[:, 0:hidden_units]
    gu_ref[...] = total[:, hidden_units : 2 * hidden_units]
    for s in (6, 4, 2, 1):
        send_kv(me.b, me.slot(s), s).wait_send()
    for s in (2, 4, 6):
        send_kv(me.slot(s), me.mate, s + 1).wait_send()
    branch.drain(n_pieces)
    back.drain(n_pieces)
    for save in (kv_save, br_save, act_save, mlp_save, dl_save):
        save.wait()


def backward_kernel(
    dims,
    hid_ref, og_ref, br_ref, dl_ref, st_ref, cs_ref, ag_ref, mg_ref, q_ref, kv_ref, ot_ref, lse_ref,
    act_ref, wq_ref, wk_ref, wv_ref, wo_ref, mlp_hbm,
    lo_ref, ig_ref, gq_ref, gk_ref, gv_ref, go_ref, gd_ref, gains_ref,
    p3, a3, b3, p4, a4, b4, dmid, dbr, dbr_t, og_t, norm_t, do_t, delta, dq, acc, bias, low_t, dqr, dkr, dvr,
    kv_held, kv_mates, kv_chips, held1, mates1, chips1, total1, held2, mates2, chips2, total2, gain, gain_in,
    load_sem, sem3, sem4, kvs_sem, rs1_sem, rs2_sem, gain_ssem, gain_rsem,
):
    rows, piece, chunk, share = dims["rows"], dims["piece"], dims["chunk"], dims["share"]
    q_heads, group, kv_width = dims["q_heads"], dims["group"], dims["kv_width"]
    n_pieces, n_chunks = rows // piece, rows // chunk
    per = chunk // piece
    width = hid_ref.shape[1]
    hidden_units = act_ref.shape[1]
    q_width = q_heads * HEAD_SIZE
    me = Place()
    load = pltpu.make_async_copy(mlp_hbm, p3, load_sem)
    load.start()
    enter(me, tuple(range(1, 8)))
    load.wait()

    def each(f, lo, hi):
        def one(p, carry):
            f(p)
            return carry

        lax.fori_loop(lo, hi, one, 0)

    branch = LineSum(me, p3, a3, b3, sem3, piece)
    each(branch.give, 0, n_pieces)
    gain[...] = jnp.zeros(gain.shape, F32)

    def middle_grad(c, carry):
        r = pl.ds(pl.multiple_of(c * chunk, chunk), chunk)
        normed, inverse = norm_rows(hid_ref[r, :].astype(F32) + br_ref[r, :].astype(F32))
        grad = dl_ref[r, :].astype(F32)
        scaled = grad * mg_ref[...]
        gain[1:2, :] += jnp.sum(grad * normed, axis=0, keepdims=True)
        found = og_ref[r, :].astype(F32) + inverse * (
            scaled - normed * jnp.mean(scaled * normed, axis=-1, keepdims=True)
        )
        dmid[r, :] = found
        dbr[r, :] = found.astype(BF16)
        return carry

    lax.fori_loop(0, n_chunks, middle_grad, 0)
    do_t[...] = dot_nt(wo_ref[...], dbr[...]).astype(BF16)
    delta[...] = jnp.zeros(delta.shape, F32)
    for h in range(q_heads):
        qs, _, _ = heads_of(h, group)
        delta[h : h + 1, :] = jnp.sum(do_t[qs, :].astype(F32) * ot_ref[qs, :], axis=0, keepdims=True)
    dq[...] = jnp.zeros(dq.shape, F32)

    def kv_to_mate(k):
        return remote(kv_held.at[k], kv_mates.at[k], kvs_sem.at[0, k], kvs_sem.at[1, k], me.mate, me.t)

    def kv_to_chip(k):
        return remote(
            kv_mates.at[k], kv_chips.at[k], kvs_sem.at[2, k], kvs_sem.at[3, k],
            me.chip_at(k) * 2 + me.core, me.t,
        )

    def attend(u, carry):
        k, own = u // 2, u % 2
        chip = me.chip_at(k)
        slot = chip * 2 + (me.core + 1 - own) % 2
        branch.fold(u)

        @pl.when(u >= 1)
        def _():
            branch.unfold(u - 1)

        @pl.when(slot <= me.b)
        def _():
            fill_bias(bias, st_ref, slot * rows, me.b * rows)
            for g in range(q_heads // group):
                ks = slice(g * HEAD_SIZE, (g + 1) * HEAD_SIZE)
                vs = slice(kv_width + g * HEAD_SIZE, kv_width + (g + 1) * HEAD_SIZE)
                key_t, value_t = kv_ref[slot, ks, :], kv_ref[slot, vs, :]
                grad_k = grad_v = None
                for h in range(g * group, (g + 1) * group):
                    qs, _, _ = heads_of(h, group)
                    query_t, grad_t = q_ref[qs, :], do_t[qs, :]
                    scores = dot_tn(key_t, query_t) + bias[...]
                    probs = jnp.exp2(scores * (SCORE_SCALE * LOG2E) - lse_ref[h : h + 1, :])
                    grad_p = dot_tn(value_t, grad_t)
                    grad_s = (probs * (grad_p - delta[h : h + 1, :])).astype(BF16)
                    one_v = dot_nt(grad_t, probs.astype(BF16))
                    one_k = dot_nt(query_t, grad_s)
                    grad_v = one_v if grad_v is None else grad_v + one_v
                    grad_k = one_k if grad_k is None else grad_k + one_k
                    dq[qs, :] += dot_nn(key_t, grad_s)
                acc[ks, :] = grad_k
                acc[vs, :] = grad_v

        @pl.when(jnp.logical_and(own == 0, slot <= me.b))
        def _():
            kv_held[k] = acc[...].astype(BF16)
            kv_to_mate(k).start()

        @pl.when(jnp.logical_and(own == 1, chip < me.chip))
        def _():
            kv_to_mate(k).wait_recv()
            kv_mates[k] = (acc[...] + kv_mates[k].astype(F32)).astype(BF16)
            kv_to_chip(k).start()

        return carry

    lax.fori_loop(0, 8, attend, 0)
    branch.unfold(n_pieces - 1)

    low_t[0:q_width, :] = turn(dq[...] * SCORE_SCALE, cs_ref, -1.0).astype(BF16)
    dqr[...] = low_t[0:q_width, :].T

    dbr_t[...] = dbr[...].T
    og_t[...] = og_ref[...].T
    attn_low = ot_ref[...].astype(BF16)

    def products1(j):
        js = pl.ds(pl.multiple_of(j * share, share), share)
        yield 0, hidden_units, dot_nn(og_t[js, :], act_ref[...])
        yield hidden_units, hidden_units + q_width, dot_nt(dbr_t[js, :], attn_low)

    sum1 = BlockSum(me, products1, total1, held1, mates1, chips1, rs1_sem)
    for k in range(4):
        sum1.step(k)

    def layer_rows(c, carry):
        each(branch.take, c * per, (c + 1) * per)
        r = pl.ds(pl.multiple_of(c * chunk, chunk), chunk)
        middle = hid_ref[r, :].astype(F32) + br_ref[r, :].astype(F32)
        lo_ref[r, :] = (middle + a3[r, :].astype(F32)).astype(BF16)
        normed, _ = norm_rows(hid_ref[r, :].astype(F32))
        dbr[r, :] = (normed * ag_ref[...]).astype(BF16)
        return carry

    lax.fori_loop(0, n_chunks, layer_rows, 0)
    norm_t[...] = dbr[...].T

    @pl.when(me.core == 0)
    def _():
        kv_to_mate(3).wait_recv()
        acc[...] += kv_mates[3].astype(F32)

    for k in range(3):

        @pl.when(me.chip_at(k) > me.chip)
        def _(k=k):
            kv_to_chip(k).wait_recv()
            acc[...] += kv_chips[k].astype(F32)

    low_t[q_width : q_width + kv_width, :] = turn(acc[0:kv_width, :] * SCORE_SCALE, cs_ref, -1.0).astype(BF16)
    low_t[q_width + kv_width : q_width + 2 * kv_width, :] = acc[kv_width : 2 * kv_width, :].astype(BF16)
    dkr[...] = low_t[q_width : q_width + kv_width, :].T
    dvr[...] = low_t[q_width + kv_width : q_width + 2 * kv_width, :].T

    last = LineSum(me, p4, a4, b4, sem4, piece)

    def input_part(c, carry):
        r = pl.ds(pl.multiple_of(c * chunk, chunk), chunk)
        for n in range(0, width, 512):
            ns = slice(n, n + 512)
            p4[r, ns] = (
                dot_nt(dqr[r, :], wq_ref[ns, :])
                + dot_nt(dkr[r, :], wk_ref[ns, :])
                + dot_nt(dvr[r, :], wv_ref[ns, :])
            ).astype(BF16)
        each(last.give, c * per, (c + 1) * per)
        return carry

    lax.fori_loop(0, n_chunks, input_part, 0)

    def products2(j):
        js = pl.ds(pl.multiple_of(j * share, share), share)
        yield 0, q_width + 2 * kv_width, dot_nt(norm_t[js, :], low_t[...])

    sum2 = BlockSum(me, products2, total2, held2, mates2, chips2, rs2_sem)
    each(last.fold, 0, 2)
    sum2.step(0)
    each(last.fold, 2, 3)
    each(last.unfold, 0, 2)
    sum2.step(1)
    each(last.fold, 3, 4)
    each(last.unfold, 2, 3)
    sum2.step(2)
    each(last.fold, 4, 5)
    each(last.unfold, 3, 4)
    sum2.step(3)

    def rest(p, carry):
        last.fold(p)
        last.unfold(p - 1)
        return carry

    lax.fori_loop(5, n_pieces, rest, 0)
    last.unfold(n_pieces - 1)
    sum1.finish()
    gd_ref[...] = total1[:, 0:hidden_units].T
    go_ref[...] = total1[:, hidden_units : hidden_units + q_width].T

    def input_rows(c, carry):
        each(last.take, c * per, (c + 1) * per)
        r = pl.ds(pl.multiple_of(c * chunk, chunk), chunk)
        normed, inverse = norm_rows(hid_ref[r, :].astype(F32))
        grad = a4[r, :].astype(F32)
        scaled = grad * ag_ref[...]
        gain[0:1, :] += jnp.sum(grad * normed, axis=0, keepdims=True)
        found = inverse * (scaled - normed * jnp.mean(scaled * normed, axis=-1, keepdims=True))
        ig_ref[r, :] = (dmid[r, :] + found).astype(BF16)
        return carry

    lax.fori_loop(0, n_chunks, input_rows, 0)

    def gain_copy(s):
        return remote(gain, gain_in.at[s], gain_ssem.at[s], gain_rsem.at[s], me.slot(s), me.t)

    for s in range(1, 8):
        gain_copy(s).start()
    sum2.finish()
    gq_ref[...] = total2[:, 0:q_width]
    gk_ref[...] = total2[:, q_width : q_width + kv_width]
    gv_ref[...] = total2[:, q_width + kv_width : q_width + 2 * kv_width]
    for s in range(1, 8):
        gain_copy(s).wait_recv()
    gains = gain[...]
    for s in range(1, 8):
        gains = gains + gain_in[s]
    gains_ref[...] = gains
    for s in range(1, 8):
        gain_copy(s).wait_send()
    branch.drain(n_pieces)
    last.drain(n_pieces)
    for k in range(4):
        chip = me.chip_at(k)
        slot = chip * 2 + 1 - me.core

        @pl.when(slot <= me.b)
        def _(k=k):
            kv_to_mate(k).wait_send()

        if k < 3:

            @pl.when(chip < me.chip)
            def _(k=k):
                kv_to_chip(k).wait_send()


def kernel_shards(
    hidden_in, out_grad, lengths, attn_gain, w_query, key_projection_weight, value_projection_weight,
    w_out, mlp_gain, w_gate, w_up, w_down,
):
    rows, width = hidden_in.shape
    q_width, kv_width = w_query.shape[1], key_projection_weight.shape[1]
    hidden_units = w_gate.shape[1]
    blocks = lax.axis_size("blk")
    share = width // blocks
    piece, chunk = rows // 8, rows // 4
    pieces = rows // piece
    dims = dict(
        rows=rows, piece=piece, chunk=chunk, share=share, q_heads=q_width // HEAD_SIZE,
        group=q_width // kv_width, kv_width=kv_width,
    )
    places = lax.axis_index("blk") * rows + jnp.arange(rows, dtype=jnp.int32)
    start = jnp.zeros((rows,), jnp.int32)
    end = jnp.int32(0)
    for k in range(lengths.shape[0]):
        end = end + lengths[k]
        start = jnp.where(places >= end, end, start)
    position = (places - start).astype(F32)
    freqs = rope_base ** (-(2.0 * jnp.arange(HALF, dtype=F32)) / HEAD_SIZE)
    angle = freqs[:, None] * position[None, :]
    turns = jnp.concatenate([jnp.cos(angle), jnp.sin(angle)], axis=0)
    starts = jnp.broadcast_to(start[None, :], (8, rows))
    attn_gain, mlp_gain = attn_gain[None, :], mlp_gain[None, :]
    vmem, hbm = pl.BlockSpec(memory_space=pltpu.VMEM), pl.BlockSpec(memory_space=pl.ANY)
    dma = pltpu.SemaphoreType.DMA

    def shape(dtype, *dims_):
        return jax.ShapeDtypeStruct(dims_, dtype)

    def low(*dims_):
        return pltpu.VMEM(dims_, BF16)

    def full(*dims_):
        return pltpu.VMEM(dims_, F32)

    line = [low(rows, width)] * 3
    mlp_width = 2 * hidden_units

    def block_buffers(columns):
        return [
            low(2, share, columns), low(4, share, columns), low(3, share, columns), full(share, columns),
        ]

    outs = pl.pallas_call(
        functools.partial(forward_kernel, dims),
        out_shape=(
            shape(BF16, q_width, rows), shape(BF16, blocks, 2 * kv_width, rows), shape(F32, q_width, rows),
            shape(F32, 8, rows), shape(BF16, rows, width), shape(BF16, rows, width), shape(BF16, rows, width),
            shape(BF16, rows, hidden_units), shape(F32, share, hidden_units), shape(F32, share, hidden_units),
        ),
        in_specs=[vmem] * 10 + [hbm] * 3,
        out_specs=(vmem, hbm, vmem, vmem, hbm, hbm, hbm, hbm, vmem, vmem),
        scratch_shapes=[
            low(width, hidden_units), low(width, hidden_units), low(hidden_units, width),
            low(blocks, 2 * kv_width, rows), low(rows, width), low(width, rows), low(width, rows),
            full(8, rows), full(8, rows), full(rows, rows), full(rows, hidden_units),
            low(rows, hidden_units), low(rows, hidden_units), low(rows, hidden_units), low(rows, width),
            *line, *line, *block_buffers(mlp_width),
            dma((3,)), dma((8,)), dma((8,)), dma((6, pieces)), dma((6, pieces)), dma((4, 4)), dma((5,)),
        ],
        compiler_params=pltpu.CompilerParams(
            collective_id=0, has_side_effects=True, vmem_limit_bytes=VMEM_BYTES
        ),
    )(
        hidden_in, out_grad, starts, turns, attn_gain, mlp_gain, w_query, key_projection_weight,
        value_projection_weight, w_out, w_gate, w_up, w_down,
    )
    query_t, kv, attn_t, log_sum, branch, grad_ln, mlp_part, act, grad_gate, grad_up = outs
    outs = pl.pallas_call(
        functools.partial(backward_kernel, dims),
        out_shape=(
            shape(BF16, rows, width), shape(BF16, rows, width), shape(F32, share, q_width),
            shape(F32, share, kv_width), shape(F32, share, kv_width), shape(F32, q_width, share),
            shape(F32, hidden_units, share), shape(F32, 8, width),
        ),
        in_specs=[vmem] * 17 + [hbm],
        out_specs=(vmem,) * 8,
        scratch_shapes=[
            *line, *line, full(rows, width), low(rows, width), low(width, rows), low(width, rows),
            low(width, rows), low(q_width, rows), full(8, rows), full(q_width, rows), full(2 * kv_width, rows),
            full(rows, rows), low(q_width + 2 * kv_width, rows), low(rows, q_width), low(rows, kv_width),
            low(rows, kv_width),
            low(4, 2 * kv_width, rows), low(4, 2 * kv_width, rows), low(3, 2 * kv_width, rows),
            *block_buffers(hidden_units + q_width), *block_buffers(q_width + 2 * kv_width),
            full(8, width), full(8, 8, width),
            dma(()), dma((6, pieces)), dma((6, pieces)), dma((4, 4)), dma((4, 4)), dma((4, 4)),
            dma((8,)), dma((8,)),
        ],
        compiler_params=pltpu.CompilerParams(
            collective_id=1, has_side_effects=True, vmem_limit_bytes=VMEM_BYTES
        ),
    )(
        hidden_in, out_grad, branch, grad_ln, starts, turns, attn_gain, mlp_gain, query_t, kv, attn_t, log_sum,
        act, w_query, key_projection_weight, value_projection_weight, w_out, mlp_part,
    )
    layer_out, input_grad, grad_query, grad_key, grad_value, grad_out, grad_down, gains = outs
    mine = lax.dynamic_slice_in_dim(gains[0:2], lax.axis_index("blk") * share, share, 1)
    return (
        layer_out, input_grad, grad_query, grad_key, grad_value, grad_out, grad_gate, grad_up, grad_down,
        mine[0], mine[1],
    )


def solution(mesh):
    sizes = dict(mesh.shape)
    small = sizes["blk"] == 8 and sizes["tp"] == 4
    placed = (
        P("blk", None),
        P("blk", None),
        P(),
        P(),
        P(None, "tp"),
        P(None, "tp"),
        P(None, "tp"),
        P("tp", None),
        P(),
        P(None, "tp"),
        P(None, "tp"),
        P("tp", None),
    )
    return jax.shard_map(
        kernel_shards if small else shards,
        mesh=mesh,
        in_specs=placed,
        out_specs=(
            P("blk", None),
            P("blk", None),
            P("blk", "tp"),
            P("blk", "tp"),
            P("blk", "tp"),
            P("tp", "blk"),
            P("blk", "tp"),
            P("blk", "tp"),
            P("tp", "blk"),
            P("blk"),
            P("blk"),
        ),
        check_vma=False,
    )
```

```python
import functools
import math

import jax
import jax.numpy as jnp
from jax import lax
from jax.experimental import pallas as pl
from jax.experimental.pallas import tpu as pltpu
from jax.sharding import PartitionSpec as P

HEAD_SIZE = 96


norm_eps = 1e-05
rope_base = 100000.0
neg_fill = -1e30


def doc_places(lengths, places):
    doc_ends = jnp.cumsum(lengths)
    passed = (places[:, None] >= doc_ends[None, :]).astype(jnp.int32)
    segment = jnp.sum(passed, axis=1)
    preceding = jnp.sum(passed * lengths[None, :], axis=1)
    return (segment, places - preceding)


def apply_rotary(values, token_position, heads, sign_value):
    half_size = HEAD_SIZE // 2
    freqs = rope_base ** (-(2.0 * jnp.arange(half_size, dtype=jnp.float32)) / HEAD_SIZE)
    angle = token_position.astype(jnp.float32)[:, None] * freqs[None, :]
    cosine = jnp.cos(angle)[:, None, :]
    sine = sign_value * jnp.sin(angle)[:, None, :]
    shaped = values.reshape(values.shape[0], heads, HEAD_SIZE)
    first_half = shaped[..., :half_size]
    second_half = shaped[..., half_size:]
    turned = jnp.concatenate(
        [first_half * cosine - second_half * sine, second_half * cosine + first_half * sine],
        axis=-1,
    )
    return turned.reshape(values.shape[0], heads * HEAD_SIZE)


def rms_parts(values):
    inverse = lax.rsqrt(jnp.mean(values * values, axis=-1, keepdims=True) + norm_eps)
    return (values * inverse, inverse)


def norm_back(grad_in, normed, inverse, gain):
    scaled = grad_in * gain
    grad_values = inverse * (scaled - normed * jnp.mean(scaled * normed, axis=-1, keepdims=True))
    return (grad_values, jnp.sum(grad_in * normed, axis=0))


def left_product(left_side, right_side):
    return lax.dot_general(
        left_side, right_side, (((0,), (0,)), ((), ())), preferred_element_type=jnp.float32
    )


def right_product(left_side, weight):
    return lax.dot_general(
        left_side, weight, (((1,), (1,)), ((), ())), preferred_element_type=jnp.float32
    )


def score_block(query_four, key_rows, query_seg, query_place, key_seg, key_place):
    score_scale = HEAD_SIZE ** (-0.5)
    scores = (
        jnp.einsum("igrd,jgd->grij", query_four, key_rows, preferred_element_type=jnp.float32)
        * score_scale
    )
    allowed = (query_seg[:, None] == key_seg[None, :]) & (
        key_place[None, :] <= query_place[:, None]
    )
    return (jnp.where(allowed[None, None], scores, neg_fill), allowed)


def score_grads(
    query_four,
    grad_four,
    log_sum,
    delta,
    query_seg,
    query_place,
    key_rows,
    value_rows,
    key_seg,
    key_place,
):
    scores, allowed = score_block(query_four, key_rows, query_seg, query_place, key_seg, key_place)
    probs = jnp.where(allowed[None, None], jnp.exp(scores - log_sum[..., None]), 0.0)
    grad_probs = jnp.einsum(
        "igrd,jgd->grij", grad_four, value_rows, preferred_element_type=jnp.float32
    )
    grad_scores = (probs * (grad_probs - delta[..., None])).astype(jnp.bfloat16)
    return (grad_scores, probs.astype(jnp.bfloat16))


def keep_same(running):
    return running


def shards(
    hidden_in,
    out_grad,
    lengths,
    attn_gain,
    w_query,
    key_projection_weight,
    value_projection_weight,
    w_out,
    mlp_gain,
    w_gate,
    w_up,
    w_down,
):
    row_count = hidden_in.shape[0]
    cycle_size = lax.axis_size("blk")
    first_row = lax.axis_index("blk") * row_count
    offsets = jnp.arange(row_count, dtype=jnp.int32)
    places = first_row + offsets
    segment, token_position = doc_places(lengths, places)
    q_heads = w_query.shape[1] // HEAD_SIZE
    kv_heads = key_projection_weight.shape[1] // HEAD_SIZE
    query_group_size = q_heads // kv_heads
    kv_width = kv_heads * HEAD_SIZE
    score_scale = HEAD_SIZE ** (-0.5)
    hidden_f = hidden_in.astype(jnp.float32)
    normed_one, inverse_one = rms_parts(hidden_f)
    first_layer_norm = (normed_one * attn_gain).astype(jnp.bfloat16)
    query_raw = jnp.dot(first_layer_norm, w_query, preferred_element_type=jnp.float32)
    key_raw = jnp.dot(first_layer_norm, key_projection_weight, preferred_element_type=jnp.float32)
    value_raw = jnp.dot(
        first_layer_norm, value_projection_weight, preferred_element_type=jnp.float32
    )
    query_low = apply_rotary(query_raw, token_position, q_heads, 1.0).astype(jnp.bfloat16)
    key_low = apply_rotary(key_raw, token_position, kv_heads, 1.0).astype(jnp.bfloat16)
    value_low = value_raw.astype(jnp.bfloat16)
    kv_rows = jnp.concatenate([key_low, value_low], axis=1)
    query_four = query_low.reshape(row_count, kv_heads, query_group_size, HEAD_SIZE)

    def split_kv(piece, block_step):
        block_rows = lax.dynamic_slice_in_dim(piece, block_step * row_count, row_count, 0)
        key_rows = block_rows[:, :kv_width].reshape(row_count, kv_heads, HEAD_SIZE)
        value_rows = block_rows[:, kv_width:].reshape(row_count, kv_heads, HEAD_SIZE)
        return (key_rows, value_rows)

    start_max = jnp.full((kv_heads, query_group_size, row_count), neg_fill, jnp.float32)
    start_sum = jnp.zeros((kv_heads, query_group_size, row_count), jnp.float32)
    start_acc = jnp.zeros((kv_heads, query_group_size, row_count, HEAD_SIZE), jnp.float32)
    piece = lax.all_gather(kv_rows, "blk", axis=0, tiled=True)

    def forward_one_step(block_step, running):
        key_start = block_step * row_count

        def forward_work(running):
            row_max, row_sum, weighted = running
            key_rows, value_rows = split_kv(piece, block_step)
            key_place = key_start + offsets
            key_seg, _ = doc_places(lengths, key_place)
            scores, allowed = score_block(query_four, key_rows, segment, places, key_seg, key_place)
            new_max = jnp.maximum(row_max, jnp.max(scores, axis=-1))
            exp_scores = jnp.where(allowed[None, None], jnp.exp(scores - new_max[..., None]), 0.0)
            rescale = jnp.exp(row_max - new_max)
            row_sum = row_sum * rescale + jnp.sum(exp_scores, axis=-1)
            weighted = weighted * rescale[..., None] + jnp.einsum(
                "grij,jgd->grid",
                exp_scores.astype(jnp.bfloat16),
                value_rows,
                preferred_element_type=jnp.float32,
            )
            return (new_max, row_sum, weighted)

        return lax.cond(key_start <= first_row, forward_work, keep_same, running)

    row_max, row_sum, weighted = lax.fori_loop(
        0, piece.shape[0] // row_count, forward_one_step, (start_max, start_sum, start_acc)
    )
    attn_four = weighted / row_sum[..., None]
    log_sum = row_max + jnp.log(row_sum)
    attn_rows = jnp.transpose(attn_four, (2, 0, 1, 3)).reshape(row_count, q_heads * HEAD_SIZE)
    attn_low = attn_rows.astype(jnp.bfloat16)
    branch = lax.psum(jnp.dot(attn_low, w_out, preferred_element_type=jnp.float32), "tp")
    middle = hidden_f + branch
    normed_two, inverse_two = rms_parts(middle)
    ln_two = (normed_two * mlp_gain).astype(jnp.bfloat16)
    gate = jnp.dot(ln_two, w_gate, preferred_element_type=jnp.float32)
    up_proj = jnp.dot(ln_two, w_up, preferred_element_type=jnp.float32)
    sig_gate = jax.nn.sigmoid(gate)
    act_gate = gate * sig_gate
    hidden = (act_gate * up_proj).astype(jnp.bfloat16)
    mlp_branch = lax.psum(jnp.dot(hidden, w_down, preferred_element_type=jnp.float32), "tp")
    layer_out = (middle + mlp_branch).astype(jnp.bfloat16)
    grad_down = left_product(hidden, out_grad)
    grad_hidden = right_product(out_grad, w_down)
    grad_gate_act = (grad_hidden * up_proj * sig_gate * (1.0 + gate * (1.0 - sig_gate))).astype(
        jnp.bfloat16
    )
    grad_up_act = (grad_hidden * act_gate).astype(jnp.bfloat16)
    grad_gate = left_product(ln_two, grad_gate_act)
    grad_up = left_product(ln_two, grad_up_act)
    grad_ln_two = lax.psum(
        right_product(grad_gate_act, w_gate) + right_product(grad_up_act, w_up), "tp"
    )
    grad_middle_norm, grad_mlp_gain = norm_back(grad_ln_two, normed_two, inverse_two, mlp_gain)
    grad_middle = out_grad.astype(jnp.float32) + grad_middle_norm
    grad_branch = grad_middle.astype(jnp.bfloat16)
    grad_out = left_product(attn_low, grad_branch)
    grad_attn = right_product(grad_branch, w_out).astype(jnp.bfloat16)
    grad_four = grad_attn.reshape(row_count, kv_heads, query_group_size, HEAD_SIZE)
    delta = jnp.sum(jnp.transpose(grad_four.astype(jnp.float32), (1, 2, 0, 3)) * attn_four, axis=-1)

    def query_grads(grad_scores, key_rows):
        return (
            jnp.einsum("grij,jgd->grid", grad_scores, key_rows, preferred_element_type=jnp.float32)
            * score_scale
        )

    def key_value_grads(grad_scores, probs_low, query_rows, grad_rows):
        grad_keys = (
            jnp.einsum(
                "grij,igrd->jgd", grad_scores, query_rows, preferred_element_type=jnp.float32
            )
            * score_scale
        )
        grad_values = jnp.einsum(
            "grij,igrd->jgd", probs_low, grad_rows, preferred_element_type=jnp.float32
        )
        return jnp.concatenate(
            [grad_keys.reshape(row_count, kv_width), grad_values.reshape(row_count, kv_width)],
            axis=1,
        )

    start_dq = jnp.zeros((kv_heads, query_group_size, row_count, HEAD_SIZE), jnp.float32)
    start_kv = jnp.zeros((row_count * cycle_size, 2 * kv_width), jnp.float32)
    back_piece = lax.all_gather(kv_rows, "blk", axis=0, tiled=True)

    def back_one_step(block_step, running):
        key_start = block_step * row_count

        def back_work(running):
            grad_query_acc, grad_kv_acc = running
            key_rows, value_rows = split_kv(back_piece, block_step)
            key_place = key_start + offsets
            key_seg, _ = doc_places(lengths, key_place)
            grad_scores, probs_low = score_grads(
                query_four,
                grad_four,
                log_sum,
                delta,
                segment,
                places,
                key_rows,
                value_rows,
                key_seg,
                key_place,
            )
            grad_query_acc = grad_query_acc + query_grads(grad_scores, key_rows)
            earlier = lax.dynamic_slice_in_dim(grad_kv_acc, key_start, row_count, 0)
            added = earlier + key_value_grads(grad_scores, probs_low, query_four, grad_four)
            return (
                grad_query_acc,
                lax.dynamic_update_slice_in_dim(grad_kv_acc, added, key_start, 0),
            )

        return lax.cond(key_start <= first_row, back_work, keep_same, running)

    grad_query_four, grad_kv_all = lax.fori_loop(
        0, back_piece.shape[0] // row_count, back_one_step, (start_dq, start_kv)
    )
    grad_kv = lax.psum_scatter(grad_kv_all, "blk", scatter_dimension=0, tiled=True)
    grad_query_rows = jnp.transpose(grad_query_four, (2, 0, 1, 3)).reshape(
        row_count, q_heads * HEAD_SIZE
    )
    grad_query_low = apply_rotary(grad_query_rows, token_position, q_heads, -1.0).astype(
        jnp.bfloat16
    )
    grad_key_low = apply_rotary(grad_kv[:, :kv_width], token_position, kv_heads, -1.0).astype(
        jnp.bfloat16
    )
    grad_value_low = grad_kv[:, kv_width:].astype(jnp.bfloat16)
    grad_query = left_product(first_layer_norm, grad_query_low)
    grad_key = left_product(first_layer_norm, grad_key_low)
    grad_value = left_product(first_layer_norm, grad_value_low)
    grad_ln_part = (
        right_product(grad_query_low, w_query)
        + right_product(grad_key_low, key_projection_weight)
        + right_product(grad_value_low, value_projection_weight)
    )
    grad_ln_one = lax.psum(grad_ln_part, "tp")
    grad_input_norm, grad_attn_gain = norm_back(grad_ln_one, normed_one, inverse_one, attn_gain)
    input_grad = (grad_middle + grad_input_norm).astype(jnp.bfloat16)
    summed = (
        lax.psum_scatter(grad_query, "blk", scatter_dimension=0, tiled=True),
        lax.psum_scatter(grad_key, "blk", scatter_dimension=0, tiled=True),
        lax.psum_scatter(grad_value, "blk", scatter_dimension=0, tiled=True),
        lax.psum_scatter(grad_out, "blk", scatter_dimension=1, tiled=True),
        lax.psum_scatter(grad_gate, "blk", scatter_dimension=0, tiled=True),
        lax.psum_scatter(grad_up, "blk", scatter_dimension=0, tiled=True),
        lax.psum_scatter(grad_down, "blk", scatter_dimension=1, tiled=True),
        lax.psum_scatter(grad_attn_gain, "blk", scatter_dimension=0, tiled=True),
        lax.psum_scatter(grad_mlp_gain, "blk", scatter_dimension=0, tiled=True),
    )
    return (
        layer_out,
        input_grad,
        summed[0],
        summed[1],
        summed[2],
        summed[3],
        summed[4],
        summed[5],
        summed[6],
        summed[7],
        summed[8],
    )


MESH = pl.DeviceIdType.MESH
F32, BF16 = jnp.float32, jnp.bfloat16
LOG2E = 1.4426950408889634
SCORE_SCALE = HEAD_SIZE**-0.5
VMEM_BYTES = 64 * 2**20 - 2**19
HALF = HEAD_SIZE // 2


def dot_nn(a, b):
    return lax.dot_general(a, b, (((1,), (0,)), ((), ())), preferred_element_type=F32)


def dot_nt(a, b):
    return lax.dot_general(a, b, (((1,), (1,)), ((), ())), preferred_element_type=F32)


def dot_tn(a, b):
    return lax.dot_general(a, b, (((0,), (0,)), ((), ())), preferred_element_type=F32)


class Place:
    def __init__(self):
        self.b = lax.axis_index("blk")
        self.t = lax.axis_index("tp")
        self.core = self.b % 2
        self.chip = self.b // 2
        self.x = self.chip % 2
        self.y = self.b // 4
        self.mate = self.b + 1 - 2 * self.core
        self.inner = jnp.logical_or(self.t == 1, self.t == 2)
        self.outer = jnp.logical_not(self.inner)
        self.pair = self.t + 1 - 2 * (self.t % 2)
        self.across = 3 - self.t

    def slot(self, s):
        core = (self.core + s % 2) % 2
        x = (self.x + (s // 2) % 2) % 2
        y = (self.y + s // 4) % 2
        return (y * 2 + x) * 2 + core

    def chip_at(self, k):
        x = (self.x + (k + 1) % 2) % 2
        y = (self.y + 1 - k // 2) % 2
        return y * 2 + x


def remote(src, dst, ssem, rsem, b, t):
    return pltpu.make_async_remote_copy(
        src_ref=src, dst_ref=dst, send_sem=ssem, recv_sem=rsem, device_id=(b, t), device_id_type=MESH
    )


def enter(me, blk_steps):
    barrier = pltpu.get_barrier_semaphore()
    for s in blk_steps:
        pl.semaphore_signal(barrier, inc=1, device_id=(me.slot(s), me.t), device_id_type=MESH)
    for z in (me.pair, me.across):
        pl.semaphore_signal(barrier, inc=1, device_id=(me.b, z), device_id_type=MESH)
    pl.semaphore_wait(barrier, len(blk_steps) + 2)


class LineSum:
    def __init__(self, me, part, first, second, sems, rows):
        self.me, self.part, self.first, self.second, self.sems, self.rows = (
            me, part, first, second, sems, rows,
        )

    def at(self, ref, p):
        return ref.at[pl.ds(pl.multiple_of(p * self.rows, self.rows), self.rows), :]

    def copy(self, stage, p):
        me = self.me
        src = (self.part, self.part, self.first)[stage]
        dst = (self.first, self.second, self.first)[stage]
        target = (me.pair, me.across, me.pair)[stage]
        return remote(
            self.at(src, p), self.at(dst, p),
            self.sems.at[2 * stage, p], self.sems.at[2 * stage + 1, p], me.b, target,
        )

    def give(self, p):
        @pl.when(self.me.outer)
        def _():
            self.copy(0, p).start()

    def fold(self, p):
        @pl.when(self.me.inner)
        def _():
            self.copy(0, p).wait_recv()
            mine, got = self.at(self.part, p), self.at(self.first, p)
            mine[...] = (mine[...].astype(F32) + got[...].astype(F32)).astype(BF16)
            self.copy(1, p).start()

    def unfold(self, p):
        @pl.when(self.me.inner)
        def _():
            self.copy(1, p).wait_recv()
            mine, got, out = self.at(self.part, p), self.at(self.second, p), self.at(self.first, p)
            out[...] = (mine[...].astype(F32) + got[...].astype(F32)).astype(BF16)
            self.copy(2, p).start()

    def take(self, p):
        @pl.when(self.me.outer)
        def _():
            self.copy(2, p).wait_recv()

    def drain(self, pieces):
        def one(p, carry):
            @pl.when(self.me.outer)
            def _():
                self.copy(0, p).wait_send()

            @pl.when(self.me.inner)
            def _():
                self.copy(1, p).wait_send()
                self.copy(2, p).wait_send()

            return carry

        lax.fori_loop(0, pieces, one, 0)


class LineGather:
    def __init__(self, me, view, ssem, rsem, last):
        self.me, self.view, self.ssem, self.rsem, self.last = me, view, ssem, rsem, last

    def copy(self, way, hop, p):
        t = self.me.t

        def sent():
            slot = t - (hop - 1) if way == 0 else t + (hop - 1)
            ref = self.view(slot, p)
            target = t + 1 if way == 0 else t - 1
            return remote(ref, ref, self.ssem.at[way, hop - 1, p], self.rsem.at[way, hop - 1, p], self.me.b, target)

        def got():
            slot = t - hop if way == 0 else t + hop
            ref = self.view(slot, p)
            target = t - 1 if way == 0 else t + 1
            return remote(ref, ref, self.ssem.at[way, hop - 1, p], self.rsem.at[way, hop - 1, p], self.me.b, target)

        return sent, got

    def sends(self, way, hop):
        t = self.me.t
        if way == 0:
            return jnp.logical_and(t - (hop - 1) >= 0, t + 1 <= self.last)
        return jnp.logical_and(t + (hop - 1) <= self.last, t >= 1)

    def gets(self, way, hop):
        t = self.me.t
        return t - hop >= 0 if way == 0 else t + hop <= self.last

    def send(self, hop, p):
        for way in (0, 1):

            @pl.when(self.sends(way, hop))
            def _(way=way):
                self.copy(way, hop, p)[0]().start()

    def step(self, hop, p, also=None):
        for way in (0, 1):

            @pl.when(self.gets(way, hop))
            def _(way=way):
                self.copy(way, hop, p)[1]().wait_recv()
                if also is not None:
                    also(way, hop).start()

        if hop < self.last:
            self.send(hop + 1, p)

    def drain(self, p):
        for hop in range(1, self.last + 1):
            for way in (0, 1):

                @pl.when(self.sends(way, hop))
                def _(way=way, hop=hop):
                    self.copy(way, hop, p)[0]().wait_send()


class BlockSum:
    def __init__(self, me, make, outs, held, mates, chips, sems):
        self.me, self.make, self.outs = me, make, outs
        self.held, self.mates, self.chips, self.sems = held, mates, chips, sems

    def to_mate(self, k):
        me = self.me
        return remote(
            self.held(k % 2), self.mates(k), self.sems.at[0, k], self.sems.at[1, k], me.mate, me.t
        )

    def to_chip(self, k):
        me = self.me
        return remote(
            self.mates(k), self.chips(k), self.sems.at[2, k], self.sems.at[3, k],
            me.chip_at(k) * 2 + me.core, me.t,
        )

    def lend(self, k):
        me = self.me
        if k >= 2:
            self.to_mate(k - 2).wait_send()
        held = self.held(k % 2)
        even = me.core == 0
        for (lo, hi, value), out in zip(self.make(me.chip_at(k)), self.outs):
            half = value.shape[0] // 2
            low, high = value[:half], value[half:]
            held[:, lo:hi] = jnp.where(even, high, low).astype(BF16)
            out[...] = jnp.where(even, low, high)
        self.to_mate(k).start()

    def merge(self, k, spans):
        self.to_mate(k).wait_recv()
        mates = self.mates(k)
        for (lo, hi), out in zip(spans, self.outs):
            total = out[...] + mates[:, lo:hi].astype(F32)
            if k < 3:
                mates[:, lo:hi] = total.astype(BF16)
            else:
                out[...] = total
        if k < 3:
            self.to_chip(k).start()

    def finish(self, spans):
        for k in range(3):
            self.to_chip(k).wait_recv()
            chips = self.chips(k)
            for (lo, hi), out in zip(spans, self.outs):
                out[...] += chips[:, lo:hi].astype(F32)

    def drain(self):
        for k in (2, 3):
            self.to_mate(k).wait_send()
        for k in range(3):
            self.to_chip(k).wait_send()


def norm_rows(values):
    inverse = lax.rsqrt(jnp.mean(values * values, axis=-1, keepdims=True) + norm_eps)
    return values * inverse, inverse


def turn(values, cs_ref, sign):
    cosine, sine = cs_ref[0:HALF, :], cs_ref[HALF:HEAD_SIZE, :] * sign
    pieces = []
    for h in range(values.shape[0] // HEAD_SIZE):
        low = values[h * HEAD_SIZE : h * HEAD_SIZE + HALF]
        high = values[h * HEAD_SIZE + HALF : (h + 1) * HEAD_SIZE]
        pieces.append(low * cosine - high * sine)
        pieces.append(high * cosine + low * sine)
    return jnp.concatenate(pieces, axis=0)


def fill_bias(bias, st_ref, key_start, query_start):
    key_place = lax.broadcasted_iota(jnp.int32, bias.shape, 0) + key_start
    query_place = lax.broadcasted_iota(jnp.int32, bias.shape, 1) + query_start
    allowed = jnp.logical_and(key_place >= st_ref[0:1, :], key_place <= query_place)
    bias[...] = jnp.where(allowed, 0.0, neg_fill)


def heads_of(h, group):
    g = h // group
    return slice(h * HEAD_SIZE, (h + 1) * HEAD_SIZE), slice(g * HEAD_SIZE, (g + 1) * HEAD_SIZE), g


def layer_kernel(
    dims,
    len_ref, ag_ref, mg_ref, hid_hbm, og_hbm, wq_hbm, wk_hbm, wv_hbm, wo_hbm, wg_hbm, wu_hbm, wd_hbm,
    lo_out, ig_out, gq_ref, gk_ref, gv_ref, go_ref, gg_ref, gu_ref, gd_ref, gag_ref, gmg_ref,
    hid, og, wq, wkv, wo, wg, wu, wd, kv, norm, attn, qt, ot, bias, mid, act, dg, du,
    p2, a2, b2, p3, a3, b3, dbr, dot_ref, dq, acc, low_t, dqr, dkvr,
    kv_mates, kv_chips, held_a, held_b, chips_b, held_c, mates_c, chips_c, total_c,
    turns, starts, m_ref, l_ref, lse, delta, gain, gain_in,
    load_sem, kv_sem, wo_sem, wo_mate_sem, at_sem, sem2, sem3, sem4, kvs_sem, rs_sem, gain_sem, out_sem,
    mate_ready, chip_ready,
):
    rows, piece, chunk, share = dims["rows"], dims["piece"], dims["chunk"], dims["share"]
    q_heads, group, kv_width, n_docs = dims["q_heads"], dims["group"], dims["kv_width"], dims["n_docs"]
    n_pieces, n_chunks = rows // piece, rows // chunk
    per = chunk // piece
    width, hidden_units = wg.shape
    q_width = q_heads * HEAD_SIZE
    last = wo.shape[0] - 1
    me = Place()
    scale2 = SCORE_SCALE * LOG2E

    def each(f, lo, hi):
        def one(p, carry):
            f(p)
            return carry

        lax.fori_loop(lo, hi, one, 0)

    barrier = pltpu.get_barrier_semaphore()
    for s in range(1, 8):
        pl.semaphore_signal(barrier, inc=1, device_id=(me.slot(s), me.t), device_id_type=MESH)
    for z in (me.pair, me.across):
        pl.semaphore_signal(barrier, inc=1, device_id=(me.b, z), device_id_type=MESH)
    loads = {}
    for i, (name, source, target) in enumerate((
        ("hid", hid_hbm, hid), ("wo", wo_hbm, wo.at[me.t]), ("wk", wk_hbm, wkv.at[0:kv_width]),
        ("wv", wv_hbm, wkv.at[kv_width : 2 * kv_width]), ("wq", wq_hbm, wq), ("wg", wg_hbm, wg),
        ("wu", wu_hbm, wu), ("og", og_hbm, og), ("wd", wd_hbm, wd),
    )):
        loads[name] = pltpu.make_async_copy(source, target, load_sem.at[i])
        loads[name].start()

    places = me.b * rows + lax.broadcasted_iota(jnp.int32, (1, rows), 1)
    start, end = jnp.zeros((1, rows), jnp.int32), jnp.int32(0)
    for k in range(n_docs):
        end = end + len_ref[k]
        start = jnp.where(places >= end, end, start)
    starts[...] = jnp.broadcast_to(start, starts.shape)
    order = lax.broadcasted_iota(jnp.int32, (HALF, 1), 0).astype(F32)
    freqs = jnp.exp(order * (-2.0 / HEAD_SIZE * math.log(rope_base)))
    angle = freqs * (places - start).astype(F32)
    turns[0:HALF, :] = jnp.cos(angle)
    turns[HALF:HEAD_SIZE, :] = jnp.sin(angle)
    attn_gain, mlp_gain = ag_ref[...].reshape(1, width), mg_ref[...].reshape(1, width)

    def chunk_rows(c):
        return pl.ds(pl.multiple_of(c * chunk, chunk), chunk)

    def first_norm(c):
        r = chunk_rows(c)
        normed, _ = norm_rows(hid[r, :].astype(F32))
        norm[r, :] = (normed * attn_gain).astype(BF16)

    loads["hid"].wait()
    each(first_norm, 0, n_chunks)
    loads["wo"].wait()
    pl.semaphore_wait(barrier, 9)

    my_half = pl.ds(pl.multiple_of(me.core * share, share), share)
    whole_wo = LineGather(me, lambda slot, p: wo.at[slot, my_half, :], wo_sem.at[0], wo_sem.at[1], last)

    def wo_to_mate(way, hop):
        slot = me.t - hop if way == 0 else me.t + hop
        ref = wo.at[slot, my_half, :]
        return remote(
            ref, ref, wo_mate_sem.at[0, way, hop - 1], wo_mate_sem.at[1, way, hop - 1], me.mate, me.t
        )

    whole_wo.send(1, 0)

    loads["wk"].wait()
    loads["wv"].wait()
    both_t = dot_nt(wkv[...], norm[...])
    kv[me.b, 0:kv_width, :] = turn(both_t[0:kv_width], turns, 1.0).astype(BF16)
    kv[me.b, kv_width : 2 * kv_width, :] = both_t[kv_width : 2 * kv_width].astype(BF16)

    def kv_copy(slot, target, n):
        return remote(kv.at[slot], kv.at[slot], kv_sem.at[0, n], kv_sem.at[1, n], target, me.t)

    def share_kv(s):
        @pl.when(me.slot(s) > me.b)
        def _():
            kv_copy(me.b, me.slot(s), s).start()

    for s in (1, 2, 4):
        share_kv(s)
    loads["wq"].wait()
    qt[...] = turn(dot_nn(norm[...], wq[...]).T, turns, 1.0).astype(BF16)
    m_ref[...] = jnp.full(m_ref.shape, neg_fill, F32)
    l_ref[...] = jnp.zeros(l_ref.shape, F32)
    ot[...] = jnp.zeros(ot.shape, F32)

    def attend(s, carry):
        slot = me.slot(s)
        arrives = jnp.logical_and(s > 0, slot < me.b)

        @pl.when(arrives)
        def _():
            kv_copy(slot, me.mate, s).wait_recv()

        @pl.when(jnp.logical_and(arrives, s % 2 == 0))
        def _():
            kv_copy(slot, me.mate, s + 1).start()

        @pl.when(s == 5)
        def _():
            whole_wo.step(1, 0, wo_to_mate)

        @pl.when(slot <= me.b)
        def _():
            fill_bias(bias, starts, slot * rows, me.b * rows)
            for h in range(q_heads):
                qs, ks, g = heads_of(h, group)
                vs = slice(kv_width + g * HEAD_SIZE, kv_width + (g + 1) * HEAD_SIZE)
                scores = dot_tn(kv[slot, ks, :], qt[qs, :]) + bias[...]
                old = m_ref[h : h + 1, :]
                new = jnp.maximum(old, jnp.max(scores, axis=0, keepdims=True))
                probs = jnp.exp2((scores - new) * scale2)
                keep = jnp.exp2((old - new) * scale2)
                m_ref[h : h + 1, :] = new
                l_ref[h : h + 1, :] = l_ref[h : h + 1, :] * keep + jnp.sum(probs, axis=0, keepdims=True)
                ot[qs, :] = ot[qs, :] * keep + dot_nn(kv[slot, vs, :], probs.astype(BF16))

        @pl.when(s == 1)
        def _():
            share_kv(6)

        return carry

    lax.fori_loop(0, 8, attend, 0)
    whole_wo.step(2, 0, wo_to_mate)

    line_attn = LineGather(
        me, lambda slot, p: attn.at[slot, chunk_rows(p), :], at_sem.at[0], at_sem.at[1], last
    )
    for h in range(q_heads):
        qs, _, _ = heads_of(h, group)
        ot[qs, :] = ot[qs, :] / l_ref[h : h + 1, :]
    for c in range(n_chunks):
        attn[me.t, c * chunk : (c + 1) * chunk, :] = ot[:, c * chunk : (c + 1) * chunk].T.astype(BF16)
        if c < 2:
            line_attn.send(1, c)
    lse[...] = jnp.zeros(lse.shape, F32)
    lse[0:q_heads, :] = m_ref[0:q_heads, :] * scale2 + jnp.log2(l_ref[0:q_heads, :])
    for name in ("wg", "wu", "og", "wd"):
        loads[name].wait()
    for hop in range(1, last + 1):
        line_attn.step(hop, 0)
    whole_wo.step(3, 0, wo_to_mate)
    for hop in range(1, last + 1):
        for way in (0, 1):

            @pl.when(whole_wo.gets(way, hop))
            def _(way=way, hop=hop):
                wo_to_mate(way, hop).wait_recv()

    back = LineSum(me, p2, a2, b2, sem2, piece)
    forth = LineSum(me, p3, a3, b3, sem3, piece)
    adds_middle = (me.t == 1).astype(F32)

    def feed(c, carry):
        r = chunk_rows(c)
        for n in range(0, width, 512):
            ns = slice(n, n + 512)
            total = hid[r, ns].astype(F32)
            for z in range(last + 1):
                total = total + dot_nn(attn[z, r, :], wo[z, :, ns])
            mid[r, ns] = total
        normed, _ = norm_rows(mid[r, :])
        norm[r, :] = (normed * mlp_gain).astype(BF16)

        @pl.when(c >= 1)
        def _():
            each(back.fold, (c - 1) * per, c * per)

        @pl.when(c < n_chunks - 1)
        def _():
            line_attn.step(1, c + 1)

        for n in range(0, hidden_units, 512):
            ns = slice(n, n + 512)
            gate = dot_nn(norm[r, :], wg[:, ns])
            up = dot_nn(norm[r, :], wu[:, ns])
            grad = dot_nt(og[r, :], wd[ns, :])
            sig = 1.0 / (1.0 + jnp.exp(-gate))
            silu = gate * sig
            act[r, ns] = (silu * up).astype(BF16)
            dg[r, ns] = (grad * up * sig * (1.0 + gate * (1.0 - sig))).astype(BF16)
            du[r, ns] = (grad * silu).astype(BF16)
            if n == 0:

                @pl.when(c < n_chunks - 1)
                def _():
                    line_attn.step(2, c + 1)

                @pl.when(c < n_chunks - 2)
                def _():
                    line_attn.send(1, c + 2)

        for n in range(0, width, 512):
            ns = slice(n, n + 512)
            p2[r, ns] = (dot_nt(dg[r, :], wg[ns, :]) + dot_nt(du[r, :], wu[ns, :])).astype(BF16)
        each(back.give, c * per, (c + 1) * per)

        @pl.when(c >= 1)
        def _():
            each(back.unfold, (c - 1) * per, c * per)

        @pl.when(c < n_chunks - 1)
        def _():
            line_attn.step(3, c + 1)

        for n in range(0, width, 512):
            ns = slice(n, n + 512)
            p3[r, ns] = (dot_nn(act[r, :], wd[:, ns]) + mid[r, ns] * adds_middle).astype(BF16)
        return carry

    lax.fori_loop(0, n_chunks, feed, 0)
    pl.semaphore_signal(mate_ready, inc=1, device_id=(me.mate, me.t), device_id_type=MESH)
    for k in range(3):
        pl.semaphore_signal(
            chip_ready, inc=1, device_id=(me.chip_at(k) * 2 + me.core, me.t), device_id_type=MESH
        )
    each(forth.give, 0, n_pieces)
    pair = 2 * share

    def pair_columns(ref, chip):
        return ref[:, pl.ds(pl.multiple_of(chip * pair, pair), pair)]

    def slots(ref, first, columns):
        return lambda k: ref.at[(first + k) * share : (first + k + 1) * share, 0:columns]

    sum_gate = BlockSum(
        me, lambda m: [(0, hidden_units, dot_tn(pair_columns(norm, m), dg[...]))], [gg_ref],
        lambda k: held_a.at[0, k], slots(wg, 0, hidden_units), slots(wg, 4, hidden_units), rs_sem.at[0],
    )
    sum_up = BlockSum(
        me, lambda m: [(0, hidden_units, dot_tn(pair_columns(norm, m), du[...]))], [gu_ref],
        lambda k: held_a.at[1, k], slots(wu, 0, hidden_units), slots(wu, 4, hidden_units), rs_sem.at[1],
    )
    span_a = [(0, hidden_units)]
    pl.semaphore_wait(mate_ready, 1)
    gain[...] = jnp.zeros(gain.shape, F32)

    def middle_grad(c):
        each(back.take, c * per, (c + 1) * per)
        r = chunk_rows(c)
        normed, inverse = norm_rows(mid[r, :])
        grad = a2[r, :].astype(F32)
        scaled = grad * mlp_gain
        gain[1:2, :] += jnp.sum(grad * normed, axis=0, keepdims=True)
        found = og[r, :].astype(F32) + inverse * (
            scaled - normed * jnp.mean(scaled * normed, axis=-1, keepdims=True)
        )
        mid[r, :] = found
        dbr[r, :] = found.astype(BF16)

    sum_gate.lend(0)
    sum_up.lend(0)
    each(back.fold, n_pieces - per, n_pieces)
    pl.semaphore_wait(chip_ready, 3)
    sum_gate.merge(0, span_a)
    sum_up.merge(0, span_a)
    sum_gate.lend(1)
    sum_up.lend(1)
    each(back.unfold, n_pieces - per, n_pieces)
    sum_gate.merge(1, span_a)
    sum_up.merge(1, span_a)
    each(middle_grad, 0, n_chunks - 1)
    sum_gate.lend(2)
    sum_up.lend(2)
    each(middle_grad, n_chunks - 1, n_chunks)
    dot_ref[...] = dot_nt(wo[me.t], dbr[...]).astype(BF16)
    sum_gate.merge(2, span_a)
    sum_up.merge(2, span_a)
    delta[...] = jnp.zeros(delta.shape, F32)
    for h in range(q_heads):
        qs, _, _ = heads_of(h, group)
        delta[h : h + 1, :] = jnp.sum(dot_ref[qs, :].astype(F32) * ot[qs, :], axis=0, keepdims=True)
    dq[...] = jnp.zeros(dq.shape, F32)
    back.drain(n_pieces)

    for s in (1, 2, 4, 6):

        @pl.when(me.slot(s) > me.b)
        def _(s=s):
            kv_copy(me.b, me.slot(s), s).wait_send()

    for s in (2, 4, 6):

        @pl.when(me.slot(s) < me.b)
        def _(s=s):
            kv_copy(me.slot(s), me.mate, s + 1).wait_send()

    def kv_to_mate(k):
        return remote(
            kv.at[me.chip_at(k) * 2 + 1 - me.core], kv_mates.at[k], kvs_sem.at[0, k], kvs_sem.at[1, k],
            me.mate, me.t,
        )

    def kv_to_chip(k):
        return remote(
            kv_mates.at[k], kv_chips.at[k], kvs_sem.at[2, k], kvs_sem.at[3, k],
            me.chip_at(k) * 2 + me.core, me.t,
        )

    def attend_back(u, carry):
        k, own = u // 2, u % 2
        chip = me.chip_at(k)
        slot = chip * 2 + (me.core + 1 - own) % 2
        forth.fold(u)

        @pl.when(u >= 1)
        def _():
            forth.unfold(u - 1)

        @pl.when(slot <= me.b)
        def _():
            fill_bias(bias, starts, slot * rows, me.b * rows)
            for g in range(q_heads // group):
                ks = slice(g * HEAD_SIZE, (g + 1) * HEAD_SIZE)
                vs = slice(kv_width + g * HEAD_SIZE, kv_width + (g + 1) * HEAD_SIZE)
                key_t, value_t = kv[slot, ks, :], kv[slot, vs, :]
                grad_k = grad_v = None
                for h in range(g * group, (g + 1) * group):
                    qs, _, _ = heads_of(h, group)
                    query_t, grad_t = qt[qs, :], dot_ref[qs, :]
                    scores = dot_tn(key_t, query_t) + bias[...]
                    probs = jnp.exp2(scores * scale2 - lse[h : h + 1, :])
                    grad_p = dot_tn(value_t, grad_t)
                    grad_s = (probs * (grad_p - delta[h : h + 1, :])).astype(BF16)
                    one_v = dot_nt(grad_t, probs.astype(BF16))
                    one_k = dot_nt(query_t, grad_s)
                    grad_v = one_v if grad_v is None else grad_v + one_v
                    grad_k = one_k if grad_k is None else grad_k + one_k
                    dq[qs, :] += dot_nn(key_t, grad_s)
                acc[ks, :] = grad_k
                acc[vs, :] = grad_v

        @pl.when(jnp.logical_and(own == 0, slot <= me.b))
        def _():
            kv[slot] = acc[...].astype(BF16)
            kv_to_mate(k).start()

        @pl.when(jnp.logical_and(own == 1, chip < me.chip))
        def _():
            kv_to_mate(k).wait_recv()
            kv_mates[k] = (acc[...] + kv_mates[k].astype(F32)).astype(BF16)
            kv_to_chip(k).start()

        return carry

    lax.fori_loop(0, 8, attend_back, 0)
    forth.unfold(n_pieces - 1)
    low_t[0:q_width, :] = turn(dq[...] * SCORE_SCALE, turns, -1.0).astype(BF16)
    dqr[...] = low_t[0:q_width, :].T

    def first_norm_again(c):
        r = chunk_rows(c)
        normed, _ = norm_rows(hid[r, :].astype(F32))
        norm[r, :] = (normed * attn_gain).astype(BF16)

    sum_gate.lend(3)
    sum_up.lend(3)
    each(first_norm_again, 0, n_chunks)
    sum_gate.merge(3, span_a)
    sum_up.merge(3, span_a)

    @pl.when(me.core == 0)
    def _():
        kv_to_mate(3).wait_recv()
        acc[...] += kv_mates[3].astype(F32)

    for k in range(3):

        @pl.when(me.chip_at(k) > me.chip)
        def _(k=k):
            kv_to_chip(k).wait_recv()
            acc[...] += kv_chips[k].astype(F32)

    low_t[q_width : q_width + kv_width, :] = turn(acc[0:kv_width, :] * SCORE_SCALE, turns, -1.0).astype(BF16)
    low_t[q_width + kv_width :, :] = acc[kv_width : 2 * kv_width, :].astype(BF16)
    dkvr[...] = low_t[q_width:, :].T

    each(forth.take, 0, n_pieces)
    lo_save = pltpu.make_async_copy(a3, lo_out, out_sem.at[0])
    lo_save.start()
    end_sum = LineSum(me, p2, a2, b2, sem4, piece)

    def input_part(c):
        r = chunk_rows(c)
        for n in range(0, width, 512):
            ns = slice(n, n + 512)
            p2[r, ns] = (dot_nt(dqr[r, :], wq[ns, :]) + dot_nn(dkvr[r, :], wkv[:, ns])).astype(BF16)
        each(end_sum.give, c * per, (c + 1) * per)

    each(input_part, 0, n_chunks)

    def make_b(m):
        yield 0, hidden_units, dot_tn(pair_columns(og, m), act[...])
        yield hidden_units, hidden_units + q_width, dot_tn(pair_columns(dbr, m), attn[me.t])

    def make_c(m):
        columns = pair_columns(norm, m)
        yield 0, q_width, dot_tn(columns, dqr[...])
        yield q_width, q_width + 2 * kv_width, dot_tn(columns, dkvr[...])

    width_b = hidden_units + q_width
    in_wd = slots(wd, 0, width_b)
    sum_b = BlockSum(
        me, make_b, [gd_ref, go_ref], lambda k: held_b.at[k], in_wd,
        lambda k: in_wd(4) if k == 0 else chips_b.at[k - 1], rs_sem.at[2],
    )
    span_b = [(0, hidden_units), (hidden_units, width_b)]
    total_parts = [total_c.at[:, 0:q_width], total_c.at[:, q_width : q_width + 2 * kv_width]]
    sum_c = BlockSum(
        me, make_c, total_parts, lambda k: held_c.at[k], lambda k: mates_c.at[k], lambda k: chips_c.at[k],
        rs_sem.at[3],
    )
    span_c = [(0, q_width), (q_width, q_width + 2 * kv_width)]
    work = []
    for sums, spans in ((sum_b, span_b), (sum_c, span_c)):
        for k in range(4):
            work.append((sums, k, spans))
    for p in range(n_pieces):
        if p >= 1:
            sums, k, spans = work[p - 1]
            sums.merge(k, spans)
        sums, k, spans = work[p]
        sums.lend(k)
        end_sum.fold(p)
        if p >= 1:
            end_sum.unfold(p - 1)
    end_sum.unfold(n_pieces - 1)
    sums, k, spans = work[n_pieces - 1]
    sums.merge(k, spans)

    def input_rows(c):
        each(end_sum.take, c * per, (c + 1) * per)
        r = chunk_rows(c)
        normed, inverse = norm_rows(hid[r, :].astype(F32))
        grad = a2[r, :].astype(F32)
        scaled = grad * attn_gain
        gain[0:1, :] += jnp.sum(grad * normed, axis=0, keepdims=True)
        found = inverse * (scaled - normed * jnp.mean(scaled * normed, axis=-1, keepdims=True))
        dbr[r, :] = (mid[r, :] + found).astype(BF16)

    each(input_rows, 0, n_chunks)

    def gain_copy(s):
        return remote(gain, gain_in.at[s], gain_sem.at[0, s], gain_sem.at[1, s], me.slot(s), me.t)

    for s in range(1, 8):
        gain_copy(s).start()
    ig_save = pltpu.make_async_copy(dbr, ig_out, out_sem.at[1])
    ig_save.start()
    sum_gate.finish(span_a)
    sum_up.finish(span_a)
    sum_b.finish(span_b)
    sum_c.finish(span_c)
    gq_ref[...] = total_c[:, 0:q_width]
    gk_ref[...] = total_c[:, q_width : q_width + kv_width]
    gv_ref[...] = total_c[:, q_width + kv_width : q_width + 2 * kv_width]
    for s in range(1, 8):
        gain_copy(s).wait_recv()
    gains = gain[...]
    for s in range(1, 8):
        gains = gains + gain_in[s]
    gain_in[0] = gains
    mine = jnp.zeros((8, share), F32)
    for j in range(8):
        mine = mine + jnp.where(me.b == j, gain_in[0, :, j * share : (j + 1) * share], 0.0)
    gag_ref[...] = mine[0, :]
    gmg_ref[...] = mine[1, :]

    for s in range(1, 8):
        gain_copy(s).wait_send()
    whole_wo.drain(0)
    for hop in range(1, last + 1):
        for way in (0, 1):

            @pl.when(whole_wo.gets(way, hop))
            def _(way=way, hop=hop):
                wo_to_mate(way, hop).wait_send()

    each(line_attn.drain, 0, n_chunks)
    forth.drain(n_pieces)
    end_sum.drain(n_pieces)
    for sums in (sum_gate, sum_up, sum_b, sum_c):
        sums.drain()
    for k in range(4):
        chip = me.chip_at(k)
        slot = chip * 2 + 1 - me.core

        @pl.when(slot <= me.b)
        def _(k=k):
            kv_to_mate(k).wait_send()

        if k < 3:

            @pl.when(chip < me.chip)
            def _(k=k):
                kv_to_chip(k).wait_send()

    lo_save.wait()
    ig_save.wait()


def hand_over(n, *refs):
    sources, targets, held, sems = refs[:n], refs[n : 2 * n], refs[2 * n : 3 * n], refs[3 * n]
    ins = [pltpu.make_async_copy(a, h, sems.at[0, i]) for i, (a, h) in enumerate(zip(sources, held))]
    outs = [pltpu.make_async_copy(h, b, sems.at[1, i]) for i, (h, b) in enumerate(zip(held, targets))]
    for copy in ins:
        copy.start()
    for first, second in zip(ins, outs):
        first.wait()
        second.start()
    for copy in outs:
        copy.wait()


def kernel_shards(
    hidden_in, out_grad, lengths, attn_gain, w_query, key_projection_weight, value_projection_weight,
    w_out, mlp_gain, w_gate, w_up, w_down,
):
    rows, width = hidden_in.shape
    q_width, kv_width = w_query.shape[1], key_projection_weight.shape[1]
    hidden_units = w_gate.shape[1]
    blocks, line_size = lax.axis_size("blk"), lax.axis_size("tp")
    share = width // blocks
    piece, chunk = rows // 8, rows // 4
    pieces, chunks = rows // piece, rows // chunk
    dims = dict(
        rows=rows, piece=piece, chunk=chunk, share=share, q_heads=q_width // HEAD_SIZE,
        group=q_width // kv_width, kv_width=kv_width, n_docs=lengths.shape[0],
    )
    vmem, hbm = pl.BlockSpec(memory_space=pltpu.VMEM), pl.BlockSpec(memory_space=pl.ANY)
    smem = pl.BlockSpec(memory_space=pltpu.SMEM)
    dma, regular = pltpu.SemaphoreType.DMA, pltpu.SemaphoreType.REGULAR

    def shape(dtype, *dims_):
        return jax.ShapeDtypeStruct(dims_, dtype)

    def low(*dims_):
        return pltpu.VMEM(dims_, BF16)

    def full(*dims_):
        return pltpu.VMEM(dims_, F32)

    line = [low(rows, width)] * 3
    width_b, width_c = hidden_units + q_width, q_width + 2 * kv_width
    shapes = (
        shape(BF16, rows, width), shape(BF16, rows, width), shape(F32, share, q_width),
        shape(F32, share, kv_width), shape(F32, share, kv_width), shape(F32, share, q_width),
        shape(F32, share, hidden_units), shape(F32, share, hidden_units), shape(F32, share, hidden_units),
        shape(F32, share), shape(F32, share),
    )
    outs = pl.pallas_call(
        functools.partial(layer_kernel, dims),
        out_shape=shapes,
        in_specs=[smem, vmem, vmem] + [hbm] * 9,
        out_specs=(hbm, hbm) + (vmem,) * 9,
        scratch_shapes=[
            low(rows, width), low(rows, width), low(width, q_width), low(2 * kv_width, width),
            low(line_size, q_width, width), low(width, hidden_units), low(width, hidden_units),
            low(hidden_units, width), low(blocks, 2 * kv_width, rows), low(rows, width),
            low(line_size, rows, q_width), low(q_width, rows), full(q_width, rows), full(rows, rows),
            full(rows, width), low(rows, hidden_units), low(rows, hidden_units), low(rows, hidden_units),
            *line, *line, low(rows, width), low(q_width, rows), full(q_width, rows), full(2 * kv_width, rows),
            low(width_c, rows), low(rows, q_width), low(rows, 2 * kv_width),
            low(4, 2 * kv_width, rows), low(3, 2 * kv_width, rows),
            low(2, 2, share, hidden_units), low(2, share, width_b), low(2, share, width_b),
            low(2, share, width_c), low(4, share, width_c), low(3, share, width_c), full(share, width_c),
            full(HEAD_SIZE, rows), pltpu.VMEM((8, rows), jnp.int32), full(8, rows), full(8, rows), full(8, rows),
            full(8, rows), full(8, width), full(8, 8, width),
            dma((9,)), dma((2, 8)), dma((2, 2, line_size - 1, 1)), dma((2, 2, line_size - 1)),
            dma((2, 2, line_size - 1, chunks)), dma((6, pieces)), dma((6, pieces)), dma((6, pieces)),
            dma((4, 4)), dma((4, 4, 4)), dma((2, 8)), dma((2,)), regular, regular,
        ],
        compiler_params=pltpu.CompilerParams(
            collective_id=0, has_side_effects=True, vmem_limit_bytes=VMEM_BYTES
        ),
    )(
        lengths, attn_gain, mlp_gain, hidden_in, out_grad, w_query, key_projection_weight.T,
        value_projection_weight.T, w_out, w_gate, w_up, w_down,
    )
    outs = pl.pallas_call(
        functools.partial(hand_over, len(shapes)),
        out_shape=shapes,
        in_specs=[hbm] * len(shapes),
        out_specs=(hbm,) * len(shapes),
        scratch_shapes=[pltpu.VMEM(s.shape, s.dtype) for s in shapes] + [dma((2, len(shapes)))],
    )(*outs)
    layer_out, input_grad, grad_query, grad_key, grad_value, grad_out, grad_gate, grad_up, grad_down, g1, g2 = outs
    return (
        layer_out, input_grad, grad_query, grad_key, grad_value, grad_out.T, grad_gate, grad_up, grad_down.T, g1, g2,
    )


def solution(mesh):
    sizes = dict(mesh.shape)
    small = sizes["blk"] == 8 and sizes["tp"] == 4
    placed = (
        P("blk", None),
        P("blk", None),
        P(),
        P(),
        P(None, "tp"),
        P(None, "tp"),
        P(None, "tp"),
        P("tp", None),
        P(),
        P(None, "tp"),
        P(None, "tp"),
        P("tp", None),
    )
    return jax.shard_map(
        kernel_shards if small else shards,
        mesh=mesh,
        in_specs=placed,
        out_specs=(
            P("blk", None),
            P("blk", None),
            P("blk", "tp"),
            P("blk", "tp"),
            P("blk", "tp"),
            P("tp", "blk"),
            P("blk", "tp"),
            P("blk", "tp"),
            P("tp", "blk"),
            P("blk"),
            P("blk"),
        ),
        check_vma=False,
    )
```

```python
import functools
import math

import jax
import jax.numpy as jnp
from jax import lax
from jax.experimental import pallas as pl
from jax.experimental.pallas import tpu as pltpu
from jax.sharding import PartitionSpec as P

HEAD_SIZE = 96


norm_eps = 1e-05
rope_base = 100000.0
neg_fill = -1e30


def doc_places(lengths, places):
    doc_ends = jnp.cumsum(lengths)
    passed = (places[:, None] >= doc_ends[None, :]).astype(jnp.int32)
    segment = jnp.sum(passed, axis=1)
    preceding = jnp.sum(passed * lengths[None, :], axis=1)
    return (segment, places - preceding)


def apply_rotary(values, token_position, heads, sign_value):
    half_size = HEAD_SIZE // 2
    freqs = rope_base ** (-(2.0 * jnp.arange(half_size, dtype=jnp.float32)) / HEAD_SIZE)
    angle = token_position.astype(jnp.float32)[:, None] * freqs[None, :]
    cosine = jnp.cos(angle)[:, None, :]
    sine = sign_value * jnp.sin(angle)[:, None, :]
    shaped = values.reshape(values.shape[0], heads, HEAD_SIZE)
    first_half = shaped[..., :half_size]
    second_half = shaped[..., half_size:]
    turned = jnp.concatenate(
        [first_half * cosine - second_half * sine, second_half * cosine + first_half * sine],
        axis=-1,
    )
    return turned.reshape(values.shape[0], heads * HEAD_SIZE)


def rms_parts(values):
    inverse = lax.rsqrt(jnp.mean(values * values, axis=-1, keepdims=True) + norm_eps)
    return (values * inverse, inverse)


def norm_back(grad_in, normed, inverse, gain):
    scaled = grad_in * gain
    grad_values = inverse * (scaled - normed * jnp.mean(scaled * normed, axis=-1, keepdims=True))
    return (grad_values, jnp.sum(grad_in * normed, axis=0))


def left_product(left_side, right_side):
    return lax.dot_general(
        left_side, right_side, (((0,), (0,)), ((), ())), preferred_element_type=jnp.float32
    )


def right_product(left_side, weight):
    return lax.dot_general(
        left_side, weight, (((1,), (1,)), ((), ())), preferred_element_type=jnp.float32
    )


def score_block(query_four, key_rows, query_seg, query_place, key_seg, key_place):
    score_scale = HEAD_SIZE ** (-0.5)
    scores = (
        jnp.einsum("igrd,jgd->grij", query_four, key_rows, preferred_element_type=jnp.float32)
        * score_scale
    )
    allowed = (query_seg[:, None] == key_seg[None, :]) & (
        key_place[None, :] <= query_place[:, None]
    )
    return (jnp.where(allowed[None, None], scores, neg_fill), allowed)


def score_grads(
    query_four,
    grad_four,
    log_sum,
    delta,
    query_seg,
    query_place,
    key_rows,
    value_rows,
    key_seg,
    key_place,
):
    scores, allowed = score_block(query_four, key_rows, query_seg, query_place, key_seg, key_place)
    probs = jnp.where(allowed[None, None], jnp.exp(scores - log_sum[..., None]), 0.0)
    grad_probs = jnp.einsum(
        "igrd,jgd->grij", grad_four, value_rows, preferred_element_type=jnp.float32
    )
    grad_scores = (probs * (grad_probs - delta[..., None])).astype(jnp.bfloat16)
    return (grad_scores, probs.astype(jnp.bfloat16))


def keep_same(running):
    return running


def shards(
    hidden_in,
    out_grad,
    lengths,
    attn_gain,
    w_query,
    key_projection_weight,
    value_projection_weight,
    w_out,
    mlp_gain,
    w_gate,
    w_up,
    w_down,
):
    row_count = hidden_in.shape[0]
    cycle_size = lax.axis_size("blk")
    first_row = lax.axis_index("blk") * row_count
    offsets = jnp.arange(row_count, dtype=jnp.int32)
    places = first_row + offsets
    segment, token_position = doc_places(lengths, places)
    q_heads = w_query.shape[1] // HEAD_SIZE
    kv_heads = key_projection_weight.shape[1] // HEAD_SIZE
    query_group_size = q_heads // kv_heads
    kv_width = kv_heads * HEAD_SIZE
    score_scale = HEAD_SIZE ** (-0.5)
    hidden_f = hidden_in.astype(jnp.float32)
    normed_one, inverse_one = rms_parts(hidden_f)
    first_layer_norm = (normed_one * attn_gain).astype(jnp.bfloat16)
    query_raw = jnp.dot(first_layer_norm, w_query, preferred_element_type=jnp.float32)
    key_raw = jnp.dot(first_layer_norm, key_projection_weight, preferred_element_type=jnp.float32)
    value_raw = jnp.dot(
        first_layer_norm, value_projection_weight, preferred_element_type=jnp.float32
    )
    query_low = apply_rotary(query_raw, token_position, q_heads, 1.0).astype(jnp.bfloat16)
    key_low = apply_rotary(key_raw, token_position, kv_heads, 1.0).astype(jnp.bfloat16)
    value_low = value_raw.astype(jnp.bfloat16)
    kv_rows = jnp.concatenate([key_low, value_low], axis=1)
    query_four = query_low.reshape(row_count, kv_heads, query_group_size, HEAD_SIZE)

    def split_kv(piece, block_step):
        block_rows = lax.dynamic_slice_in_dim(piece, block_step * row_count, row_count, 0)
        key_rows = block_rows[:, :kv_width].reshape(row_count, kv_heads, HEAD_SIZE)
        value_rows = block_rows[:, kv_width:].reshape(row_count, kv_heads, HEAD_SIZE)
        return (key_rows, value_rows)

    start_max = jnp.full((kv_heads, query_group_size, row_count), neg_fill, jnp.float32)
    start_sum = jnp.zeros((kv_heads, query_group_size, row_count), jnp.float32)
    start_acc = jnp.zeros((kv_heads, query_group_size, row_count, HEAD_SIZE), jnp.float32)
    piece = lax.all_gather(kv_rows, "blk", axis=0, tiled=True)

    def forward_one_step(block_step, running):
        key_start = block_step * row_count

        def forward_work(running):
            row_max, row_sum, weighted = running
            key_rows, value_rows = split_kv(piece, block_step)
            key_place = key_start + offsets
            key_seg, _ = doc_places(lengths, key_place)
            scores, allowed = score_block(query_four, key_rows, segment, places, key_seg, key_place)
            new_max = jnp.maximum(row_max, jnp.max(scores, axis=-1))
            exp_scores = jnp.where(allowed[None, None], jnp.exp(scores - new_max[..., None]), 0.0)
            rescale = jnp.exp(row_max - new_max)
            row_sum = row_sum * rescale + jnp.sum(exp_scores, axis=-1)
            weighted = weighted * rescale[..., None] + jnp.einsum(
                "grij,jgd->grid",
                exp_scores.astype(jnp.bfloat16),
                value_rows,
                preferred_element_type=jnp.float32,
            )
            return (new_max, row_sum, weighted)

        return lax.cond(key_start <= first_row, forward_work, keep_same, running)

    row_max, row_sum, weighted = lax.fori_loop(
        0, piece.shape[0] // row_count, forward_one_step, (start_max, start_sum, start_acc)
    )
    attn_four = weighted / row_sum[..., None]
    log_sum = row_max + jnp.log(row_sum)
    attn_rows = jnp.transpose(attn_four, (2, 0, 1, 3)).reshape(row_count, q_heads * HEAD_SIZE)
    attn_low = attn_rows.astype(jnp.bfloat16)
    branch = lax.psum(jnp.dot(attn_low, w_out, preferred_element_type=jnp.float32), "tp")
    middle = hidden_f + branch
    normed_two, inverse_two = rms_parts(middle)
    ln_two = (normed_two * mlp_gain).astype(jnp.bfloat16)
    gate = jnp.dot(ln_two, w_gate, preferred_element_type=jnp.float32)
    up_proj = jnp.dot(ln_two, w_up, preferred_element_type=jnp.float32)
    sig_gate = jax.nn.sigmoid(gate)
    act_gate = gate * sig_gate
    hidden = (act_gate * up_proj).astype(jnp.bfloat16)
    mlp_branch = lax.psum(jnp.dot(hidden, w_down, preferred_element_type=jnp.float32), "tp")
    layer_out = (middle + mlp_branch).astype(jnp.bfloat16)
    grad_down = left_product(hidden, out_grad)
    grad_hidden = right_product(out_grad, w_down)
    grad_gate_act = (grad_hidden * up_proj * sig_gate * (1.0 + gate * (1.0 - sig_gate))).astype(
        jnp.bfloat16
    )
    grad_up_act = (grad_hidden * act_gate).astype(jnp.bfloat16)
    grad_gate = left_product(ln_two, grad_gate_act)
    grad_up = left_product(ln_two, grad_up_act)
    grad_ln_two = lax.psum(
        right_product(grad_gate_act, w_gate) + right_product(grad_up_act, w_up), "tp"
    )
    grad_middle_norm, grad_mlp_gain = norm_back(grad_ln_two, normed_two, inverse_two, mlp_gain)
    grad_middle = out_grad.astype(jnp.float32) + grad_middle_norm
    grad_branch = grad_middle.astype(jnp.bfloat16)
    grad_out = left_product(attn_low, grad_branch)
    grad_attn = right_product(grad_branch, w_out).astype(jnp.bfloat16)
    grad_four = grad_attn.reshape(row_count, kv_heads, query_group_size, HEAD_SIZE)
    delta = jnp.sum(jnp.transpose(grad_four.astype(jnp.float32), (1, 2, 0, 3)) * attn_four, axis=-1)

    def query_grads(grad_scores, key_rows):
        return (
            jnp.einsum("grij,jgd->grid", grad_scores, key_rows, preferred_element_type=jnp.float32)
            * score_scale
        )

    def key_value_grads(grad_scores, probs_low, query_rows, grad_rows):
        grad_keys = (
            jnp.einsum(
                "grij,igrd->jgd", grad_scores, query_rows, preferred_element_type=jnp.float32
            )
            * score_scale
        )
        grad_values = jnp.einsum(
            "grij,igrd->jgd", probs_low, grad_rows, preferred_element_type=jnp.float32
        )
        return jnp.concatenate(
            [grad_keys.reshape(row_count, kv_width), grad_values.reshape(row_count, kv_width)],
            axis=1,
        )

    start_dq = jnp.zeros((kv_heads, query_group_size, row_count, HEAD_SIZE), jnp.float32)
    start_kv = jnp.zeros((row_count * cycle_size, 2 * kv_width), jnp.float32)
    back_piece = lax.all_gather(kv_rows, "blk", axis=0, tiled=True)

    def back_one_step(block_step, running):
        key_start = block_step * row_count

        def back_work(running):
            grad_query_acc, grad_kv_acc = running
            key_rows, value_rows = split_kv(back_piece, block_step)
            key_place = key_start + offsets
            key_seg, _ = doc_places(lengths, key_place)
            grad_scores, probs_low = score_grads(
                query_four,
                grad_four,
                log_sum,
                delta,
                segment,
                places,
                key_rows,
                value_rows,
                key_seg,
                key_place,
            )
            grad_query_acc = grad_query_acc + query_grads(grad_scores, key_rows)
            earlier = lax.dynamic_slice_in_dim(grad_kv_acc, key_start, row_count, 0)
            added = earlier + key_value_grads(grad_scores, probs_low, query_four, grad_four)
            return (
                grad_query_acc,
                lax.dynamic_update_slice_in_dim(grad_kv_acc, added, key_start, 0),
            )

        return lax.cond(key_start <= first_row, back_work, keep_same, running)

    grad_query_four, grad_kv_all = lax.fori_loop(
        0, back_piece.shape[0] // row_count, back_one_step, (start_dq, start_kv)
    )
    grad_kv = lax.psum_scatter(grad_kv_all, "blk", scatter_dimension=0, tiled=True)
    grad_query_rows = jnp.transpose(grad_query_four, (2, 0, 1, 3)).reshape(
        row_count, q_heads * HEAD_SIZE
    )
    grad_query_low = apply_rotary(grad_query_rows, token_position, q_heads, -1.0).astype(
        jnp.bfloat16
    )
    grad_key_low = apply_rotary(grad_kv[:, :kv_width], token_position, kv_heads, -1.0).astype(
        jnp.bfloat16
    )
    grad_value_low = grad_kv[:, kv_width:].astype(jnp.bfloat16)
    grad_query = left_product(first_layer_norm, grad_query_low)
    grad_key = left_product(first_layer_norm, grad_key_low)
    grad_value = left_product(first_layer_norm, grad_value_low)
    grad_ln_part = (
        right_product(grad_query_low, w_query)
        + right_product(grad_key_low, key_projection_weight)
        + right_product(grad_value_low, value_projection_weight)
    )
    grad_ln_one = lax.psum(grad_ln_part, "tp")
    grad_input_norm, grad_attn_gain = norm_back(grad_ln_one, normed_one, inverse_one, attn_gain)
    input_grad = (grad_middle + grad_input_norm).astype(jnp.bfloat16)
    summed = (
        lax.psum_scatter(grad_query, "blk", scatter_dimension=0, tiled=True),
        lax.psum_scatter(grad_key, "blk", scatter_dimension=0, tiled=True),
        lax.psum_scatter(grad_value, "blk", scatter_dimension=0, tiled=True),
        lax.psum_scatter(grad_out, "blk", scatter_dimension=1, tiled=True),
        lax.psum_scatter(grad_gate, "blk", scatter_dimension=0, tiled=True),
        lax.psum_scatter(grad_up, "blk", scatter_dimension=0, tiled=True),
        lax.psum_scatter(grad_down, "blk", scatter_dimension=1, tiled=True),
        lax.psum_scatter(grad_attn_gain, "blk", scatter_dimension=0, tiled=True),
        lax.psum_scatter(grad_mlp_gain, "blk", scatter_dimension=0, tiled=True),
    )
    return (
        layer_out,
        input_grad,
        summed[0],
        summed[1],
        summed[2],
        summed[3],
        summed[4],
        summed[5],
        summed[6],
        summed[7],
        summed[8],
    )


MESH = pl.DeviceIdType.MESH
F32, BF16 = jnp.float32, jnp.bfloat16
LOG2E = 1.4426950408889634
SCORE_SCALE = HEAD_SIZE**-0.5
VMEM_BYTES = 64 * 2**20 - 2**19
HALF = HEAD_SIZE // 2


def dot_nn(a, b):
    return lax.dot_general(a, b, (((1,), (0,)), ((), ())), preferred_element_type=F32)


def dot_nt(a, b):
    return lax.dot_general(a, b, (((1,), (1,)), ((), ())), preferred_element_type=F32)


def dot_tn(a, b):
    return lax.dot_general(a, b, (((0,), (0,)), ((), ())), preferred_element_type=F32)


class Place:
    def __init__(self):
        self.b = lax.axis_index("blk")
        self.t = lax.axis_index("tp")
        self.core = self.b % 2
        self.chip = self.b // 2
        self.x = self.chip % 2
        self.y = self.b // 4
        self.mate = self.b + 1 - 2 * self.core
        self.inner = jnp.logical_or(self.t == 1, self.t == 2)
        self.outer = jnp.logical_not(self.inner)
        self.pair = self.t + 1 - 2 * (self.t % 2)
        self.across = 3 - self.t

    def slot(self, s):
        core = (self.core + s % 2) % 2
        x = (self.x + (s // 2) % 2) % 2
        y = (self.y + s // 4) % 2
        return (y * 2 + x) * 2 + core

    def chip_at(self, k):
        x = (self.x + (k + 1) % 2) % 2
        y = (self.y + 1 - k // 2) % 2
        return y * 2 + x


def remote(src, dst, ssem, rsem, b, t):
    return pltpu.make_async_remote_copy(
        src_ref=src, dst_ref=dst, send_sem=ssem, recv_sem=rsem, device_id=(b, t), device_id_type=MESH
    )


def enter(me, blk_steps):
    barrier = pltpu.get_barrier_semaphore()
    for s in blk_steps:
        pl.semaphore_signal(barrier, inc=1, device_id=(me.slot(s), me.t), device_id_type=MESH)
    for z in (me.pair, me.across):
        pl.semaphore_signal(barrier, inc=1, device_id=(me.b, z), device_id_type=MESH)
    pl.semaphore_wait(barrier, len(blk_steps) + 2)


class LineSum:
    def __init__(self, me, part, first, second, sems, rows):
        self.me, self.part, self.first, self.second, self.sems, self.rows = (
            me, part, first, second, sems, rows,
        )

    def at(self, ref, p):
        return ref.at[pl.ds(pl.multiple_of(p * self.rows, self.rows), self.rows), :]

    def copy(self, stage, p):
        me = self.me
        src = (self.part, self.part, self.first)[stage]
        dst = (self.first, self.second, self.first)[stage]
        target = (me.pair, me.across, me.pair)[stage]
        return remote(
            self.at(src, p), self.at(dst, p),
            self.sems.at[2 * stage, p], self.sems.at[2 * stage + 1, p], me.b, target,
        )

    def give(self, p):
        @pl.when(self.me.outer)
        def _():
            self.copy(0, p).start()

    def fold(self, p):
        @pl.when(self.me.inner)
        def _():
            self.copy(0, p).wait_recv()
            mine, got = self.at(self.part, p), self.at(self.first, p)
            mine[...] = (mine[...].astype(F32) + got[...].astype(F32)).astype(BF16)
            self.copy(1, p).start()

    def unfold(self, p):
        @pl.when(self.me.inner)
        def _():
            self.copy(1, p).wait_recv()
            mine, got, out = self.at(self.part, p), self.at(self.second, p), self.at(self.first, p)
            out[...] = (mine[...].astype(F32) + got[...].astype(F32)).astype(BF16)
            self.copy(2, p).start()

    def take(self, p):
        @pl.when(self.me.outer)
        def _():
            self.copy(2, p).wait_recv()

    def drain_outer(self, pieces):
        @pl.when(self.me.outer)
        def _():
            def one(p, carry):
                self.copy(0, p).wait_send()
                return carry

            lax.fori_loop(0, pieces, one, 0)

    def drain_inner(self, pieces):
        @pl.when(self.me.inner)
        def _():
            def one(p, carry):
                self.copy(1, p).wait_send()
                self.copy(2, p).wait_send()
                return carry

            lax.fori_loop(0, pieces, one, 0)

    def drain(self, pieces):
        self.drain_outer(pieces)
        self.drain_inner(pieces)


class LineGather:
    def __init__(self, me, view, ssem, rsem, last):
        self.me, self.view, self.ssem, self.rsem, self.last = me, view, ssem, rsem, last

    def copy(self, way, hop, p):
        t = self.me.t

        def sent():
            slot = t - (hop - 1) if way == 0 else t + (hop - 1)
            ref = self.view(slot, p)
            target = t + 1 if way == 0 else t - 1
            return remote(ref, ref, self.ssem.at[way, hop - 1, p], self.rsem.at[way, hop - 1, p], self.me.b, target)

        def got():
            slot = t - hop if way == 0 else t + hop
            ref = self.view(slot, p)
            target = t - 1 if way == 0 else t + 1
            return remote(ref, ref, self.ssem.at[way, hop - 1, p], self.rsem.at[way, hop - 1, p], self.me.b, target)

        return sent, got

    def sends(self, way, hop):
        t = self.me.t
        if way == 0:
            return jnp.logical_and(t - (hop - 1) >= 0, t + 1 <= self.last)
        return jnp.logical_and(t + (hop - 1) <= self.last, t >= 1)

    def gets(self, way, hop):
        t = self.me.t
        return t - hop >= 0 if way == 0 else t + hop <= self.last

    def send(self, hop, p):
        for way in (0, 1):

            @pl.when(self.sends(way, hop))
            def _(way=way):
                self.copy(way, hop, p)[0]().start()

    def step(self, hop, p, also=None):
        for way in (0, 1):

            @pl.when(self.gets(way, hop))
            def _(way=way):
                self.copy(way, hop, p)[1]().wait_recv()
                if also is not None:
                    also(way, hop).start()

        if hop < self.last:
            self.send(hop + 1, p)

    def drain(self, p):
        for hop in range(1, self.last + 1):
            for way in (0, 1):

                @pl.when(self.sends(way, hop))
                def _(way=way, hop=hop):
                    self.copy(way, hop, p)[0]().wait_send()


class BlockSum:
    def __init__(self, me, make, outs, held, mates, chips, sems, spare):
        self.me, self.make, self.outs, self.spare = me, make, outs, spare
        self.held, self.mates, self.chips, self.sems = held, mates, chips, sems

    def to_mate(self, k):
        me = self.me
        return remote(
            self.held(k % 2), self.mates(k), self.sems.at[0, k], self.sems.at[1, k], me.mate, me.t
        )

    def to_chip(self, k):
        me = self.me
        return remote(
            self.mates(k), self.chips(k), self.sems.at[2, k], self.sems.at[3, k],
            me.chip_at(k) * 2 + me.core, me.t,
        )

    def lend(self, k):
        me = self.me
        if k >= 2:
            self.to_mate(k - 2).wait_send()
        held = self.held(k % 2)
        even = me.core == 0
        for (lo, hi, value), out, spare in zip(self.make(me.chip_at(k)), self.outs, self.spare):
            half = value.shape[0] // 2
            low, high = value[:half], value[half:]
            held[:, lo:hi] = jnp.where(even, high, low).astype(BF16)
            if k % 2 == 0:
                spare[...] = jnp.where(even, low, high).astype(BF16)
            else:
                out[...] = jnp.where(even, low, high)
        self.to_mate(k).start()

    def merge(self, k, spans):
        self.to_mate(k).wait_recv()
        mates = self.mates(k)
        for (lo, hi), out, spare in zip(spans, self.outs, self.spare):
            own = spare[...].astype(F32) if k % 2 == 0 else out[...]
            total = own + mates[:, lo:hi].astype(F32)
            if k < 3:
                mates[:, lo:hi] = total.astype(BF16)
            else:
                out[...] = total
        if k < 3:
            self.to_chip(k).start()

    def finish(self, spans):
        for k in range(3):
            self.to_chip(k).wait_recv()
            chips = self.chips(k)
            for (lo, hi), out in zip(spans, self.outs):
                out[...] += chips[:, lo:hi].astype(F32)

    def drain(self):
        for k in (2, 3):
            self.to_mate(k).wait_send()
        for k in range(3):
            self.to_chip(k).wait_send()


def norm_rows(values):
    inverse = lax.rsqrt(jnp.mean(values * values, axis=-1, keepdims=True) + norm_eps)
    return values * inverse, inverse


def turn(values, cs_ref, sign):
    cosine, sine = cs_ref[0:HALF, :], cs_ref[HALF:HEAD_SIZE, :] * sign
    pieces = []
    for h in range(values.shape[0] // HEAD_SIZE):
        low = values[h * HEAD_SIZE : h * HEAD_SIZE + HALF]
        high = values[h * HEAD_SIZE + HALF : (h + 1) * HEAD_SIZE]
        pieces.append(low * cosine - high * sine)
        pieces.append(high * cosine + low * sine)
    return jnp.concatenate(pieces, axis=0)


def fill_bias(bias, st_ref, key_start, query_start):
    key_place = lax.broadcasted_iota(jnp.int32, bias.shape, 0) + key_start
    query_place = lax.broadcasted_iota(jnp.int32, bias.shape, 1) + query_start
    allowed = jnp.logical_and(key_place >= st_ref[0:1, :], key_place <= query_place)
    bias[...] = jnp.where(allowed, 0.0, neg_fill)


def heads_of(h, group):
    g = h // group
    return slice(h * HEAD_SIZE, (h + 1) * HEAD_SIZE), slice(g * HEAD_SIZE, (g + 1) * HEAD_SIZE), g


def layer_kernel(
    dims,
    len_ref, ag_ref, mg_ref, hid_hbm, og_hbm, wq_hbm, wk_hbm, wv_hbm, wo_hbm, wg_hbm, wu_hbm, wd_hbm,
    lo_out, ig_out, gq_ref, gk_ref, gv_ref, go_ref, gg_ref, gu_ref, gd_ref, gag_ref, gmg_ref,
    hid, og, wq, wkv, wo, wg, wu, wd, kv, norm, attn, qt, ot, bias, mid, act, dg, du,
    p2, a2, b2, p3, a3, b3, dbr, dot_ref, dq, acc, low_t, dqr, dkvr,
    kv_mates, kv_chips, held_a, held_b, chips_b, held_c, mates_c, chips_c, total_c,
    turns, starts, m_ref, l_ref, lse, delta, gain, gain_in,
    load_sem, kv_sem, wo_sem, wo_plane_sem, wo_mate_sem, at_sem, sem2, sem3, sem4, kvs_sem, rs_sem, gain_sem, out_sem,
    mate_ready, chip_ready,
):
    rows, piece, chunk, share = dims["rows"], dims["piece"], dims["chunk"], dims["share"]
    q_heads, group, kv_width, n_docs = dims["q_heads"], dims["group"], dims["kv_width"], dims["n_docs"]
    n_pieces, n_chunks = rows // piece, rows // chunk
    per = chunk // piece
    width, hidden_units = wg.shape
    q_width = q_heads * HEAD_SIZE
    last = wo.shape[0] - 1
    me = Place()
    scale2 = SCORE_SCALE * LOG2E

    def each(f, lo, hi):
        def one(p, carry):
            f(p)
            return carry

        lax.fori_loop(lo, hi, one, 0)

    barrier = pltpu.get_barrier_semaphore()
    for s in range(1, 8):
        pl.semaphore_signal(barrier, inc=1, device_id=(me.slot(s), me.t), device_id_type=MESH)
    for z in (me.pair, me.across):
        pl.semaphore_signal(barrier, inc=1, device_id=(me.b, z), device_id_type=MESH)
    loads = {}
    for i, (name, source, target) in enumerate((
        ("wo", wo_hbm, wo.at[me.t]), ("hid", hid_hbm, hid), ("wk", wk_hbm, wkv.at[0:kv_width]),
        ("wv", wv_hbm, wkv.at[kv_width : 2 * kv_width]), ("wq", wq_hbm, wq), ("wg", wg_hbm, wg),
        ("wu", wu_hbm, wu), ("og", og_hbm, og), ("wd", wd_hbm, wd),
    )):
        loads[name] = pltpu.make_async_copy(source, target, load_sem.at[i])
    for name in ("wo", "hid", "wk", "wv"):
        loads[name].start()

    attn_gain, mlp_gain = ag_ref[...].reshape(1, width), mg_ref[...].reshape(1, width)

    def chunk_rows(c):
        return pl.ds(pl.multiple_of(c * chunk, chunk), chunk)

    def first_norm(c):
        r = chunk_rows(c)
        normed, _ = norm_rows(hid[r, :].astype(F32))
        norm[r, :] = (normed * attn_gain).astype(BF16)

    part = share // 4
    my_half = pl.ds(pl.multiple_of(me.core * share, share), share)

    def wo_rows(slot, p):
        first = me.core * share + p * 2 * part + (me.x, me.y)[p] * part
        return wo.at[slot, pl.ds(pl.multiple_of(first, part), part), :]

    whole_wo = LineGather(me, wo_rows, wo_sem.at[0], wo_sem.at[1], last)

    def wo_plane(way, hop, p):
        ref = wo_rows(me.t - hop if way == 0 else me.t + hop, p)
        return remote(
            ref, ref, wo_plane_sem.at[0, p, way, hop - 1], wo_plane_sem.at[1, p, way, hop - 1],
            me.slot(2 + 2 * p), me.t,
        )

    def wo_to_mate(way, hop):
        ref = wo.at[me.t - hop if way == 0 else me.t + hop, my_half, :]
        return remote(
            ref, ref, wo_mate_sem.at[0, way, hop - 1], wo_mate_sem.at[1, way, hop - 1], me.mate, me.t
        )

    def each_wo(hops, action):
        for hop in hops:
            for way in (0, 1):

                @pl.when(whole_wo.gets(way, hop))
                def _(way=way, hop=hop):
                    action(way, hop)

    def wo_spread(way, hop):
        for p in (0, 1):
            wo_plane(way, hop, p).start()

    def wo_lend(way, hop):
        for p in (0, 1):
            wo_plane(way, hop, p).wait_recv()
        wo_to_mate(way, hop).start()

    def wo_line(hop):
        for p in (0, 1):
            whole_wo.step(hop, p)

    loads["wo"].wait()
    pl.semaphore_wait(barrier, 9)
    for p in (0, 1):
        whole_wo.send(1, p)
    loads["wq"].start()
    places = me.b * rows + lax.broadcasted_iota(jnp.int32, (1, rows), 1)
    start, end = jnp.zeros((1, rows), jnp.int32), jnp.int32(0)
    for k in range(n_docs):
        end = end + len_ref[k]
        start = jnp.where(places >= end, end, start)
    starts[...] = jnp.broadcast_to(start, starts.shape)
    order = lax.broadcasted_iota(jnp.int32, (HALF, 1), 0).astype(F32)
    freqs = jnp.exp(order * (-2.0 / HEAD_SIZE * math.log(rope_base)))
    angle = freqs * (places - start).astype(F32)
    turns[0:HALF, :] = jnp.cos(angle)
    turns[HALF:HEAD_SIZE, :] = jnp.sin(angle)
    loads["hid"].wait()
    each(first_norm, 0, n_chunks)
    loads["wk"].wait()
    loads["wv"].wait()
    both_t = dot_nt(wkv[...], norm[...])
    kv[me.b, 0:kv_width, :] = turn(both_t[0:kv_width], turns, 1.0).astype(BF16)
    kv[me.b, kv_width : 2 * kv_width, :] = both_t[kv_width : 2 * kv_width].astype(BF16)

    def kv_copy(slot, target, n):
        return remote(kv.at[slot], kv.at[slot], kv_sem.at[0, n], kv_sem.at[1, n], target, me.t)

    def share_kv(s):
        @pl.when(me.slot(s) > me.b)
        def _():
            kv_copy(me.b, me.slot(s), s).start()

    for s in (1, 2, 4):
        share_kv(s)
    for name in ("wg", "wu", "og", "wd"):
        loads[name].start()
    loads["wq"].wait()
    qt[...] = turn(dot_nn(norm[...], wq[...]).T, turns, 1.0).astype(BF16)
    m_ref[...] = jnp.full(m_ref.shape, neg_fill, F32)
    l_ref[...] = jnp.zeros(l_ref.shape, F32)
    ot[...] = jnp.zeros(ot.shape, F32)

    def attend(s, carry):
        slot = me.slot(s)
        arrives = jnp.logical_and(s > 0, slot < me.b)

        @pl.when(arrives)
        def _():
            kv_copy(slot, me.mate, s).wait_recv()

        @pl.when(jnp.logical_and(arrives, s % 2 == 0))
        def _():
            kv_copy(slot, me.mate, s + 1).start()

        for hop, turn_at in ((1, 2), (2, 3), (3, 5)):

            @pl.when(s == turn_at)
            def _(hop=hop):
                wo_line(hop)

        @pl.when(s == 6)
        def _():
            each_wo((1, 2, 3), wo_spread)

        @pl.when(slot <= me.b)
        def _():
            fill_bias(bias, starts, slot * rows, me.b * rows)
            for h in range(q_heads):
                qs, ks, g = heads_of(h, group)
                vs = slice(kv_width + g * HEAD_SIZE, kv_width + (g + 1) * HEAD_SIZE)
                scores = dot_tn(kv[slot, ks, :], qt[qs, :]) + bias[...]
                old = m_ref[h : h + 1, :]
                new = jnp.maximum(old, jnp.max(scores, axis=0, keepdims=True))
                probs = jnp.exp2((scores - new) * scale2)
                keep = jnp.exp2((old - new) * scale2)
                m_ref[h : h + 1, :] = new
                l_ref[h : h + 1, :] = l_ref[h : h + 1, :] * keep + jnp.sum(probs, axis=0, keepdims=True)
                ot[qs, :] = ot[qs, :] * keep + dot_nn(kv[slot, vs, :], probs.astype(BF16))

        @pl.when(s == 1)
        def _():
            share_kv(6)

        return carry

    lax.fori_loop(0, 8, attend, 0)

    line_attn = LineGather(
        me, lambda slot, p: attn.at[slot, chunk_rows(p), :], at_sem.at[0], at_sem.at[1], last
    )
    for h in range(q_heads):
        qs, _, _ = heads_of(h, group)
        ot[qs, :] = ot[qs, :] / l_ref[h : h + 1, :]
    for c in range(n_chunks):
        attn[me.t, c * chunk : (c + 1) * chunk, :] = ot[:, c * chunk : (c + 1) * chunk].T.astype(BF16)
        if c < 2:
            line_attn.send(1, c)
    lse[...] = jnp.zeros(lse.shape, F32)
    lse[0:q_heads, :] = m_ref[0:q_heads, :] * scale2 + jnp.log2(l_ref[0:q_heads, :])
    for name in ("wg", "wu", "og", "wd"):
        loads[name].wait()
    line_attn.step(1, 0)
    line_attn.step(2, 0)
    each_wo((1, 2, 3), wo_lend)
    line_attn.step(3, 0)
    line_attn.step(1, 1)
    each_wo((1, 2, 3), lambda way, hop: wo_to_mate(way, hop).wait_recv())

    back = LineSum(me, p2, a2, b2, sem2, piece)
    forth_rows = rows // 8
    forth = LineSum(me, p3, a3, b3, sem3, forth_rows)
    forth_pieces = 8
    adds_middle = (me.t == 1).astype(F32)

    def feed(c, carry):
        r = chunk_rows(c)

        @pl.when(c < n_chunks - 2)
        def _():
            line_attn.send(1, c + 2)

        for n in range(0, width, 512):
            ns = slice(n, n + 512)
            total = hid[r, ns].astype(F32)
            for z in range(last + 1):
                total = total + dot_nn(attn[z, r, :], wo[z, :, ns])
            mid[r, ns] = total
        normed, _ = norm_rows(mid[r, :])
        norm[r, :] = (normed * mlp_gain).astype(BF16)

        @pl.when(c < n_chunks - 1)
        def _():
            line_attn.step(2, c + 1)

        for n in range(0, hidden_units, 512):
            ns = slice(n, n + 512)
            gate = dot_nn(norm[r, :], wg[:, ns])
            up = dot_nn(norm[r, :], wu[:, ns])
            grad = dot_nt(og[r, :], wd[ns, :])
            sig = 1.0 / (1.0 + jnp.exp(-gate))
            silu = gate * sig
            act[r, ns] = (silu * up).astype(BF16)
            dg[r, ns] = (grad * up * sig * (1.0 + gate * (1.0 - sig))).astype(BF16)
            du[r, ns] = (grad * silu).astype(BF16)
            if n == 0:

                @pl.when(c < n_chunks - 2)
                def _():
                    line_attn.step(1, c + 2)

        for n in range(0, width, 512):
            ns = slice(n, n + 512)
            p2[r, ns] = (dot_nt(dg[r, :], wg[ns, :]) + dot_nt(du[r, :], wu[ns, :])).astype(BF16)
        each(back.give, c * per, (c + 1) * per)

        @pl.when(c < n_chunks - 1)
        def _():
            line_attn.step(3, c + 1)

        @pl.when(c >= 2)
        def _():
            each(back.fold, (c - 2) * per, (c - 1) * per)

        @pl.when(c >= 3)
        def _():
            each(back.unfold, (c - 3) * per, (c - 2) * per)

        for n in range(0, width, 512):
            ns = slice(n, n + 512)
            p3[r, ns] = (dot_nn(act[r, :], wd[:, ns]) + mid[r, ns] * adds_middle).astype(BF16)
        return carry

    lax.fori_loop(0, n_chunks, feed, 0)
    pl.semaphore_signal(mate_ready, inc=1, device_id=(me.mate, me.t), device_id_type=MESH)
    for k in range(3):
        pl.semaphore_signal(
            chip_ready, inc=1, device_id=(me.chip_at(k) * 2 + me.core, me.t), device_id_type=MESH
        )
    pair = 2 * share

    def pair_columns(ref, chip):
        return ref[:, pl.ds(pl.multiple_of(chip * pair, pair), pair)]

    def slots(ref, first, columns):
        return lambda k: ref.at[(first + k) * share : (first + k + 1) * share, 0:columns]

    sum_gate = BlockSum(
        me, lambda m: [(0, hidden_units, dot_tn(pair_columns(norm, m), dg[...]))], [gg_ref],
        lambda k: held_a.at[0, k], slots(wg, 0, hidden_units), slots(wg, 4, hidden_units), rs_sem.at[0],
        [slots(wg, 7, hidden_units)(0)],
    )
    sum_up = BlockSum(
        me, lambda m: [(0, hidden_units, dot_tn(pair_columns(norm, m), du[...]))], [gu_ref],
        lambda k: held_a.at[1, k], slots(wu, 0, hidden_units), slots(wu, 4, hidden_units), rs_sem.at[1],
        [slots(wu, 7, hidden_units)(0)],
    )
    span_a = [(0, hidden_units)]
    pl.semaphore_wait(mate_ready, 1)
    gain[...] = jnp.zeros(gain.shape, F32)

    def middle_grad(c):
        each(back.take, c * per, (c + 1) * per)
        r = chunk_rows(c)
        normed, inverse = norm_rows(mid[r, :])
        grad = a2[r, :].astype(F32)
        scaled = grad * mlp_gain
        gain[1:2, :] += jnp.sum(grad * normed, axis=0, keepdims=True)
        found = og[r, :].astype(F32) + inverse * (
            scaled - normed * jnp.mean(scaled * normed, axis=-1, keepdims=True)
        )
        mid[r, :] = found
        dbr[r, :] = found.astype(BF16)

    def fold_on(lo, hi):
        def one(p, carry):
            back.fold(p)
            back.unfold(p - per)
            return carry

        lax.fori_loop(lo, hi, one, 0)

    def lend_both(k):
        sum_gate.lend(k)
        sum_up.lend(k)

    def merge_both(k):
        sum_gate.merge(k, span_a)
        sum_up.merge(k, span_a)

    lend_both(0)
    fold_on((n_chunks - 2) * per, (n_chunks - 2) * per + per // 2)
    lend_both(1)
    back.drain_outer(n_pieces)
    each(forth.give, 0, forth_pieces)
    fold_on((n_chunks - 2) * per + per // 2, (n_chunks - 1) * per)
    pl.semaphore_wait(chip_ready, 3)
    merge_both(0)
    fold_on((n_chunks - 1) * per, n_pieces - per // 2)
    lend_both(2)
    merge_both(1)
    fold_on(n_pieces - per // 2, n_pieces)
    merge_both(2)
    each(back.unfold, n_pieces - per, n_pieces)
    each(middle_grad, 0, n_chunks - 1)
    each(middle_grad, n_chunks - 1, n_chunks)
    dot_ref[...] = dot_nt(wo[me.t], dbr[...]).astype(BF16)
    delta[...] = jnp.zeros(delta.shape, F32)
    for h in range(q_heads):
        qs, _, _ = heads_of(h, group)
        delta[h : h + 1, :] = jnp.sum(dot_ref[qs, :].astype(F32) * ot[qs, :], axis=0, keepdims=True)
    dq[...] = jnp.zeros(dq.shape, F32)
    back.drain_inner(n_pieces)
    ahead = 3
    each(forth.fold, 0, ahead)

    for s in (1, 2, 4, 6):

        @pl.when(me.slot(s) > me.b)
        def _(s=s):
            kv_copy(me.b, me.slot(s), s).wait_send()

    for s in (2, 4, 6):

        @pl.when(me.slot(s) < me.b)
        def _(s=s):
            kv_copy(me.slot(s), me.mate, s + 1).wait_send()

    def kv_to_mate(k):
        return remote(
            kv.at[me.chip_at(k) * 2 + 1 - me.core], kv_mates.at[k], kvs_sem.at[0, k], kvs_sem.at[1, k],
            me.mate, me.t,
        )

    def kv_to_chip(k):
        return remote(
            kv_mates.at[k], kv_chips.at[k], kvs_sem.at[2, k], kvs_sem.at[3, k],
            me.chip_at(k) * 2 + me.core, me.t,
        )

    def attend_back(u, carry):
        k, own = u // 2, u % 2
        chip = me.chip_at(k)
        slot = chip * 2 + (me.core + 1 - own) % 2

        @pl.when(u + ahead < forth_pieces)
        def _():
            forth.fold(u + ahead)

        @pl.when(u >= 2)
        def _():
            forth.unfold(u - 2)

        @pl.when(slot <= me.b)
        def _():
            fill_bias(bias, starts, slot * rows, me.b * rows)
            for g in range(q_heads // group):
                ks = slice(g * HEAD_SIZE, (g + 1) * HEAD_SIZE)
                vs = slice(kv_width + g * HEAD_SIZE, kv_width + (g + 1) * HEAD_SIZE)
                key_t, value_t = kv[slot, ks, :], kv[slot, vs, :]
                grad_k = grad_v = None
                for h in range(g * group, (g + 1) * group):
                    qs, _, _ = heads_of(h, group)
                    query_t, grad_t = qt[qs, :], dot_ref[qs, :]
                    scores = dot_tn(key_t, query_t) + bias[...]
                    probs = jnp.exp2(scores * scale2 - lse[h : h + 1, :])
                    grad_p = dot_tn(value_t, grad_t)
                    grad_s = (probs * (grad_p - delta[h : h + 1, :])).astype(BF16)
                    one_v = dot_nt(grad_t, probs.astype(BF16))
                    one_k = dot_nt(query_t, grad_s)
                    grad_v = one_v if grad_v is None else grad_v + one_v
                    grad_k = one_k if grad_k is None else grad_k + one_k
                    dq[qs, :] += dot_nn(key_t, grad_s)
                acc[ks, :] = grad_k
                acc[vs, :] = grad_v

        @pl.when(jnp.logical_and(own == 0, slot <= me.b))
        def _():
            kv[slot] = acc[...].astype(BF16)
            kv_to_mate(k).start()

        @pl.when(jnp.logical_and(own == 1, chip < me.chip))
        def _():
            kv_to_mate(k).wait_recv()
            kv_mates[k] = (acc[...] + kv_mates[k].astype(F32)).astype(BF16)
            kv_to_chip(k).start()

        return carry

    lax.fori_loop(0, 8, attend_back, 0)
    low_t[0:q_width, :] = turn(dq[...] * SCORE_SCALE, turns, -1.0).astype(BF16)
    dqr[...] = low_t[0:q_width, :].T

    def first_norm_again(c):
        r = chunk_rows(c)
        normed, _ = norm_rows(hid[r, :].astype(F32))
        norm[r, :] = (normed * attn_gain).astype(BF16)


    @pl.when(me.core == 0)
    def _():
        kv_to_mate(3).wait_recv()
        acc[...] += kv_mates[3].astype(F32)

    for k in range(3):

        @pl.when(me.chip_at(k) > me.chip)
        def _(k=k):
            kv_to_chip(k).wait_recv()
            acc[...] += kv_chips[k].astype(F32)

    low_t[q_width : q_width + kv_width, :] = turn(acc[0:kv_width, :] * SCORE_SCALE, turns, -1.0).astype(BF16)
    low_t[q_width + kv_width :, :] = acc[kv_width : 2 * kv_width, :].astype(BF16)
    dkvr[...] = low_t[q_width:, :].T

    each(forth.take, 0, 2)
    end_sum = LineSum(me, p2, a2, b2, sem4, piece)

    def input_part(c):
        r = chunk_rows(c)
        for n in range(0, width, 512):
            ns = slice(n, n + 512)
            p2[r, ns] = (dot_nt(dqr[r, :], wq[ns, :]) + dot_nn(dkvr[r, :], wkv[:, ns])).astype(BF16)
        each(end_sum.give, c * per, (c + 1) * per)

    each(input_part, 0, n_chunks)
    each(forth.unfold, forth_pieces - 2, forth_pieces)

    def make_b(m):
        yield 0, hidden_units, dot_tn(pair_columns(og, m), act[...])
        yield hidden_units, hidden_units + q_width, dot_tn(pair_columns(dbr, m), attn[me.t])

    def make_c(m):
        columns = pair_columns(norm, m)
        yield 0, q_width, dot_tn(columns, dqr[...])
        yield q_width, q_width + 2 * kv_width, dot_tn(columns, dkvr[...])

    width_b = hidden_units + q_width
    in_wd = slots(wd, 0, width_b)
    sum_b = BlockSum(
        me, make_b, [gd_ref, go_ref], lambda k: held_b.at[k], in_wd,
        lambda k: in_wd(4) if k == 0 else chips_b.at[k - 1], rs_sem.at[2],
        [dg.at[0:share, :], du.at[0:share, 0:q_width]],
    )
    span_b = [(0, hidden_units), (hidden_units, width_b)]
    total_parts = [total_c.at[:, 0:q_width], total_c.at[:, q_width : q_width + 2 * kv_width]]
    sum_c = BlockSum(
        me, make_c, total_parts, lambda k: held_c.at[k], lambda k: mates_c.at[k], lambda k: chips_c.at[k],
        rs_sem.at[3],
        [dg.at[share : 2 * share, 0:q_width], du.at[share : 2 * share, 0 : 2 * kv_width]],
    )
    span_c = [(0, q_width), (q_width, q_width + 2 * kv_width)]
    work = [(functools.partial(lend_both, 3), functools.partial(merge_both, 3))]
    for sums, spans in ((sum_b, span_b), (sum_c, span_c)):
        for k in range(4):
            work.append((functools.partial(sums.lend, k), functools.partial(sums.merge, k, spans)))
    done, late = 0, None
    for i, (lend, merge) in enumerate(work):
        if i == 1:
            each(first_norm_again, 0, n_chunks)
        lend()
        upto = n_pieces * (i + 1) // len(work)
        for p in range(done, upto):
            end_sum.fold(p)
            if p >= 1:
                end_sum.unfold(p - 1)
        done = upto
        if late is not None:
            late()
        late = merge
    end_sum.unfold(n_pieces - 1)
    late()

    each(forth.take, 2, forth_pieces)
    lo_save = pltpu.make_async_copy(a3, lo_out, out_sem.at[0])
    lo_save.start()

    def input_rows(c):
        each(end_sum.take, c * per, (c + 1) * per)
        r = chunk_rows(c)
        normed, inverse = norm_rows(hid[r, :].astype(F32))
        grad = a2[r, :].astype(F32)
        scaled = grad * attn_gain
        gain[0:1, :] += jnp.sum(grad * normed, axis=0, keepdims=True)
        found = inverse * (scaled - normed * jnp.mean(scaled * normed, axis=-1, keepdims=True))
        dbr[r, :] = (mid[r, :] + found).astype(BF16)

    each(input_rows, 0, n_chunks)

    def gain_copy(s):
        return remote(gain, gain_in.at[s], gain_sem.at[0, s], gain_sem.at[1, s], me.slot(s), me.t)

    for s in range(1, 8):
        gain_copy(s).start()
    ig_save = pltpu.make_async_copy(dbr, ig_out, out_sem.at[1])
    ig_save.start()
    sum_gate.finish(span_a)
    sum_up.finish(span_a)
    sum_b.finish(span_b)
    sum_c.finish(span_c)
    gq_ref[...] = total_c[:, 0:q_width]
    gk_ref[...] = total_c[:, q_width : q_width + kv_width]
    gv_ref[...] = total_c[:, q_width + kv_width : q_width + 2 * kv_width]
    for s in range(1, 8):
        gain_copy(s).wait_recv()
    gains = gain[...]
    for s in range(1, 8):
        gains = gains + gain_in[s]
    gain_in[0] = gains
    mine = jnp.zeros((8, share), F32)
    for j in range(8):
        mine = mine + jnp.where(me.b == j, gain_in[0, :, j * share : (j + 1) * share], 0.0)
    gag_ref[...] = mine[0, :]
    gmg_ref[...] = mine[1, :]

    for s in range(1, 8):
        gain_copy(s).wait_send()
    for p in (0, 1):
        whole_wo.drain(p)

    def wo_done(way, hop):
        for p in (0, 1):
            wo_plane(way, hop, p).wait_send()
        wo_to_mate(way, hop).wait_send()

    each_wo((1, 2, 3), wo_done)
    each(line_attn.drain, 0, n_chunks)
    forth.drain(forth_pieces)
    end_sum.drain(n_pieces)
    for sums in (sum_gate, sum_up, sum_b, sum_c):
        sums.drain()
    for k in range(4):
        chip = me.chip_at(k)
        slot = chip * 2 + 1 - me.core

        @pl.when(slot <= me.b)
        def _(k=k):
            kv_to_mate(k).wait_send()

        if k < 3:

            @pl.when(chip < me.chip)
            def _(k=k):
                kv_to_chip(k).wait_send()

    lo_save.wait()
    ig_save.wait()


def hand_over(n, *refs):
    sources, targets, held, sems = refs[:n], refs[n : 2 * n], refs[2 * n : 3 * n], refs[3 * n]
    ins = [pltpu.make_async_copy(a, h, sems.at[0, i]) for i, (a, h) in enumerate(zip(sources, held))]
    outs = [pltpu.make_async_copy(h, b, sems.at[1, i]) for i, (h, b) in enumerate(zip(held, targets))]
    for copy in ins:
        copy.start()
    for first, second in zip(ins, outs):
        first.wait()
        second.start()
    for copy in outs:
        copy.wait()


def kernel_shards(
    hidden_in, out_grad, lengths, attn_gain, w_query, key_projection_weight, value_projection_weight,
    w_out, mlp_gain, w_gate, w_up, w_down,
):
    rows, width = hidden_in.shape
    q_width, kv_width = w_query.shape[1], key_projection_weight.shape[1]
    hidden_units = w_gate.shape[1]
    blocks, line_size = lax.axis_size("blk"), lax.axis_size("tp")
    share = width // blocks
    piece, chunk = rows // 16, rows // 4
    pieces, chunks = rows // piece, rows // chunk
    dims = dict(
        rows=rows, piece=piece, chunk=chunk, share=share, q_heads=q_width // HEAD_SIZE,
        group=q_width // kv_width, kv_width=kv_width, n_docs=lengths.shape[0],
    )
    vmem, hbm = pl.BlockSpec(memory_space=pltpu.VMEM), pl.BlockSpec(memory_space=pl.ANY)
    smem = pl.BlockSpec(memory_space=pltpu.SMEM)
    dma, regular = pltpu.SemaphoreType.DMA, pltpu.SemaphoreType.REGULAR

    def shape(dtype, *dims_):
        return jax.ShapeDtypeStruct(dims_, dtype)

    def low(*dims_):
        return pltpu.VMEM(dims_, BF16)

    def full(*dims_):
        return pltpu.VMEM(dims_, F32)

    line = [low(rows, width)] * 3
    width_b, width_c = hidden_units + q_width, q_width + 2 * kv_width
    shapes = (
        shape(BF16, rows, width), shape(BF16, rows, width), shape(F32, share, q_width),
        shape(F32, share, kv_width), shape(F32, share, kv_width), shape(F32, share, q_width),
        shape(F32, share, hidden_units), shape(F32, share, hidden_units), shape(F32, share, hidden_units),
        shape(F32, share), shape(F32, share),
    )
    outs = pl.pallas_call(
        functools.partial(layer_kernel, dims),
        out_shape=shapes,
        in_specs=[smem, vmem, vmem] + [hbm] * 9,
        out_specs=(hbm, hbm) + (vmem,) * 9,
        scratch_shapes=[
            low(rows, width), low(rows, width), low(width, q_width), low(2 * kv_width, width),
            low(line_size, q_width, width), low(width, hidden_units), low(width, hidden_units),
            low(hidden_units, width), low(blocks, 2 * kv_width, rows), low(rows, width),
            low(line_size, rows, q_width), low(q_width, rows), full(q_width, rows), full(rows, rows),
            full(rows, width), low(rows, hidden_units), low(rows, hidden_units), low(rows, hidden_units),
            *line, *line, low(rows, width), low(q_width, rows), full(q_width, rows), full(2 * kv_width, rows),
            low(width_c, rows), low(rows, q_width), low(rows, 2 * kv_width),
            low(4, 2 * kv_width, rows), low(3, 2 * kv_width, rows),
            low(2, 2, share, hidden_units), low(2, share, width_b), low(2, share, width_b),
            low(2, share, width_c), low(4, share, width_c), low(3, share, width_c), full(share, width_c),
            full(HEAD_SIZE, rows), pltpu.VMEM((8, rows), jnp.int32), full(8, rows), full(8, rows), full(8, rows),
            full(8, rows), full(8, width), full(8, 8, width),
            dma((9,)), dma((2, 8)), dma((2, 2, line_size - 1, 2)), dma((2, 2, 2, line_size - 1)),
            dma((2, 2, line_size - 1)),
            dma((2, 2, line_size - 1, chunks)), dma((6, pieces)), dma((6, pieces)), dma((6, pieces)),
            dma((4, 4)), dma((4, 4, 4)), dma((2, 8)), dma((2,)), regular, regular,
        ],
        compiler_params=pltpu.CompilerParams(
            collective_id=0, has_side_effects=True, vmem_limit_bytes=VMEM_BYTES
        ),
    )(
        lengths, attn_gain, mlp_gain, hidden_in, out_grad, w_query, key_projection_weight.T,
        value_projection_weight.T, w_out, w_gate, w_up, w_down,
    )
    outs = pl.pallas_call(
        functools.partial(hand_over, len(shapes)),
        out_shape=shapes,
        in_specs=[hbm] * len(shapes),
        out_specs=(hbm,) * len(shapes),
        scratch_shapes=[pltpu.VMEM(s.shape, s.dtype) for s in shapes] + [dma((2, len(shapes)))],
    )(*outs)
    layer_out, input_grad, grad_query, grad_key, grad_value, grad_out, grad_gate, grad_up, grad_down, g1, g2 = outs
    return (
        layer_out, input_grad, grad_query, grad_key, grad_value, grad_out.T, grad_gate, grad_up, grad_down.T, g1, g2,
    )


def solution(mesh):
    sizes = dict(mesh.shape)
    small = sizes["blk"] == 8 and sizes["tp"] == 4
    placed = (
        P("blk", None),
        P("blk", None),
        P(),
        P(),
        P(None, "tp"),
        P(None, "tp"),
        P(None, "tp"),
        P("tp", None),
        P(),
        P(None, "tp"),
        P(None, "tp"),
        P("tp", None),
    )
    return jax.shard_map(
        kernel_shards if small else shards,
        mesh=mesh,
        in_specs=placed,
        out_specs=(
            P("blk", None),
            P("blk", None),
            P("blk", "tp"),
            P("blk", "tp"),
            P("blk", "tp"),
            P("tp", "blk"),
            P("blk", "tp"),
            P("blk", "tp"),
            P("tp", "blk"),
            P("blk"),
            P("blk"),
        ),
        check_vma=False,
    )
```

```python
import functools
import math

import jax
import jax.numpy as jnp
from jax import lax
from jax.experimental import pallas as pl
from jax.experimental.pallas import tpu as pltpu
from jax.sharding import PartitionSpec as P

HEAD_SIZE = 96


norm_eps = 1e-05
rope_base = 100000.0
neg_fill = -1e30


def doc_places(lengths, places):
    doc_ends = jnp.cumsum(lengths)
    passed = (places[:, None] >= doc_ends[None, :]).astype(jnp.int32)
    segment = jnp.sum(passed, axis=1)
    preceding = jnp.sum(passed * lengths[None, :], axis=1)
    return (segment, places - preceding)


def apply_rotary(values, token_position, heads, sign_value):
    half_size = HEAD_SIZE // 2
    freqs = rope_base ** (-(2.0 * jnp.arange(half_size, dtype=jnp.float32)) / HEAD_SIZE)
    angle = token_position.astype(jnp.float32)[:, None] * freqs[None, :]
    cosine = jnp.cos(angle)[:, None, :]
    sine = sign_value * jnp.sin(angle)[:, None, :]
    shaped = values.reshape(values.shape[0], heads, HEAD_SIZE)
    first_half = shaped[..., :half_size]
    second_half = shaped[..., half_size:]
    turned = jnp.concatenate(
        [first_half * cosine - second_half * sine, second_half * cosine + first_half * sine],
        axis=-1,
    )
    return turned.reshape(values.shape[0], heads * HEAD_SIZE)


def rms_parts(values):
    inverse = lax.rsqrt(jnp.mean(values * values, axis=-1, keepdims=True) + norm_eps)
    return (values * inverse, inverse)


def norm_back(grad_in, normed, inverse, gain):
    scaled = grad_in * gain
    grad_values = inverse * (scaled - normed * jnp.mean(scaled * normed, axis=-1, keepdims=True))
    return (grad_values, jnp.sum(grad_in * normed, axis=0))


def left_product(left_side, right_side):
    return lax.dot_general(
        left_side, right_side, (((0,), (0,)), ((), ())), preferred_element_type=jnp.float32
    )


def right_product(left_side, weight):
    return lax.dot_general(
        left_side, weight, (((1,), (1,)), ((), ())), preferred_element_type=jnp.float32
    )


def score_block(query_four, key_rows, query_seg, query_place, key_seg, key_place):
    score_scale = HEAD_SIZE ** (-0.5)
    scores = (
        jnp.einsum("igrd,jgd->grij", query_four, key_rows, preferred_element_type=jnp.float32)
        * score_scale
    )
    allowed = (query_seg[:, None] == key_seg[None, :]) & (
        key_place[None, :] <= query_place[:, None]
    )
    return (jnp.where(allowed[None, None], scores, neg_fill), allowed)


def score_grads(
    query_four,
    grad_four,
    log_sum,
    delta,
    query_seg,
    query_place,
    key_rows,
    value_rows,
    key_seg,
    key_place,
):
    scores, allowed = score_block(query_four, key_rows, query_seg, query_place, key_seg, key_place)
    probs = jnp.where(allowed[None, None], jnp.exp(scores - log_sum[..., None]), 0.0)
    grad_probs = jnp.einsum(
        "igrd,jgd->grij", grad_four, value_rows, preferred_element_type=jnp.float32
    )
    grad_scores = (probs * (grad_probs - delta[..., None])).astype(jnp.bfloat16)
    return (grad_scores, probs.astype(jnp.bfloat16))


def keep_same(running):
    return running


def shards(
    hidden_in,
    out_grad,
    lengths,
    attn_gain,
    w_query,
    key_projection_weight,
    value_projection_weight,
    w_out,
    mlp_gain,
    w_gate,
    w_up,
    w_down,
):
    row_count = hidden_in.shape[0]
    cycle_size = lax.axis_size("blk")
    first_row = lax.axis_index("blk") * row_count
    offsets = jnp.arange(row_count, dtype=jnp.int32)
    places = first_row + offsets
    segment, token_position = doc_places(lengths, places)
    q_heads = w_query.shape[1] // HEAD_SIZE
    kv_heads = key_projection_weight.shape[1] // HEAD_SIZE
    query_group_size = q_heads // kv_heads
    kv_width = kv_heads * HEAD_SIZE
    score_scale = HEAD_SIZE ** (-0.5)
    hidden_f = hidden_in.astype(jnp.float32)
    normed_one, inverse_one = rms_parts(hidden_f)
    first_layer_norm = (normed_one * attn_gain).astype(jnp.bfloat16)
    query_raw = jnp.dot(first_layer_norm, w_query, preferred_element_type=jnp.float32)
    key_raw = jnp.dot(first_layer_norm, key_projection_weight, preferred_element_type=jnp.float32)
    value_raw = jnp.dot(
        first_layer_norm, value_projection_weight, preferred_element_type=jnp.float32
    )
    query_low = apply_rotary(query_raw, token_position, q_heads, 1.0).astype(jnp.bfloat16)
    key_low = apply_rotary(key_raw, token_position, kv_heads, 1.0).astype(jnp.bfloat16)
    value_low = value_raw.astype(jnp.bfloat16)
    kv_rows = jnp.concatenate([key_low, value_low], axis=1)
    query_four = query_low.reshape(row_count, kv_heads, query_group_size, HEAD_SIZE)

    def split_kv(piece, block_step):
        block_rows = lax.dynamic_slice_in_dim(piece, block_step * row_count, row_count, 0)
        key_rows = block_rows[:, :kv_width].reshape(row_count, kv_heads, HEAD_SIZE)
        value_rows = block_rows[:, kv_width:].reshape(row_count, kv_heads, HEAD_SIZE)
        return (key_rows, value_rows)

    start_max = jnp.full((kv_heads, query_group_size, row_count), neg_fill, jnp.float32)
    start_sum = jnp.zeros((kv_heads, query_group_size, row_count), jnp.float32)
    start_acc = jnp.zeros((kv_heads, query_group_size, row_count, HEAD_SIZE), jnp.float32)
    piece = lax.all_gather(kv_rows, "blk", axis=0, tiled=True)

    def forward_one_step(block_step, running):
        key_start = block_step * row_count

        def forward_work(running):
            row_max, row_sum, weighted = running
            key_rows, value_rows = split_kv(piece, block_step)
            key_place = key_start + offsets
            key_seg, _ = doc_places(lengths, key_place)
            scores, allowed = score_block(query_four, key_rows, segment, places, key_seg, key_place)
            new_max = jnp.maximum(row_max, jnp.max(scores, axis=-1))
            exp_scores = jnp.where(allowed[None, None], jnp.exp(scores - new_max[..., None]), 0.0)
            rescale = jnp.exp(row_max - new_max)
            row_sum = row_sum * rescale + jnp.sum(exp_scores, axis=-1)
            weighted = weighted * rescale[..., None] + jnp.einsum(
                "grij,jgd->grid",
                exp_scores.astype(jnp.bfloat16),
                value_rows,
                preferred_element_type=jnp.float32,
            )
            return (new_max, row_sum, weighted)

        return lax.cond(key_start <= first_row, forward_work, keep_same, running)

    row_max, row_sum, weighted = lax.fori_loop(
        0, piece.shape[0] // row_count, forward_one_step, (start_max, start_sum, start_acc)
    )
    attn_four = weighted / row_sum[..., None]
    log_sum = row_max + jnp.log(row_sum)
    attn_rows = jnp.transpose(attn_four, (2, 0, 1, 3)).reshape(row_count, q_heads * HEAD_SIZE)
    attn_low = attn_rows.astype(jnp.bfloat16)
    branch = lax.psum(jnp.dot(attn_low, w_out, preferred_element_type=jnp.float32), "tp")
    middle = hidden_f + branch
    normed_two, inverse_two = rms_parts(middle)
    ln_two = (normed_two * mlp_gain).astype(jnp.bfloat16)
    gate = jnp.dot(ln_two, w_gate, preferred_element_type=jnp.float32)
    up_proj = jnp.dot(ln_two, w_up, preferred_element_type=jnp.float32)
    sig_gate = jax.nn.sigmoid(gate)
    act_gate = gate * sig_gate
    hidden = (act_gate * up_proj).astype(jnp.bfloat16)
    mlp_branch = lax.psum(jnp.dot(hidden, w_down, preferred_element_type=jnp.float32), "tp")
    layer_out = (middle + mlp_branch).astype(jnp.bfloat16)
    grad_down = left_product(hidden, out_grad)
    grad_hidden = right_product(out_grad, w_down)
    grad_gate_act = (grad_hidden * up_proj * sig_gate * (1.0 + gate * (1.0 - sig_gate))).astype(
        jnp.bfloat16
    )
    grad_up_act = (grad_hidden * act_gate).astype(jnp.bfloat16)
    grad_gate = left_product(ln_two, grad_gate_act)
    grad_up = left_product(ln_two, grad_up_act)
    grad_ln_two = lax.psum(
        right_product(grad_gate_act, w_gate) + right_product(grad_up_act, w_up), "tp"
    )
    grad_middle_norm, grad_mlp_gain = norm_back(grad_ln_two, normed_two, inverse_two, mlp_gain)
    grad_middle = out_grad.astype(jnp.float32) + grad_middle_norm
    grad_branch = grad_middle.astype(jnp.bfloat16)
    grad_out = left_product(attn_low, grad_branch)
    grad_attn = right_product(grad_branch, w_out).astype(jnp.bfloat16)
    grad_four = grad_attn.reshape(row_count, kv_heads, query_group_size, HEAD_SIZE)
    delta = jnp.sum(jnp.transpose(grad_four.astype(jnp.float32), (1, 2, 0, 3)) * attn_four, axis=-1)

    def query_grads(grad_scores, key_rows):
        return (
            jnp.einsum("grij,jgd->grid", grad_scores, key_rows, preferred_element_type=jnp.float32)
            * score_scale
        )

    def key_value_grads(grad_scores, probs_low, query_rows, grad_rows):
        grad_keys = (
            jnp.einsum(
                "grij,igrd->jgd", grad_scores, query_rows, preferred_element_type=jnp.float32
            )
            * score_scale
        )
        grad_values = jnp.einsum(
            "grij,igrd->jgd", probs_low, grad_rows, preferred_element_type=jnp.float32
        )
        return jnp.concatenate(
            [grad_keys.reshape(row_count, kv_width), grad_values.reshape(row_count, kv_width)],
            axis=1,
        )

    start_dq = jnp.zeros((kv_heads, query_group_size, row_count, HEAD_SIZE), jnp.float32)
    start_kv = jnp.zeros((row_count * cycle_size, 2 * kv_width), jnp.float32)
    back_piece = lax.all_gather(kv_rows, "blk", axis=0, tiled=True)

    def back_one_step(block_step, running):
        key_start = block_step * row_count

        def back_work(running):
            grad_query_acc, grad_kv_acc = running
            key_rows, value_rows = split_kv(back_piece, block_step)
            key_place = key_start + offsets
            key_seg, _ = doc_places(lengths, key_place)
            grad_scores, probs_low = score_grads(
                query_four,
                grad_four,
                log_sum,
                delta,
                segment,
                places,
                key_rows,
                value_rows,
                key_seg,
                key_place,
            )
            grad_query_acc = grad_query_acc + query_grads(grad_scores, key_rows)
            earlier = lax.dynamic_slice_in_dim(grad_kv_acc, key_start, row_count, 0)
            added = earlier + key_value_grads(grad_scores, probs_low, query_four, grad_four)
            return (
                grad_query_acc,
                lax.dynamic_update_slice_in_dim(grad_kv_acc, added, key_start, 0),
            )

        return lax.cond(key_start <= first_row, back_work, keep_same, running)

    grad_query_four, grad_kv_all = lax.fori_loop(
        0, back_piece.shape[0] // row_count, back_one_step, (start_dq, start_kv)
    )
    grad_kv = lax.psum_scatter(grad_kv_all, "blk", scatter_dimension=0, tiled=True)
    grad_query_rows = jnp.transpose(grad_query_four, (2, 0, 1, 3)).reshape(
        row_count, q_heads * HEAD_SIZE
    )
    grad_query_low = apply_rotary(grad_query_rows, token_position, q_heads, -1.0).astype(
        jnp.bfloat16
    )
    grad_key_low = apply_rotary(grad_kv[:, :kv_width], token_position, kv_heads, -1.0).astype(
        jnp.bfloat16
    )
    grad_value_low = grad_kv[:, kv_width:].astype(jnp.bfloat16)
    grad_query = left_product(first_layer_norm, grad_query_low)
    grad_key = left_product(first_layer_norm, grad_key_low)
    grad_value = left_product(first_layer_norm, grad_value_low)
    grad_ln_part = (
        right_product(grad_query_low, w_query)
        + right_product(grad_key_low, key_projection_weight)
        + right_product(grad_value_low, value_projection_weight)
    )
    grad_ln_one = lax.psum(grad_ln_part, "tp")
    grad_input_norm, grad_attn_gain = norm_back(grad_ln_one, normed_one, inverse_one, attn_gain)
    input_grad = (grad_middle + grad_input_norm).astype(jnp.bfloat16)
    summed = (
        lax.psum_scatter(grad_query, "blk", scatter_dimension=0, tiled=True),
        lax.psum_scatter(grad_key, "blk", scatter_dimension=0, tiled=True),
        lax.psum_scatter(grad_value, "blk", scatter_dimension=0, tiled=True),
        lax.psum_scatter(grad_out, "blk", scatter_dimension=1, tiled=True),
        lax.psum_scatter(grad_gate, "blk", scatter_dimension=0, tiled=True),
        lax.psum_scatter(grad_up, "blk", scatter_dimension=0, tiled=True),
        lax.psum_scatter(grad_down, "blk", scatter_dimension=1, tiled=True),
        lax.psum_scatter(grad_attn_gain, "blk", scatter_dimension=0, tiled=True),
        lax.psum_scatter(grad_mlp_gain, "blk", scatter_dimension=0, tiled=True),
    )
    return (
        layer_out,
        input_grad,
        summed[0],
        summed[1],
        summed[2],
        summed[3],
        summed[4],
        summed[5],
        summed[6],
        summed[7],
        summed[8],
    )


MESH = pl.DeviceIdType.MESH
F32, BF16 = jnp.float32, jnp.bfloat16
LOG2E = 1.4426950408889634
SCORE_SCALE = HEAD_SIZE**-0.5
VMEM_BYTES = 64 * 2**20 - 2**19
HALF = HEAD_SIZE // 2


def dot_nn(a, b):
    return lax.dot_general(a, b, (((1,), (0,)), ((), ())), preferred_element_type=F32)


def dot_nt(a, b):
    return lax.dot_general(a, b, (((1,), (1,)), ((), ())), preferred_element_type=F32)


def dot_tn(a, b):
    return lax.dot_general(a, b, (((0,), (0,)), ((), ())), preferred_element_type=F32)


class Place:
    def __init__(self):
        self.b = lax.axis_index("blk")
        self.t = lax.axis_index("tp")
        self.core = self.b % 2
        self.chip = self.b // 2
        self.x = self.chip % 2
        self.y = self.b // 4
        self.mate = self.b + 1 - 2 * self.core
        self.inner = jnp.logical_or(self.t == 1, self.t == 2)
        self.outer = jnp.logical_not(self.inner)
        self.pair = self.t + 1 - 2 * (self.t % 2)
        self.across = 3 - self.t

    def slot(self, s):
        core = (self.core + s % 2) % 2
        x = (self.x + (s // 2) % 2) % 2
        y = (self.y + s // 4) % 2
        return (y * 2 + x) * 2 + core

    def chip_at(self, k):
        x = (self.x + (k + 1) % 2) % 2
        y = (self.y + 1 - k // 2) % 2
        return y * 2 + x


def remote(src, dst, ssem, rsem, b, t):
    return pltpu.make_async_remote_copy(
        src_ref=src, dst_ref=dst, send_sem=ssem, recv_sem=rsem, device_id=(b, t), device_id_type=MESH
    )


def enter(me, blk_steps):
    barrier = pltpu.get_barrier_semaphore()
    for s in blk_steps:
        pl.semaphore_signal(barrier, inc=1, device_id=(me.slot(s), me.t), device_id_type=MESH)
    for z in (me.pair, me.across):
        pl.semaphore_signal(barrier, inc=1, device_id=(me.b, z), device_id_type=MESH)
    pl.semaphore_wait(barrier, len(blk_steps) + 2)


class LineSum:
    def __init__(self, me, part, first, second, sems, rows):
        self.me, self.part, self.first, self.second, self.sems, self.rows = (
            me, part, first, second, sems, rows,
        )

    def at(self, ref, p):
        return ref.at[pl.ds(pl.multiple_of(p * self.rows, self.rows), self.rows), :]

    def copy(self, stage, p):
        me = self.me
        src = (self.part, self.part, self.first)[stage]
        dst = (self.first, self.second, self.first)[stage]
        target = (me.pair, me.across, me.pair)[stage]
        return remote(
            self.at(src, p), self.at(dst, p),
            self.sems.at[2 * stage, p], self.sems.at[2 * stage + 1, p], me.b, target,
        )

    def give(self, p):
        @pl.when(self.me.outer)
        def _():
            self.copy(0, p).start()

    def fold(self, p):
        @pl.when(self.me.inner)
        def _():
            self.copy(0, p).wait_recv()
            mine, got = self.at(self.part, p), self.at(self.first, p)
            mine[...] = (mine[...].astype(F32) + got[...].astype(F32)).astype(BF16)
            self.copy(1, p).start()

    def unfold(self, p):
        @pl.when(self.me.inner)
        def _():
            self.copy(1, p).wait_recv()
            mine, got, out = self.at(self.part, p), self.at(self.second, p), self.at(self.first, p)
            out[...] = (mine[...].astype(F32) + got[...].astype(F32)).astype(BF16)
            self.copy(2, p).start()

    def take(self, p):
        @pl.when(self.me.outer)
        def _():
            self.copy(2, p).wait_recv()

    def drain_outer(self, pieces):
        @pl.when(self.me.outer)
        def _():
            def one(p, carry):
                self.copy(0, p).wait_send()
                return carry

            lax.fori_loop(0, pieces, one, 0)

    def drain_inner(self, pieces):
        @pl.when(self.me.inner)
        def _():
            def one(p, carry):
                self.copy(1, p).wait_send()
                self.copy(2, p).wait_send()
                return carry

            lax.fori_loop(0, pieces, one, 0)

    def drain(self, pieces):
        self.drain_outer(pieces)
        self.drain_inner(pieces)


class LineGather:
    def __init__(self, me, view, ssem, rsem, last):
        self.me, self.view, self.ssem, self.rsem, self.last = me, view, ssem, rsem, last

    def copy(self, way, hop, p):
        t = self.me.t

        def sent():
            slot = t - (hop - 1) if way == 0 else t + (hop - 1)
            ref = self.view(slot, p)
            target = t + 1 if way == 0 else t - 1
            return remote(ref, ref, self.ssem.at[way, hop - 1, p], self.rsem.at[way, hop - 1, p], self.me.b, target)

        def got():
            slot = t - hop if way == 0 else t + hop
            ref = self.view(slot, p)
            target = t - 1 if way == 0 else t + 1
            return remote(ref, ref, self.ssem.at[way, hop - 1, p], self.rsem.at[way, hop - 1, p], self.me.b, target)

        return sent, got

    def sends(self, way, hop):
        t = self.me.t
        if way == 0:
            return jnp.logical_and(t - (hop - 1) >= 0, t + 1 <= self.last)
        return jnp.logical_and(t + (hop - 1) <= self.last, t >= 1)

    def gets(self, way, hop):
        t = self.me.t
        return t - hop >= 0 if way == 0 else t + hop <= self.last

    def send(self, hop, p):
        for way in (0, 1):

            @pl.when(self.sends(way, hop))
            def _(way=way):
                self.copy(way, hop, p)[0]().start()

    def step(self, hop, p, also=None):
        for way in (0, 1):

            @pl.when(self.gets(way, hop))
            def _(way=way):
                self.copy(way, hop, p)[1]().wait_recv()
                if also is not None:
                    also(way, hop).start()

        if hop < self.last:
            self.send(hop + 1, p)

    def drain(self, p):
        for hop in range(1, self.last + 1):
            for way in (0, 1):

                @pl.when(self.sends(way, hop))
                def _(way=way, hop=hop):
                    self.copy(way, hop, p)[0]().wait_send()


class BlockSum:
    def __init__(self, me, make, outs, held, mates, chips, sems, spare):
        self.me, self.make, self.outs, self.spare = me, make, outs, spare
        self.held, self.mates, self.chips, self.sems = held, mates, chips, sems

    def to_mate(self, k):
        me = self.me
        return remote(
            self.held(k % 2), self.mates(k), self.sems.at[0, k], self.sems.at[1, k], me.mate, me.t
        )

    def to_chip(self, k):
        me = self.me
        return remote(
            self.mates(k), self.chips(k), self.sems.at[2, k], self.sems.at[3, k],
            me.chip_at(k) * 2 + me.core, me.t,
        )

    def lend(self, k):
        me = self.me
        if k >= 2:
            self.to_mate(k - 2).wait_send()
        held = self.held(k % 2)
        even = me.core == 0
        for (lo, hi, value), out, spare in zip(self.make(me.chip_at(k)), self.outs, self.spare):
            half = value.shape[0] // 2
            low, high = value[:half], value[half:]
            held[:, lo:hi] = jnp.where(even, high, low).astype(BF16)
            if k % 2 == 0:
                spare[...] = jnp.where(even, low, high).astype(BF16)
            else:
                out[...] = jnp.where(even, low, high)
        self.to_mate(k).start()

    def merge(self, k, spans):
        self.to_mate(k).wait_recv()
        mates = self.mates(k)
        for (lo, hi), out, spare in zip(spans, self.outs, self.spare):
            own = spare[...].astype(F32) if k % 2 == 0 else out[...]
            total = own + mates[:, lo:hi].astype(F32)
            if k < 3:
                mates[:, lo:hi] = total.astype(BF16)
            else:
                out[...] = total
        if k < 3:
            self.to_chip(k).start()

    def finish(self, spans):
        for k in range(3):
            self.to_chip(k).wait_recv()
            chips = self.chips(k)
            for (lo, hi), out in zip(spans, self.outs):
                out[...] += chips[:, lo:hi].astype(F32)

    def drain(self):
        for k in (2, 3):
            self.to_mate(k).wait_send()
        for k in range(3):
            self.to_chip(k).wait_send()


def norm_rows(values):
    inverse = lax.rsqrt(jnp.mean(values * values, axis=-1, keepdims=True) + norm_eps)
    return values * inverse, inverse


def turn(values, cs_ref, sign):
    cosine, sine = cs_ref[0:HALF, :], cs_ref[HALF:HEAD_SIZE, :] * sign
    pieces = []
    for h in range(values.shape[0] // HEAD_SIZE):
        low = values[h * HEAD_SIZE : h * HEAD_SIZE + HALF]
        high = values[h * HEAD_SIZE + HALF : (h + 1) * HEAD_SIZE]
        pieces.append(low * cosine - high * sine)
        pieces.append(high * cosine + low * sine)
    return jnp.concatenate(pieces, axis=0)


def fill_bias(bias, st_ref, key_start, query_start):
    key_place = lax.broadcasted_iota(jnp.int32, bias.shape, 0) + key_start
    query_place = lax.broadcasted_iota(jnp.int32, bias.shape, 1) + query_start
    allowed = jnp.logical_and(key_place >= st_ref[0:1, :], key_place <= query_place)
    bias[...] = jnp.where(allowed, 0.0, neg_fill)


def heads_of(h, group):
    g = h // group
    return slice(h * HEAD_SIZE, (h + 1) * HEAD_SIZE), slice(g * HEAD_SIZE, (g + 1) * HEAD_SIZE), g


def layer_kernel(
    dims,
    len_ref, ag_ref, mg_ref, hid_hbm, og_hbm, wq_hbm, wk_hbm, wv_hbm, wo_hbm, wg_hbm, wu_hbm, wd_hbm,
    lo_out, ig_out, gq_ref, gk_ref, gv_ref, go_ref, gg_ref, gu_ref, gd_ref, gag_ref, gmg_ref,
    hid, og, wq, wkv, wo, wg, wu, wd, kv, norm, attn, qt, ot, bias, mid, act, dg, du,
    p2, a2, b2, p3, a3, b3, dbr, dot_ref, dq, acc, low_t, dqr, dkvr,
    kv_mates, kv_chips, held_a, held_b, chips_b, held_c, mates_c, chips_c, total_c,
    turns, starts, m_ref, l_ref, lse, delta, gain, gain_in,
    load_sem, kv_sem, wo_sem, wo_plane_sem, wo_mate_sem, at_sem, sem2, sem3, sem4, kvs_sem, rs_sem, gain_sem, out_sem,
    mate_ready, chip_ready,
):
    rows, piece, chunk, share = dims["rows"], dims["piece"], dims["chunk"], dims["share"]
    q_heads, group, kv_width, n_docs = dims["q_heads"], dims["group"], dims["kv_width"], dims["n_docs"]
    n_pieces, n_chunks = rows // piece, rows // chunk
    per = chunk // piece
    width, hidden_units = wg.shape
    q_width = q_heads * HEAD_SIZE
    last = wo.shape[0] - 1
    me = Place()
    scale2 = SCORE_SCALE * LOG2E

    def each(f, lo, hi):
        def one(p, carry):
            f(p)
            return carry

        lax.fori_loop(lo, hi, one, 0)

    barrier = pltpu.get_barrier_semaphore()
    for s in range(1, 8):
        pl.semaphore_signal(barrier, inc=1, device_id=(me.slot(s), me.t), device_id_type=MESH)
    for z in (me.pair, me.across):
        pl.semaphore_signal(barrier, inc=1, device_id=(me.b, z), device_id_type=MESH)
    loads = {}
    for i, (name, source, target) in enumerate((
        ("wo", wo_hbm, wo.at[me.t]), ("hid", hid_hbm, hid), ("wk", wk_hbm, wkv.at[0:kv_width]),
        ("wv", wv_hbm, wkv.at[kv_width : 2 * kv_width]), ("wq", wq_hbm, wq), ("wg", wg_hbm, wg),
        ("wu", wu_hbm, wu), ("og", og_hbm, og), ("wd", wd_hbm, wd),
    )):
        loads[name] = pltpu.make_async_copy(source, target, load_sem.at[i])
    for name in ("wo", "hid", "wk", "wv"):
        loads[name].start()

    attn_gain, mlp_gain = ag_ref[...].reshape(1, width), mg_ref[...].reshape(1, width)

    def chunk_rows(c):
        return pl.ds(pl.multiple_of(c * chunk, chunk), chunk)

    def first_norm(c):
        r = chunk_rows(c)
        normed, _ = norm_rows(hid[r, :].astype(F32))
        norm[r, :] = (normed * attn_gain).astype(BF16)

    part = share // 4
    my_half = pl.ds(pl.multiple_of(me.core * share, share), share)

    def wo_rows(slot, p):
        first = me.core * share + p * 2 * part + (me.x, me.y)[p] * part
        return wo.at[slot, pl.ds(pl.multiple_of(first, part), part), :]

    whole_wo = LineGather(me, wo_rows, wo_sem.at[0], wo_sem.at[1], last)

    def wo_plane(way, hop, p):
        ref = wo_rows(me.t - hop if way == 0 else me.t + hop, p)
        return remote(
            ref, ref, wo_plane_sem.at[0, p, way, hop - 1], wo_plane_sem.at[1, p, way, hop - 1],
            me.slot(2 + 2 * p), me.t,
        )

    def wo_to_mate(way, hop):
        ref = wo.at[me.t - hop if way == 0 else me.t + hop, my_half, :]
        return remote(
            ref, ref, wo_mate_sem.at[0, way, hop - 1], wo_mate_sem.at[1, way, hop - 1], me.mate, me.t
        )

    def each_wo(hops, action):
        for hop in hops:
            for way in (0, 1):

                @pl.when(whole_wo.gets(way, hop))
                def _(way=way, hop=hop):
                    action(way, hop)

    def wo_spread(way, hop):
        for p in (0, 1):
            wo_plane(way, hop, p).start()

    def wo_lend(way, hop):
        for p in (0, 1):
            wo_plane(way, hop, p).wait_recv()
        wo_to_mate(way, hop).start()

    def wo_line(hop):
        for p in (0, 1):
            whole_wo.step(hop, p)

    loads["wq"].start()
    places = me.b * rows + lax.broadcasted_iota(jnp.int32, (1, rows), 1)
    start, end = jnp.zeros((1, rows), jnp.int32), jnp.int32(0)
    for k in range(n_docs):
        end = end + len_ref[k]
        start = jnp.where(places >= end, end, start)
    starts[...] = jnp.broadcast_to(start, starts.shape)
    order = lax.broadcasted_iota(jnp.int32, (HALF, 1), 0).astype(F32)
    freqs = jnp.exp(order * (-2.0 / HEAD_SIZE * math.log(rope_base)))
    angle = freqs * (places - start).astype(F32)
    turns[0:HALF, :] = jnp.cos(angle)
    turns[HALF:HEAD_SIZE, :] = jnp.sin(angle)
    loads["hid"].wait()
    each(first_norm, 0, n_chunks)
    loads["wk"].wait()
    loads["wv"].wait()
    both_t = dot_nt(wkv[...], norm[...])
    kv[me.b, 0:kv_width, :] = turn(both_t[0:kv_width], turns, 1.0).astype(BF16)
    kv[me.b, kv_width : 2 * kv_width, :] = both_t[kv_width : 2 * kv_width].astype(BF16)

    loads["wo"].wait()
    pl.semaphore_wait(barrier, 9)
    for p in (0, 1):
        whole_wo.send(1, p)
    def kv_copy(slot, target, n):
        return remote(kv.at[slot], kv.at[slot], kv_sem.at[0, n], kv_sem.at[1, n], target, me.t)

    def share_kv(s):
        @pl.when(me.slot(s) > me.b)
        def _():
            kv_copy(me.b, me.slot(s), s).start()

    for s in (1, 2, 4):
        share_kv(s)
    for name in ("wg", "wu", "og", "wd"):
        loads[name].start()
    loads["wq"].wait()
    qt[...] = turn(dot_nn(norm[...], wq[...]).T, turns, 1.0).astype(BF16)
    m_ref[...] = jnp.full(m_ref.shape, neg_fill, F32)
    l_ref[...] = jnp.zeros(l_ref.shape, F32)
    ot[...] = jnp.zeros(ot.shape, F32)

    def attend(s, carry):
        slot = me.slot(s)
        arrives = jnp.logical_and(s > 0, slot < me.b)

        @pl.when(arrives)
        def _():
            kv_copy(slot, me.mate, s).wait_recv()

        @pl.when(jnp.logical_and(arrives, s % 2 == 0))
        def _():
            kv_copy(slot, me.mate, s + 1).start()

        for hop, turn_at in ((1, 2), (2, 3), (3, 5)):

            @pl.when(s == turn_at)
            def _(hop=hop):
                wo_line(hop)

        @pl.when(s == 6)
        def _():
            each_wo((1, 2, 3), wo_spread)

        @pl.when(slot <= me.b)
        def _():
            fill_bias(bias, starts, slot * rows, me.b * rows)
            for h in range(q_heads):
                qs, ks, g = heads_of(h, group)
                vs = slice(kv_width + g * HEAD_SIZE, kv_width + (g + 1) * HEAD_SIZE)
                scores = dot_tn(kv[slot, ks, :], qt[qs, :]) + bias[...]
                old = m_ref[h : h + 1, :]
                new = jnp.maximum(old, jnp.max(scores, axis=0, keepdims=True))
                probs = jnp.exp2((scores - new) * scale2)
                keep = jnp.exp2((old - new) * scale2)
                m_ref[h : h + 1, :] = new
                l_ref[h : h + 1, :] = l_ref[h : h + 1, :] * keep + jnp.sum(probs, axis=0, keepdims=True)
                ot[qs, :] = ot[qs, :] * keep + dot_nn(kv[slot, vs, :], probs.astype(BF16))

        @pl.when(s == 1)
        def _():
            share_kv(6)

        return carry

    lax.fori_loop(0, 8, attend, 0)

    line_attn = LineGather(
        me, lambda slot, p: attn.at[slot, chunk_rows(p), :], at_sem.at[0], at_sem.at[1], last
    )
    for h in range(q_heads):
        qs, _, _ = heads_of(h, group)
        ot[qs, :] = ot[qs, :] / l_ref[h : h + 1, :]
    for c in range(n_chunks):
        attn[me.t, c * chunk : (c + 1) * chunk, :] = ot[:, c * chunk : (c + 1) * chunk].T.astype(BF16)
        line_attn.send(1, c)
    lse[...] = jnp.zeros(lse.shape, F32)
    lse[0:q_heads, :] = m_ref[0:q_heads, :] * scale2 + jnp.log2(l_ref[0:q_heads, :])
    for name in ("wg", "wu", "og", "wd"):
        loads[name].wait()
    line_attn.step(1, 0)
    each_wo((1, 2, 3), wo_lend)
    line_attn.step(2, 0)
    line_attn.step(3, 0)
    line_attn.step(1, 1)
    each_wo((1, 2, 3), lambda way, hop: wo_to_mate(way, hop).wait_recv())

    back = LineSum(me, p2, a2, b2, sem2, piece)
    forth_rows = rows // 8
    forth = LineSum(me, p3, a3, b3, sem3, forth_rows)
    forth_pieces = 8
    adds_middle = (me.t == 1).astype(F32)

    def feed(c, carry):
        r = chunk_rows(c)

        for n in range(0, width, 512):
            ns = slice(n, n + 512)
            total = hid[r, ns].astype(F32)
            for z in range(last + 1):
                total = total + dot_nn(attn[z, r, :], wo[z, :, ns])
            mid[r, ns] = total
        normed, _ = norm_rows(mid[r, :])
        norm[r, :] = (normed * mlp_gain).astype(BF16)

        @pl.when(c < n_chunks - 1)
        def _():
            line_attn.step(2, c + 1)

        for n in range(0, hidden_units, 512):
            ns = slice(n, n + 512)
            gate = dot_nn(norm[r, :], wg[:, ns])
            up = dot_nn(norm[r, :], wu[:, ns])
            grad = dot_nt(og[r, :], wd[ns, :])
            sig = 1.0 / (1.0 + jnp.exp(-gate))
            silu = gate * sig
            act[r, ns] = (silu * up).astype(BF16)
            dg[r, ns] = (grad * up * sig * (1.0 + gate * (1.0 - sig))).astype(BF16)
            du[r, ns] = (grad * silu).astype(BF16)
            if n == 0:

                @pl.when(c < n_chunks - 2)
                def _():
                    line_attn.step(1, c + 2)

        for n in range(0, width, 512):
            ns = slice(n, n + 512)
            p2[r, ns] = (dot_nt(dg[r, :], wg[ns, :]) + dot_nt(du[r, :], wu[ns, :])).astype(BF16)
        each(back.give, c * per, (c + 1) * per)

        @pl.when(c < n_chunks - 1)
        def _():
            line_attn.step(3, c + 1)

        @pl.when(c >= 2)
        def _():
            each(back.fold, (c - 2) * per, (c - 1) * per)

        @pl.when(c >= 3)
        def _():
            each(back.unfold, (c - 3) * per, (c - 2) * per)

        for n in range(0, width, 512):
            ns = slice(n, n + 512)
            p3[r, ns] = (dot_nn(act[r, :], wd[:, ns]) + mid[r, ns] * adds_middle).astype(BF16)
        return carry

    lax.fori_loop(0, n_chunks, feed, 0)
    pl.semaphore_signal(mate_ready, inc=1, device_id=(me.mate, me.t), device_id_type=MESH)
    for k in range(3):
        pl.semaphore_signal(
            chip_ready, inc=1, device_id=(me.chip_at(k) * 2 + me.core, me.t), device_id_type=MESH
        )
    pair = 2 * share

    def pair_columns(ref, chip):
        return ref[:, pl.ds(pl.multiple_of(chip * pair, pair), pair)]

    def slots(ref, first, columns):
        return lambda k: ref.at[(first + k) * share : (first + k + 1) * share, 0:columns]

    sum_gate = BlockSum(
        me, lambda m: [(0, hidden_units, dot_tn(pair_columns(norm, m), dg[...]))], [gg_ref],
        lambda k: held_a.at[0, k], slots(wg, 0, hidden_units), slots(wg, 4, hidden_units), rs_sem.at[0],
        [slots(wg, 7, hidden_units)(0)],
    )
    sum_up = BlockSum(
        me, lambda m: [(0, hidden_units, dot_tn(pair_columns(norm, m), du[...]))], [gu_ref],
        lambda k: held_a.at[1, k], slots(wu, 0, hidden_units), slots(wu, 4, hidden_units), rs_sem.at[1],
        [slots(wu, 7, hidden_units)(0)],
    )
    span_a = [(0, hidden_units)]
    pl.semaphore_wait(mate_ready, 1)
    gain[...] = jnp.zeros(gain.shape, F32)

    def middle_grad(c):
        each(back.take, c * per, (c + 1) * per)
        r = chunk_rows(c)
        normed, inverse = norm_rows(mid[r, :])
        grad = a2[r, :].astype(F32)
        scaled = grad * mlp_gain
        gain[1:2, :] += jnp.sum(grad * normed, axis=0, keepdims=True)
        found = og[r, :].astype(F32) + inverse * (
            scaled - normed * jnp.mean(scaled * normed, axis=-1, keepdims=True)
        )
        mid[r, :] = found
        dbr[r, :] = found.astype(BF16)

    def fold_on(lo, hi):
        def one(p, carry):
            back.fold(p)
            back.unfold(p - per)
            return carry

        lax.fori_loop(lo, hi, one, 0)

    def lend_both(k):
        sum_gate.lend(k)
        sum_up.lend(k)

    def merge_both(k):
        sum_gate.merge(k, span_a)
        sum_up.merge(k, span_a)

    lend_both(0)
    fold_on((n_chunks - 2) * per, (n_chunks - 2) * per + per // 2)
    lend_both(1)
    back.drain_outer(n_pieces)
    each(forth.give, 0, forth_pieces)
    fold_on((n_chunks - 2) * per + per // 2, (n_chunks - 1) * per)
    pl.semaphore_wait(chip_ready, 3)
    merge_both(0)
    fold_on((n_chunks - 1) * per, n_pieces - per // 2)
    lend_both(2)
    merge_both(1)
    fold_on(n_pieces - per // 2, n_pieces)
    merge_both(2)
    each(back.unfold, n_pieces - per, n_pieces)
    each(middle_grad, 0, n_chunks - 1)
    each(middle_grad, n_chunks - 1, n_chunks)
    dot_ref[...] = dot_nt(wo[me.t], dbr[...]).astype(BF16)
    delta[...] = jnp.zeros(delta.shape, F32)
    for h in range(q_heads):
        qs, _, _ = heads_of(h, group)
        delta[h : h + 1, :] = jnp.sum(dot_ref[qs, :].astype(F32) * ot[qs, :], axis=0, keepdims=True)
    dq[...] = jnp.zeros(dq.shape, F32)
    back.drain_inner(n_pieces)
    ahead = 3
    each(forth.fold, 0, ahead)

    for s in (1, 2, 4, 6):

        @pl.when(me.slot(s) > me.b)
        def _(s=s):
            kv_copy(me.b, me.slot(s), s).wait_send()

    for s in (2, 4, 6):

        @pl.when(me.slot(s) < me.b)
        def _(s=s):
            kv_copy(me.slot(s), me.mate, s + 1).wait_send()

    def kv_to_mate(k):
        return remote(
            kv.at[me.chip_at(k) * 2 + 1 - me.core], kv_mates.at[k], kvs_sem.at[0, k], kvs_sem.at[1, k],
            me.mate, me.t,
        )

    def kv_to_chip(k):
        return remote(
            kv_mates.at[k], kv_chips.at[k], kvs_sem.at[2, k], kvs_sem.at[3, k],
            me.chip_at(k) * 2 + me.core, me.t,
        )

    def attend_back(u, carry):
        k, own = u // 2, u % 2
        chip = me.chip_at(k)
        slot = chip * 2 + (me.core + 1 - own) % 2

        @pl.when(u + ahead < forth_pieces)
        def _():
            forth.fold(u + ahead)

        @pl.when(u >= 2)
        def _():
            forth.unfold(u - 2)

        @pl.when(slot <= me.b)
        def _():
            fill_bias(bias, starts, slot * rows, me.b * rows)
            for g in range(q_heads // group):
                ks = slice(g * HEAD_SIZE, (g + 1) * HEAD_SIZE)
                vs = slice(kv_width + g * HEAD_SIZE, kv_width + (g + 1) * HEAD_SIZE)
                key_t, value_t = kv[slot, ks, :], kv[slot, vs, :]
                grad_k = grad_v = None
                for h in range(g * group, (g + 1) * group):
                    qs, _, _ = heads_of(h, group)
                    query_t, grad_t = qt[qs, :], dot_ref[qs, :]
                    scores = dot_tn(key_t, query_t) + bias[...]
                    probs = jnp.exp2(scores * scale2 - lse[h : h + 1, :])
                    grad_p = dot_tn(value_t, grad_t)
                    grad_s = (probs * (grad_p - delta[h : h + 1, :])).astype(BF16)
                    one_v = dot_nt(grad_t, probs.astype(BF16))
                    one_k = dot_nt(query_t, grad_s)
                    grad_v = one_v if grad_v is None else grad_v + one_v
                    grad_k = one_k if grad_k is None else grad_k + one_k
                    dq[qs, :] += dot_nn(key_t, grad_s)
                acc[ks, :] = grad_k
                acc[vs, :] = grad_v

        @pl.when(jnp.logical_and(own == 0, slot <= me.b))
        def _():
            kv[slot] = acc[...].astype(BF16)
            kv_to_mate(k).start()

        @pl.when(jnp.logical_and(own == 1, chip < me.chip))
        def _():
            kv_to_mate(k).wait_recv()
            kv_mates[k] = (acc[...] + kv_mates[k].astype(F32)).astype(BF16)
            kv_to_chip(k).start()

        return carry

    lax.fori_loop(0, 8, attend_back, 0)
    low_t[0:q_width, :] = turn(dq[...] * SCORE_SCALE, turns, -1.0).astype(BF16)
    dqr[...] = low_t[0:q_width, :].T

    def first_norm_again(c):
        r = chunk_rows(c)
        normed, _ = norm_rows(hid[r, :].astype(F32))
        norm[r, :] = (normed * attn_gain).astype(BF16)


    @pl.when(me.core == 0)
    def _():
        kv_to_mate(3).wait_recv()
        acc[...] += kv_mates[3].astype(F32)

    for k in range(3):

        @pl.when(me.chip_at(k) > me.chip)
        def _(k=k):
            kv_to_chip(k).wait_recv()
            acc[...] += kv_chips[k].astype(F32)

    low_t[q_width : q_width + kv_width, :] = turn(acc[0:kv_width, :] * SCORE_SCALE, turns, -1.0).astype(BF16)
    low_t[q_width + kv_width :, :] = acc[kv_width : 2 * kv_width, :].astype(BF16)
    dkvr[...] = low_t[q_width:, :].T

    each(forth.take, 0, 2)
    end_sum = LineSum(me, p2, a2, b2, sem4, piece)

    def input_part(c):
        r = chunk_rows(c)
        for n in range(0, width, 512):
            ns = slice(n, n + 512)
            p2[r, ns] = (dot_nt(dqr[r, :], wq[ns, :]) + dot_nn(dkvr[r, :], wkv[:, ns])).astype(BF16)
        each(end_sum.give, c * per, (c + 1) * per)

    each(input_part, 0, n_chunks)
    each(forth.unfold, forth_pieces - 2, forth_pieces)

    def make_b(m):
        yield 0, hidden_units, dot_tn(pair_columns(og, m), act[...])
        yield hidden_units, hidden_units + q_width, dot_tn(pair_columns(dbr, m), attn[me.t])

    def make_c(m):
        columns = pair_columns(norm, m)
        yield 0, q_width, dot_tn(columns, dqr[...])
        yield q_width, q_width + 2 * kv_width, dot_tn(columns, dkvr[...])

    width_b = hidden_units + q_width
    in_wd = slots(wd, 0, width_b)
    sum_b = BlockSum(
        me, make_b, [gd_ref, go_ref], lambda k: held_b.at[k], in_wd,
        lambda k: in_wd(4) if k == 0 else chips_b.at[k - 1], rs_sem.at[2],
        [dg.at[0:share, :], du.at[0:share, 0:q_width]],
    )
    span_b = [(0, hidden_units), (hidden_units, width_b)]
    total_parts = [total_c.at[:, 0:q_width], total_c.at[:, q_width : q_width + 2 * kv_width]]
    sum_c = BlockSum(
        me, make_c, total_parts, lambda k: held_c.at[k], lambda k: mates_c.at[k], lambda k: chips_c.at[k],
        rs_sem.at[3],
        [dg.at[share : 2 * share, 0:q_width], du.at[share : 2 * share, 0 : 2 * kv_width]],
    )
    span_c = [(0, q_width), (q_width, q_width + 2 * kv_width)]
    work = [(functools.partial(lend_both, 3), functools.partial(merge_both, 3))]
    for sums, spans in ((sum_b, span_b), (sum_c, span_c)):
        for k in range(4):
            work.append((functools.partial(sums.lend, k), functools.partial(sums.merge, k, spans)))
    done, late = 0, None
    for i, (lend, merge) in enumerate(work):
        if i == 1:
            each(first_norm_again, 0, n_chunks)
        lend()
        upto = n_pieces * (i + 1) // len(work)
        for p in range(done, upto):
            end_sum.fold(p)
            if p >= 1:
                end_sum.unfold(p - 1)
        done = upto
        if late is not None:
            late()
        late = merge
    end_sum.unfold(n_pieces - 1)
    late()

    each(forth.take, 2, forth_pieces)
    lo_save = pltpu.make_async_copy(a3, lo_out, out_sem.at[0])
    lo_save.start()

    def input_rows(c):
        each(end_sum.take, c * per, (c + 1) * per)
        r = chunk_rows(c)
        normed, inverse = norm_rows(hid[r, :].astype(F32))
        grad = a2[r, :].astype(F32)
        scaled = grad * attn_gain
        gain[0:1, :] += jnp.sum(grad * normed, axis=0, keepdims=True)
        found = inverse * (scaled - normed * jnp.mean(scaled * normed, axis=-1, keepdims=True))
        dbr[r, :] = (mid[r, :] + found).astype(BF16)

    each(input_rows, 0, n_chunks)

    def gain_copy(s):
        return remote(gain, gain_in.at[s], gain_sem.at[0, s], gain_sem.at[1, s], me.slot(s), me.t)

    for s in range(1, 8):
        gain_copy(s).start()
    ig_save = pltpu.make_async_copy(dbr, ig_out, out_sem.at[1])
    ig_save.start()
    sum_gate.finish(span_a)
    sum_up.finish(span_a)
    sum_b.finish(span_b)
    sum_c.finish(span_c)
    gq_ref[...] = total_c[:, 0:q_width]
    gk_ref[...] = total_c[:, q_width : q_width + kv_width]
    gv_ref[...] = total_c[:, q_width + kv_width : q_width + 2 * kv_width]
    for s in range(1, 8):
        gain_copy(s).wait_recv()
    gains = gain[...]
    for s in range(1, 8):
        gains = gains + gain_in[s]
    gain_in[0] = gains
    mine = jnp.zeros((8, share), F32)
    for j in range(8):
        mine = mine + jnp.where(me.b == j, gain_in[0, :, j * share : (j + 1) * share], 0.0)
    gag_ref[...] = mine[0, :]
    gmg_ref[...] = mine[1, :]

    for s in range(1, 8):
        gain_copy(s).wait_send()
    for p in (0, 1):
        whole_wo.drain(p)

    def wo_done(way, hop):
        for p in (0, 1):
            wo_plane(way, hop, p).wait_send()
        wo_to_mate(way, hop).wait_send()

    each_wo((1, 2, 3), wo_done)
    each(line_attn.drain, 0, n_chunks)
    forth.drain(forth_pieces)
    end_sum.drain(n_pieces)
    for sums in (sum_gate, sum_up, sum_b, sum_c):
        sums.drain()
    for k in range(4):
        chip = me.chip_at(k)
        slot = chip * 2 + 1 - me.core

        @pl.when(slot <= me.b)
        def _(k=k):
            kv_to_mate(k).wait_send()

        if k < 3:

            @pl.when(chip < me.chip)
            def _(k=k):
                kv_to_chip(k).wait_send()

    lo_save.wait()
    ig_save.wait()


def hand_over(n, *refs):
    sources, targets, held, sems = refs[:n], refs[n : 2 * n], refs[2 * n : 3 * n], refs[3 * n]
    ins = [pltpu.make_async_copy(a, h, sems.at[0, i]) for i, (a, h) in enumerate(zip(sources, held))]
    outs = [pltpu.make_async_copy(h, b, sems.at[1, i]) for i, (h, b) in enumerate(zip(held, targets))]
    for copy in ins:
        copy.start()
    for first, second in zip(ins, outs):
        first.wait()
        second.start()
    for copy in outs:
        copy.wait()


def kernel_shards(
    hidden_in, out_grad, lengths, attn_gain, w_query, key_projection_weight, value_projection_weight,
    w_out, mlp_gain, w_gate, w_up, w_down,
):
    rows, width = hidden_in.shape
    q_width, kv_width = w_query.shape[1], key_projection_weight.shape[1]
    hidden_units = w_gate.shape[1]
    blocks, line_size = lax.axis_size("blk"), lax.axis_size("tp")
    share = width // blocks
    piece, chunk = rows // 16, rows // 4
    pieces, chunks = rows // piece, rows // chunk
    dims = dict(
        rows=rows, piece=piece, chunk=chunk, share=share, q_heads=q_width // HEAD_SIZE,
        group=q_width // kv_width, kv_width=kv_width, n_docs=lengths.shape[0],
    )
    vmem, hbm = pl.BlockSpec(memory_space=pltpu.VMEM), pl.BlockSpec(memory_space=pl.ANY)
    smem = pl.BlockSpec(memory_space=pltpu.SMEM)
    dma, regular = pltpu.SemaphoreType.DMA, pltpu.SemaphoreType.REGULAR

    def shape(dtype, *dims_):
        return jax.ShapeDtypeStruct(dims_, dtype)

    def low(*dims_):
        return pltpu.VMEM(dims_, BF16)

    def full(*dims_):
        return pltpu.VMEM(dims_, F32)

    line = [low(rows, width)] * 3
    width_b, width_c = hidden_units + q_width, q_width + 2 * kv_width
    shapes = (
        shape(BF16, rows, width), shape(BF16, rows, width), shape(F32, share, q_width),
        shape(F32, share, kv_width), shape(F32, share, kv_width), shape(F32, share, q_width),
        shape(F32, share, hidden_units), shape(F32, share, hidden_units), shape(F32, share, hidden_units),
        shape(F32, share), shape(F32, share),
    )
    outs = pl.pallas_call(
        functools.partial(layer_kernel, dims),
        out_shape=shapes,
        in_specs=[smem, vmem, vmem] + [hbm] * 9,
        out_specs=(hbm, hbm) + (vmem,) * 9,
        scratch_shapes=[
            low(rows, width), low(rows, width), low(width, q_width), low(2 * kv_width, width),
            low(line_size, q_width, width), low(width, hidden_units), low(width, hidden_units),
            low(hidden_units, width), low(blocks, 2 * kv_width, rows), low(rows, width),
            low(line_size, rows, q_width), low(q_width, rows), full(q_width, rows), full(rows, rows),
            full(rows, width), low(rows, hidden_units), low(rows, hidden_units), low(rows, hidden_units),
            *line, *line, low(rows, width), low(q_width, rows), full(q_width, rows), full(2 * kv_width, rows),
            low(width_c, rows), low(rows, q_width), low(rows, 2 * kv_width),
            low(4, 2 * kv_width, rows), low(3, 2 * kv_width, rows),
            low(2, 2, share, hidden_units), low(2, share, width_b), low(2, share, width_b),
            low(2, share, width_c), low(4, share, width_c), low(3, share, width_c), full(share, width_c),
            full(HEAD_SIZE, rows), pltpu.VMEM((8, rows), jnp.int32), full(8, rows), full(8, rows), full(8, rows),
            full(8, rows), full(8, width), full(8, 8, width),
            dma((9,)), dma((2, 8)), dma((2, 2, line_size - 1, 2)), dma((2, 2, 2, line_size - 1)),
            dma((2, 2, line_size - 1)),
            dma((2, 2, line_size - 1, chunks)), dma((6, pieces)), dma((6, pieces)), dma((6, pieces)),
            dma((4, 4)), dma((4, 4, 4)), dma((2, 8)), dma((2,)), regular, regular,
        ],
        compiler_params=pltpu.CompilerParams(
            collective_id=0, has_side_effects=True, vmem_limit_bytes=VMEM_BYTES
        ),
    )(
        lengths, attn_gain, mlp_gain, hidden_in, out_grad, w_query, key_projection_weight.T,
        value_projection_weight.T, w_out, w_gate, w_up, w_down,
    )
    outs = pl.pallas_call(
        functools.partial(hand_over, len(shapes)),
        out_shape=shapes,
        in_specs=[hbm] * len(shapes),
        out_specs=(hbm,) * len(shapes),
        scratch_shapes=[pltpu.VMEM(s.shape, s.dtype) for s in shapes] + [dma((2, len(shapes)))],
    )(*outs)
    layer_out, input_grad, grad_query, grad_key, grad_value, grad_out, grad_gate, grad_up, grad_down, g1, g2 = outs
    return (
        layer_out, input_grad, grad_query, grad_key, grad_value, grad_out.T, grad_gate, grad_up, grad_down.T, g1, g2,
    )


def solution(mesh):
    sizes = dict(mesh.shape)
    small = sizes["blk"] == 8 and sizes["tp"] == 4
    placed = (
        P("blk", None),
        P("blk", None),
        P(),
        P(),
        P(None, "tp"),
        P(None, "tp"),
        P(None, "tp"),
        P("tp", None),
        P(),
        P(None, "tp"),
        P(None, "tp"),
        P("tp", None),
    )
    return jax.shard_map(
        kernel_shards if small else shards,
        mesh=mesh,
        in_specs=placed,
        out_specs=(
            P("blk", None),
            P("blk", None),
            P("blk", "tp"),
            P("blk", "tp"),
            P("blk", "tp"),
            P("tp", "blk"),
            P("blk", "tp"),
            P("blk", "tp"),
            P("tp", "blk"),
            P("blk"),
            P("blk"),
        ),
        check_vma=False,
    )
```

```python
import functools
import math

import jax
import jax.numpy as jnp
from jax import lax
from jax.experimental import pallas as pl
from jax.experimental.pallas import tpu as pltpu
from jax.sharding import PartitionSpec as P

HEAD_SIZE = 96


norm_eps = 1e-05
rope_base = 100000.0
neg_fill = -1e30


def doc_places(lengths, places):
    doc_ends = jnp.cumsum(lengths)
    passed = (places[:, None] >= doc_ends[None, :]).astype(jnp.int32)
    segment = jnp.sum(passed, axis=1)
    preceding = jnp.sum(passed * lengths[None, :], axis=1)
    return (segment, places - preceding)


def apply_rotary(values, token_position, heads, sign_value):
    half_size = HEAD_SIZE // 2
    freqs = rope_base ** (-(2.0 * jnp.arange(half_size, dtype=jnp.float32)) / HEAD_SIZE)
    angle = token_position.astype(jnp.float32)[:, None] * freqs[None, :]
    cosine = jnp.cos(angle)[:, None, :]
    sine = sign_value * jnp.sin(angle)[:, None, :]
    shaped = values.reshape(values.shape[0], heads, HEAD_SIZE)
    first_half = shaped[..., :half_size]
    second_half = shaped[..., half_size:]
    turned = jnp.concatenate(
        [first_half * cosine - second_half * sine, second_half * cosine + first_half * sine],
        axis=-1,
    )
    return turned.reshape(values.shape[0], heads * HEAD_SIZE)


def rms_parts(values):
    inverse = lax.rsqrt(jnp.mean(values * values, axis=-1, keepdims=True) + norm_eps)
    return (values * inverse, inverse)


def norm_back(grad_in, normed, inverse, gain):
    scaled = grad_in * gain
    grad_values = inverse * (scaled - normed * jnp.mean(scaled * normed, axis=-1, keepdims=True))
    return (grad_values, jnp.sum(grad_in * normed, axis=0))


def left_product(left_side, right_side):
    return lax.dot_general(
        left_side, right_side, (((0,), (0,)), ((), ())), preferred_element_type=jnp.float32
    )


def right_product(left_side, weight):
    return lax.dot_general(
        left_side, weight, (((1,), (1,)), ((), ())), preferred_element_type=jnp.float32
    )


def score_block(query_four, key_rows, query_seg, query_place, key_seg, key_place):
    score_scale = HEAD_SIZE ** (-0.5)
    scores = (
        jnp.einsum("igrd,jgd->grij", query_four, key_rows, preferred_element_type=jnp.float32)
        * score_scale
    )
    allowed = (query_seg[:, None] == key_seg[None, :]) & (
        key_place[None, :] <= query_place[:, None]
    )
    return (jnp.where(allowed[None, None], scores, neg_fill), allowed)


def score_grads(
    query_four,
    grad_four,
    log_sum,
    delta,
    query_seg,
    query_place,
    key_rows,
    value_rows,
    key_seg,
    key_place,
):
    scores, allowed = score_block(query_four, key_rows, query_seg, query_place, key_seg, key_place)
    probs = jnp.where(allowed[None, None], jnp.exp(scores - log_sum[..., None]), 0.0)
    grad_probs = jnp.einsum(
        "igrd,jgd->grij", grad_four, value_rows, preferred_element_type=jnp.float32
    )
    grad_scores = (probs * (grad_probs - delta[..., None])).astype(jnp.bfloat16)
    return (grad_scores, probs.astype(jnp.bfloat16))


def keep_same(running):
    return running


def shards(
    hidden_in,
    out_grad,
    lengths,
    attn_gain,
    w_query,
    key_projection_weight,
    value_projection_weight,
    w_out,
    mlp_gain,
    w_gate,
    w_up,
    w_down,
):
    row_count = hidden_in.shape[0]
    cycle_size = lax.axis_size("blk")
    first_row = lax.axis_index("blk") * row_count
    offsets = jnp.arange(row_count, dtype=jnp.int32)
    places = first_row + offsets
    segment, token_position = doc_places(lengths, places)
    q_heads = w_query.shape[1] // HEAD_SIZE
    kv_heads = key_projection_weight.shape[1] // HEAD_SIZE
    query_group_size = q_heads // kv_heads
    kv_width = kv_heads * HEAD_SIZE
    score_scale = HEAD_SIZE ** (-0.5)
    hidden_f = hidden_in.astype(jnp.float32)
    normed_one, inverse_one = rms_parts(hidden_f)
    first_layer_norm = (normed_one * attn_gain).astype(jnp.bfloat16)
    query_raw = jnp.dot(first_layer_norm, w_query, preferred_element_type=jnp.float32)
    key_raw = jnp.dot(first_layer_norm, key_projection_weight, preferred_element_type=jnp.float32)
    value_raw = jnp.dot(
        first_layer_norm, value_projection_weight, preferred_element_type=jnp.float32
    )
    query_low = apply_rotary(query_raw, token_position, q_heads, 1.0).astype(jnp.bfloat16)
    key_low = apply_rotary(key_raw, token_position, kv_heads, 1.0).astype(jnp.bfloat16)
    value_low = value_raw.astype(jnp.bfloat16)
    kv_rows = jnp.concatenate([key_low, value_low], axis=1)
    query_four = query_low.reshape(row_count, kv_heads, query_group_size, HEAD_SIZE)

    def split_kv(piece, block_step):
        block_rows = lax.dynamic_slice_in_dim(piece, block_step * row_count, row_count, 0)
        key_rows = block_rows[:, :kv_width].reshape(row_count, kv_heads, HEAD_SIZE)
        value_rows = block_rows[:, kv_width:].reshape(row_count, kv_heads, HEAD_SIZE)
        return (key_rows, value_rows)

    start_max = jnp.full((kv_heads, query_group_size, row_count), neg_fill, jnp.float32)
    start_sum = jnp.zeros((kv_heads, query_group_size, row_count), jnp.float32)
    start_acc = jnp.zeros((kv_heads, query_group_size, row_count, HEAD_SIZE), jnp.float32)
    piece = lax.all_gather(kv_rows, "blk", axis=0, tiled=True)

    def forward_one_step(block_step, running):
        key_start = block_step * row_count

        def forward_work(running):
            row_max, row_sum, weighted = running
            key_rows, value_rows = split_kv(piece, block_step)
            key_place = key_start + offsets
            key_seg, _ = doc_places(lengths, key_place)
            scores, allowed = score_block(query_four, key_rows, segment, places, key_seg, key_place)
            new_max = jnp.maximum(row_max, jnp.max(scores, axis=-1))
            exp_scores = jnp.where(allowed[None, None], jnp.exp(scores - new_max[..., None]), 0.0)
            rescale = jnp.exp(row_max - new_max)
            row_sum = row_sum * rescale + jnp.sum(exp_scores, axis=-1)
            weighted = weighted * rescale[..., None] + jnp.einsum(
                "grij,jgd->grid",
                exp_scores.astype(jnp.bfloat16),
                value_rows,
                preferred_element_type=jnp.float32,
            )
            return (new_max, row_sum, weighted)

        return lax.cond(key_start <= first_row, forward_work, keep_same, running)

    row_max, row_sum, weighted = lax.fori_loop(
        0, piece.shape[0] // row_count, forward_one_step, (start_max, start_sum, start_acc)
    )
    attn_four = weighted / row_sum[..., None]
    log_sum = row_max + jnp.log(row_sum)
    attn_rows = jnp.transpose(attn_four, (2, 0, 1, 3)).reshape(row_count, q_heads * HEAD_SIZE)
    attn_low = attn_rows.astype(jnp.bfloat16)
    branch = lax.psum(jnp.dot(attn_low, w_out, preferred_element_type=jnp.float32), "tp")
    middle = hidden_f + branch
    normed_two, inverse_two = rms_parts(middle)
    ln_two = (normed_two * mlp_gain).astype(jnp.bfloat16)
    gate = jnp.dot(ln_two, w_gate, preferred_element_type=jnp.float32)
    up_proj = jnp.dot(ln_two, w_up, preferred_element_type=jnp.float32)
    sig_gate = jax.nn.sigmoid(gate)
    act_gate = gate * sig_gate
    hidden = (act_gate * up_proj).astype(jnp.bfloat16)
    mlp_branch = lax.psum(jnp.dot(hidden, w_down, preferred_element_type=jnp.float32), "tp")
    layer_out = (middle + mlp_branch).astype(jnp.bfloat16)
    grad_down = left_product(hidden, out_grad)
    grad_hidden = right_product(out_grad, w_down)
    grad_gate_act = (grad_hidden * up_proj * sig_gate * (1.0 + gate * (1.0 - sig_gate))).astype(
        jnp.bfloat16
    )
    grad_up_act = (grad_hidden * act_gate).astype(jnp.bfloat16)
    grad_gate = left_product(ln_two, grad_gate_act)
    grad_up = left_product(ln_two, grad_up_act)
    grad_ln_two = lax.psum(
        right_product(grad_gate_act, w_gate) + right_product(grad_up_act, w_up), "tp"
    )
    grad_middle_norm, grad_mlp_gain = norm_back(grad_ln_two, normed_two, inverse_two, mlp_gain)
    grad_middle = out_grad.astype(jnp.float32) + grad_middle_norm
    grad_branch = grad_middle.astype(jnp.bfloat16)
    grad_out = left_product(attn_low, grad_branch)
    grad_attn = right_product(grad_branch, w_out).astype(jnp.bfloat16)
    grad_four = grad_attn.reshape(row_count, kv_heads, query_group_size, HEAD_SIZE)
    delta = jnp.sum(jnp.transpose(grad_four.astype(jnp.float32), (1, 2, 0, 3)) * attn_four, axis=-1)

    def query_grads(grad_scores, key_rows):
        return (
            jnp.einsum("grij,jgd->grid", grad_scores, key_rows, preferred_element_type=jnp.float32)
            * score_scale
        )

    def key_value_grads(grad_scores, probs_low, query_rows, grad_rows):
        grad_keys = (
            jnp.einsum(
                "grij,igrd->jgd", grad_scores, query_rows, preferred_element_type=jnp.float32
            )
            * score_scale
        )
        grad_values = jnp.einsum(
            "grij,igrd->jgd", probs_low, grad_rows, preferred_element_type=jnp.float32
        )
        return jnp.concatenate(
            [grad_keys.reshape(row_count, kv_width), grad_values.reshape(row_count, kv_width)],
            axis=1,
        )

    start_dq = jnp.zeros((kv_heads, query_group_size, row_count, HEAD_SIZE), jnp.float32)
    start_kv = jnp.zeros((row_count * cycle_size, 2 * kv_width), jnp.float32)
    back_piece = lax.all_gather(kv_rows, "blk", axis=0, tiled=True)

    def back_one_step(block_step, running):
        key_start = block_step * row_count

        def back_work(running):
            grad_query_acc, grad_kv_acc = running
            key_rows, value_rows = split_kv(back_piece, block_step)
            key_place = key_start + offsets
            key_seg, _ = doc_places(lengths, key_place)
            grad_scores, probs_low = score_grads(
                query_four,
                grad_four,
                log_sum,
                delta,
                segment,
                places,
                key_rows,
                value_rows,
                key_seg,
                key_place,
            )
            grad_query_acc = grad_query_acc + query_grads(grad_scores, key_rows)
            earlier = lax.dynamic_slice_in_dim(grad_kv_acc, key_start, row_count, 0)
            added = earlier + key_value_grads(grad_scores, probs_low, query_four, grad_four)
            return (
                grad_query_acc,
                lax.dynamic_update_slice_in_dim(grad_kv_acc, added, key_start, 0),
            )

        return lax.cond(key_start <= first_row, back_work, keep_same, running)

    grad_query_four, grad_kv_all = lax.fori_loop(
        0, back_piece.shape[0] // row_count, back_one_step, (start_dq, start_kv)
    )
    grad_kv = lax.psum_scatter(grad_kv_all, "blk", scatter_dimension=0, tiled=True)
    grad_query_rows = jnp.transpose(grad_query_four, (2, 0, 1, 3)).reshape(
        row_count, q_heads * HEAD_SIZE
    )
    grad_query_low = apply_rotary(grad_query_rows, token_position, q_heads, -1.0).astype(
        jnp.bfloat16
    )
    grad_key_low = apply_rotary(grad_kv[:, :kv_width], token_position, kv_heads, -1.0).astype(
        jnp.bfloat16
    )
    grad_value_low = grad_kv[:, kv_width:].astype(jnp.bfloat16)
    grad_query = left_product(first_layer_norm, grad_query_low)
    grad_key = left_product(first_layer_norm, grad_key_low)
    grad_value = left_product(first_layer_norm, grad_value_low)
    grad_ln_part = (
        right_product(grad_query_low, w_query)
        + right_product(grad_key_low, key_projection_weight)
        + right_product(grad_value_low, value_projection_weight)
    )
    grad_ln_one = lax.psum(grad_ln_part, "tp")
    grad_input_norm, grad_attn_gain = norm_back(grad_ln_one, normed_one, inverse_one, attn_gain)
    input_grad = (grad_middle + grad_input_norm).astype(jnp.bfloat16)
    summed = (
        lax.psum_scatter(grad_query, "blk", scatter_dimension=0, tiled=True),
        lax.psum_scatter(grad_key, "blk", scatter_dimension=0, tiled=True),
        lax.psum_scatter(grad_value, "blk", scatter_dimension=0, tiled=True),
        lax.psum_scatter(grad_out, "blk", scatter_dimension=1, tiled=True),
        lax.psum_scatter(grad_gate, "blk", scatter_dimension=0, tiled=True),
        lax.psum_scatter(grad_up, "blk", scatter_dimension=0, tiled=True),
        lax.psum_scatter(grad_down, "blk", scatter_dimension=1, tiled=True),
        lax.psum_scatter(grad_attn_gain, "blk", scatter_dimension=0, tiled=True),
        lax.psum_scatter(grad_mlp_gain, "blk", scatter_dimension=0, tiled=True),
    )
    return (
        layer_out,
        input_grad,
        summed[0],
        summed[1],
        summed[2],
        summed[3],
        summed[4],
        summed[5],
        summed[6],
        summed[7],
        summed[8],
    )


MESH = pl.DeviceIdType.MESH
F32, BF16 = jnp.float32, jnp.bfloat16
LOG2E = 1.4426950408889634
SCORE_SCALE = HEAD_SIZE**-0.5
VMEM_BYTES = 64 * 2**20 - 2**19
HALF = HEAD_SIZE // 2


def dot_nn(a, b):
    return lax.dot_general(a, b, (((1,), (0,)), ((), ())), preferred_element_type=F32)


def dot_nt(a, b):
    return lax.dot_general(a, b, (((1,), (1,)), ((), ())), preferred_element_type=F32)


def dot_tn(a, b):
    return lax.dot_general(a, b, (((0,), (0,)), ((), ())), preferred_element_type=F32)


class Place:
    def __init__(self):
        self.b = lax.axis_index("blk")
        self.t = lax.axis_index("tp")
        self.core = self.b % 2
        self.chip = self.b // 2
        self.x = self.chip % 2
        self.y = self.b // 4
        self.mate = self.b + 1 - 2 * self.core
        self.inner = jnp.logical_or(self.t == 1, self.t == 2)
        self.outer = jnp.logical_not(self.inner)
        self.pair = self.t + 1 - 2 * (self.t % 2)
        self.across = 3 - self.t

    def slot(self, s):
        core = (self.core + s % 2) % 2
        x = (self.x + (s // 2) % 2) % 2
        y = (self.y + s // 4) % 2
        return (y * 2 + x) * 2 + core

    def chip_at(self, k):
        x = (self.x + (k + 1) % 2) % 2
        y = (self.y + 1 - k // 2) % 2
        return y * 2 + x


def remote(src, dst, ssem, rsem, b, t):
    return pltpu.make_async_remote_copy(
        src_ref=src, dst_ref=dst, send_sem=ssem, recv_sem=rsem, device_id=(b, t), device_id_type=MESH
    )


def enter(me, blk_steps):
    barrier = pltpu.get_barrier_semaphore()
    for s in blk_steps:
        pl.semaphore_signal(barrier, inc=1, device_id=(me.slot(s), me.t), device_id_type=MESH)
    for z in (me.pair, me.across):
        pl.semaphore_signal(barrier, inc=1, device_id=(me.b, z), device_id_type=MESH)
    pl.semaphore_wait(barrier, len(blk_steps) + 2)


class LineSum:
    def __init__(self, me, part, first, second, sems, rows):
        self.me, self.part, self.first, self.second, self.sems, self.rows = (
            me, part, first, second, sems, rows,
        )

    def at(self, ref, p):
        return ref.at[pl.ds(pl.multiple_of(p * self.rows, self.rows), self.rows), :]

    def copy(self, stage, p):
        me = self.me
        src = (self.part, self.part, self.first)[stage]
        dst = (self.first, self.second, self.first)[stage]
        target = (me.pair, me.across, me.pair)[stage]
        return remote(
            self.at(src, p), self.at(dst, p),
            self.sems.at[2 * stage, p], self.sems.at[2 * stage + 1, p], me.b, target,
        )

    def give(self, p):
        @pl.when(self.me.outer)
        def _():
            self.copy(0, p).start()

    def fold(self, p):
        @pl.when(self.me.inner)
        def _():
            self.copy(0, p).wait_recv()
            mine, got = self.at(self.part, p), self.at(self.first, p)
            mine[...] = (mine[...].astype(F32) + got[...].astype(F32)).astype(BF16)
            self.copy(1, p).start()

    def unfold(self, p):
        @pl.when(self.me.inner)
        def _():
            self.copy(1, p).wait_recv()
            mine, got, out = self.at(self.part, p), self.at(self.second, p), self.at(self.first, p)
            out[...] = (mine[...].astype(F32) + got[...].astype(F32)).astype(BF16)
            self.copy(2, p).start()

    def take(self, p):
        @pl.when(self.me.outer)
        def _():
            self.copy(2, p).wait_recv()

    def drain_outer(self, pieces):
        @pl.when(self.me.outer)
        def _():
            def one(p, carry):
                self.copy(0, p).wait_send()
                return carry

            lax.fori_loop(0, pieces, one, 0)

    def drain_inner(self, pieces):
        @pl.when(self.me.inner)
        def _():
            def one(p, carry):
                self.copy(1, p).wait_send()
                self.copy(2, p).wait_send()
                return carry

            lax.fori_loop(0, pieces, one, 0)

    def drain(self, pieces):
        self.drain_outer(pieces)
        self.drain_inner(pieces)


class LineGather:
    def __init__(self, me, view, ssem, rsem, last):
        self.me, self.view, self.ssem, self.rsem, self.last = me, view, ssem, rsem, last

    def copy(self, way, hop, p):
        t = self.me.t

        def sent():
            slot = t - (hop - 1) if way == 0 else t + (hop - 1)
            ref = self.view(slot, p)
            target = t + 1 if way == 0 else t - 1
            return remote(ref, ref, self.ssem.at[way, hop - 1, p], self.rsem.at[way, hop - 1, p], self.me.b, target)

        def got():
            slot = t - hop if way == 0 else t + hop
            ref = self.view(slot, p)
            target = t - 1 if way == 0 else t + 1
            return remote(ref, ref, self.ssem.at[way, hop - 1, p], self.rsem.at[way, hop - 1, p], self.me.b, target)

        return sent, got

    def sends(self, way, hop):
        t = self.me.t
        if way == 0:
            return jnp.logical_and(t - (hop - 1) >= 0, t + 1 <= self.last)
        return jnp.logical_and(t + (hop - 1) <= self.last, t >= 1)

    def gets(self, way, hop):
        t = self.me.t
        return t - hop >= 0 if way == 0 else t + hop <= self.last

    def send(self, hop, p):
        for way in (0, 1):

            @pl.when(self.sends(way, hop))
            def _(way=way):
                self.copy(way, hop, p)[0]().start()

    def step(self, hop, p, also=None):
        for way in (0, 1):

            @pl.when(self.gets(way, hop))
            def _(way=way):
                self.copy(way, hop, p)[1]().wait_recv()
                if also is not None:
                    also(way, hop).start()

        if hop < self.last:
            self.send(hop + 1, p)

    def drain(self, p):
        for hop in range(1, self.last + 1):
            for way in (0, 1):

                @pl.when(self.sends(way, hop))
                def _(way=way, hop=hop):
                    self.copy(way, hop, p)[0]().wait_send()


class BlockSum:
    def __init__(self, me, make, outs, held, mates, chips, sems, spare):
        self.me, self.make, self.outs, self.spare = me, make, outs, spare
        self.held, self.mates, self.chips, self.sems = held, mates, chips, sems

    def to_mate(self, k):
        me = self.me
        return remote(
            self.held(k % 2), self.mates(k), self.sems.at[0, k], self.sems.at[1, k], me.mate, me.t
        )

    def to_chip(self, k):
        me = self.me
        return remote(
            self.mates(k), self.chips(k), self.sems.at[2, k], self.sems.at[3, k],
            me.chip_at(k) * 2 + me.core, me.t,
        )

    def lend(self, k):
        me = self.me
        if k >= 2:
            self.to_mate(k - 2).wait_send()
        held = self.held(k % 2)
        even = me.core == 0
        for (lo, hi, value), out, spare in zip(self.make(me.chip_at(k)), self.outs, self.spare):
            half = value.shape[0] // 2
            low, high = value[:half], value[half:]
            held[:, lo:hi] = jnp.where(even, high, low).astype(BF16)
            if k % 2 == 0:
                spare[...] = jnp.where(even, low, high).astype(BF16)
            else:
                out[...] = jnp.where(even, low, high)
        self.to_mate(k).start()

    def merge(self, k, spans):
        self.to_mate(k).wait_recv()
        mates = self.mates(k)
        for (lo, hi), out, spare in zip(spans, self.outs, self.spare):
            own = spare[...].astype(F32) if k % 2 == 0 else out[...]
            total = own + mates[:, lo:hi].astype(F32)
            if k < 3:
                mates[:, lo:hi] = total.astype(BF16)
            else:
                out[...] = total
        if k < 3:
            self.to_chip(k).start()

    def finish(self, spans):
        for k in range(3):
            self.to_chip(k).wait_recv()
            chips = self.chips(k)
            for (lo, hi), out in zip(spans, self.outs):
                out[...] += chips[:, lo:hi].astype(F32)

    def drain(self):
        for k in (2, 3):
            self.to_mate(k).wait_send()
        for k in range(3):
            self.to_chip(k).wait_send()


def norm_rows(values):
    inverse = lax.rsqrt(jnp.mean(values * values, axis=-1, keepdims=True) + norm_eps)
    return values * inverse, inverse


def turn(values, cs_ref, sign):
    cosine, sine = cs_ref[0:HALF, :], cs_ref[HALF:HEAD_SIZE, :] * sign
    pieces = []
    for h in range(values.shape[0] // HEAD_SIZE):
        low = values[h * HEAD_SIZE : h * HEAD_SIZE + HALF]
        high = values[h * HEAD_SIZE + HALF : (h + 1) * HEAD_SIZE]
        pieces.append(low * cosine - high * sine)
        pieces.append(high * cosine + low * sine)
    return jnp.concatenate(pieces, axis=0)


def fill_bias(bias, st_ref, key_start, query_start):
    key_place = lax.broadcasted_iota(jnp.int32, bias.shape, 0) + key_start
    query_place = lax.broadcasted_iota(jnp.int32, bias.shape, 1) + query_start
    allowed = jnp.logical_and(key_place >= st_ref[0:1, :], key_place <= query_place)
    bias[...] = jnp.where(allowed, 0.0, neg_fill)


def heads_of(h, group):
    g = h // group
    return slice(h * HEAD_SIZE, (h + 1) * HEAD_SIZE), slice(g * HEAD_SIZE, (g + 1) * HEAD_SIZE), g


def layer_kernel(
    dims,
    len_ref, ag_ref, mg_ref, hid_hbm, og_hbm, wq_hbm, wk_hbm, wv_hbm, wo_hbm, wg_hbm, wu_hbm, wd_hbm,
    lo_out, ig_out, gq_ref, gk_ref, gv_ref, go_ref, gg_ref, gu_ref, gd_ref, gag_ref, gmg_ref,
    hid, og, wq, wkv, wo, wg, wu, wd, kv, norm, attn, qt, ot, bias, mid, act, dg, du,
    p2, a2, b2, p3, a3, b3, dbr, dot_ref, dq, acc, low_t, dqr, dkvr,
    kv_mates, kv_chips, held_a, held_b, chips_b, held_c, mates_c, chips_c, total_c,
    turns, starts, m_ref, l_ref, lse, delta, gain, gain_in,
    load_sem, kv_sem, wo_sem, wo_plane_sem, wo_mate_sem, at_sem, sem2, sem3, sem4, kvs_sem, rs_sem, gain_sem, out_sem,
    mate_ready, chip_ready,
):
    rows, piece, chunk, share = dims["rows"], dims["piece"], dims["chunk"], dims["share"]
    q_heads, group, kv_width, n_docs = dims["q_heads"], dims["group"], dims["kv_width"], dims["n_docs"]
    n_pieces, n_chunks = rows // piece, rows // chunk
    per = chunk // piece
    width, hidden_units = wg.shape
    q_width = q_heads * HEAD_SIZE
    last = wo.shape[0] - 1
    me = Place()
    scale2 = SCORE_SCALE * LOG2E

    def each(f, lo, hi):
        def one(p, carry):
            f(p)
            return carry

        lax.fori_loop(lo, hi, one, 0)

    barrier = pltpu.get_barrier_semaphore()
    for s in range(1, 8):
        pl.semaphore_signal(barrier, inc=1, device_id=(me.slot(s), me.t), device_id_type=MESH)
    for z in (me.pair, me.across):
        pl.semaphore_signal(barrier, inc=1, device_id=(me.b, z), device_id_type=MESH)
    loads = {}
    for i, (name, source, target) in enumerate((
        ("wo", wo_hbm, wo.at[me.t]), ("hid", hid_hbm, hid), ("wk", wk_hbm, wkv.at[0:kv_width]),
        ("wv", wv_hbm, wkv.at[kv_width : 2 * kv_width]), ("wq", wq_hbm, wq), ("wg", wg_hbm, wg),
        ("wu", wu_hbm, wu), ("og", og_hbm, og), ("wd", wd_hbm, wd),
    )):
        loads[name] = pltpu.make_async_copy(source, target, load_sem.at[i])
    for name in ("wo", "hid", "wk", "wv"):
        loads[name].start()

    attn_gain, mlp_gain = ag_ref[...].reshape(1, width), mg_ref[...].reshape(1, width)

    def chunk_rows(c):
        return pl.ds(pl.multiple_of(c * chunk, chunk), chunk)

    def first_norm(c):
        r = chunk_rows(c)
        normed, _ = norm_rows(hid[r, :].astype(F32))
        norm[r, :] = (normed * attn_gain).astype(BF16)

    part = share // 4
    my_half = pl.ds(pl.multiple_of(me.core * share, share), share)

    def wo_rows(slot, p):
        first = me.core * share + p * 2 * part + (me.x, me.y)[p] * part
        return wo.at[slot, pl.ds(pl.multiple_of(first, part), part), :]

    whole_wo = LineGather(me, wo_rows, wo_sem.at[0], wo_sem.at[1], last)

    def wo_plane(way, hop, p):
        ref = wo_rows(me.t - hop if way == 0 else me.t + hop, p)
        return remote(
            ref, ref, wo_plane_sem.at[0, p, way, hop - 1], wo_plane_sem.at[1, p, way, hop - 1],
            me.slot(2 + 2 * p), me.t,
        )

    def wo_to_mate(way, hop):
        ref = wo.at[me.t - hop if way == 0 else me.t + hop, my_half, :]
        return remote(
            ref, ref, wo_mate_sem.at[0, way, hop - 1], wo_mate_sem.at[1, way, hop - 1], me.mate, me.t
        )

    def each_wo(hops, action):
        for hop in hops:
            for way in (0, 1):

                @pl.when(whole_wo.gets(way, hop))
                def _(way=way, hop=hop):
                    action(way, hop)

    def wo_spread(way, hop):
        for p in (0, 1):
            wo_plane(way, hop, p).start()

    def wo_lend(way, hop):
        for p in (0, 1):
            wo_plane(way, hop, p).wait_recv()
        wo_to_mate(way, hop).start()

    def wo_line(hop):
        for p in (0, 1):
            whole_wo.step(hop, p)

    loads["wq"].start()
    places = me.b * rows + lax.broadcasted_iota(jnp.int32, (1, rows), 1)
    start, end = jnp.zeros((1, rows), jnp.int32), jnp.int32(0)
    for k in range(n_docs):
        end = end + len_ref[k]
        start = jnp.where(places >= end, end, start)
    starts[...] = jnp.broadcast_to(start, starts.shape)
    order = lax.broadcasted_iota(jnp.int32, (HALF, 1), 0).astype(F32)
    freqs = jnp.exp(order * (-2.0 / HEAD_SIZE * math.log(rope_base)))
    angle = freqs * (places - start).astype(F32)
    turns[0:HALF, :] = jnp.cos(angle)
    turns[HALF:HEAD_SIZE, :] = jnp.sin(angle)
    loads["hid"].wait()
    each(first_norm, 0, n_chunks)
    loads["wk"].wait()
    loads["wv"].wait()
    both_t = dot_nt(wkv[...], norm[...])
    kv[me.b, 0:kv_width, :] = turn(both_t[0:kv_width], turns, 1.0).astype(BF16)
    kv[me.b, kv_width : 2 * kv_width, :] = both_t[kv_width : 2 * kv_width].astype(BF16)

    loads["wo"].wait()
    pl.semaphore_wait(barrier, 9)
    for p in (0, 1):
        whole_wo.send(1, p)
    def kv_copy(slot, target, n):
        return remote(kv.at[slot], kv.at[slot], kv_sem.at[0, n], kv_sem.at[1, n], target, me.t)

    def share_kv(s):
        @pl.when(me.slot(s) > me.b)
        def _():
            kv_copy(me.b, me.slot(s), s).start()

    for s in (1, 2, 4):
        share_kv(s)
    for name in ("wg", "wu", "og", "wd"):
        loads[name].start()
    loads["wq"].wait()
    qt[...] = turn(dot_nn(norm[...], wq[...]).T, turns, 1.0).astype(BF16)
    m_ref[...] = jnp.full(m_ref.shape, neg_fill, F32)
    l_ref[...] = jnp.zeros(l_ref.shape, F32)
    ot[...] = jnp.zeros(ot.shape, F32)

    def attend(s, carry):
        slot = me.slot(s)
        arrives = jnp.logical_and(s > 0, slot < me.b)

        @pl.when(arrives)
        def _():
            kv_copy(slot, me.mate, s).wait_recv()

        @pl.when(jnp.logical_and(arrives, s % 2 == 0))
        def _():
            kv_copy(slot, me.mate, s + 1).start()

        for hop, turn_at in ((1, 2), (2, 3), (3, 5)):

            @pl.when(s == turn_at)
            def _(hop=hop):
                wo_line(hop)

        @pl.when(s == 6)
        def _():
            each_wo((1, 2, 3), wo_spread)

        @pl.when(slot <= me.b)
        def _():
            fill_bias(bias, starts, slot * rows, me.b * rows)
            for h in range(q_heads):
                qs, ks, g = heads_of(h, group)
                vs = slice(kv_width + g * HEAD_SIZE, kv_width + (g + 1) * HEAD_SIZE)
                scores = dot_tn(kv[slot, ks, :], qt[qs, :]) + bias[...]
                old = m_ref[h : h + 1, :]
                new = jnp.maximum(old, jnp.max(scores, axis=0, keepdims=True))
                probs = jnp.exp2((scores - new) * scale2)
                keep = jnp.exp2((old - new) * scale2)
                m_ref[h : h + 1, :] = new
                l_ref[h : h + 1, :] = l_ref[h : h + 1, :] * keep + jnp.sum(probs, axis=0, keepdims=True)
                ot[qs, :] = ot[qs, :] * keep + dot_nn(kv[slot, vs, :], probs.astype(BF16))

        @pl.when(s == 1)
        def _():
            share_kv(6)

        return carry

    lax.fori_loop(0, 8, attend, 0)

    line_attn = LineGather(
        me, lambda slot, p: attn.at[slot, chunk_rows(p), :], at_sem.at[0], at_sem.at[1], last
    )
    for h in range(q_heads):
        qs, _, _ = heads_of(h, group)
        ot[qs, :] = ot[qs, :] / l_ref[h : h + 1, :]
    for c in range(n_chunks):
        attn[me.t, c * chunk : (c + 1) * chunk, :] = ot[:, c * chunk : (c + 1) * chunk].T.astype(BF16)
        line_attn.send(1, c)
    lse[...] = jnp.zeros(lse.shape, F32)
    lse[0:q_heads, :] = m_ref[0:q_heads, :] * scale2 + jnp.log2(l_ref[0:q_heads, :])
    for name in ("wg", "wu", "og", "wd"):
        loads[name].wait()
    line_attn.step(1, 0)
    each_wo((1, 2, 3), wo_lend)
    line_attn.step(2, 0)
    line_attn.step(3, 0)
    line_attn.step(1, 1)
    each_wo((1, 2, 3), lambda way, hop: wo_to_mate(way, hop).wait_recv())

    back = LineSum(me, p2, a2, b2, sem2, piece)
    forth_rows = rows // 8
    forth = LineSum(me, p3, a3, b3, sem3, forth_rows)
    forth_pieces = 8
    adds_middle = (me.t == 1).astype(F32)

    def feed(c, carry):
        r = chunk_rows(c)

        for n in range(0, width, 512):
            ns = slice(n, n + 512)
            total = hid[r, ns].astype(F32)
            for z in range(last + 1):
                total = total + dot_nn(attn[z, r, :], wo[z, :, ns])
            mid[r, ns] = total
        normed, _ = norm_rows(mid[r, :])
        norm[r, :] = (normed * mlp_gain).astype(BF16)

        @pl.when(c < n_chunks - 1)
        def _():
            line_attn.step(2, c + 1)

        for n in range(0, hidden_units, 512):
            ns = slice(n, n + 512)
            gate = dot_nn(norm[r, :], wg[:, ns])
            up = dot_nn(norm[r, :], wu[:, ns])
            grad = dot_nt(og[r, :], wd[ns, :])
            sig = 1.0 / (1.0 + jnp.exp(-gate))
            silu = gate * sig
            act[r, ns] = (silu * up).astype(BF16)
            dg[r, ns] = (grad * up * sig * (1.0 + gate * (1.0 - sig))).astype(BF16)
            du[r, ns] = (grad * silu).astype(BF16)
            if n == 0:

                @pl.when(c < n_chunks - 2)
                def _():
                    line_attn.step(1, c + 2)

        for n in range(0, width, 512):
            ns = slice(n, n + 512)
            p2[r, ns] = (dot_nt(dg[r, :], wg[ns, :]) + dot_nt(du[r, :], wu[ns, :])).astype(BF16)
        each(back.give, c * per, (c + 1) * per)

        @pl.when(c < n_chunks - 1)
        def _():
            line_attn.step(3, c + 1)

        @pl.when(c >= 2)
        def _():
            each(back.fold, (c - 2) * per, (c - 1) * per)

        @pl.when(c >= 3)
        def _():
            each(back.unfold, (c - 3) * per, (c - 2) * per)

        for n in range(0, width, 512):
            ns = slice(n, n + 512)
            p3[r, ns] = (dot_nn(act[r, :], wd[:, ns]) + mid[r, ns] * adds_middle).astype(BF16)
        return carry

    lax.fori_loop(0, n_chunks, feed, 0)
    pl.semaphore_signal(mate_ready, inc=1, device_id=(me.mate, me.t), device_id_type=MESH)
    for k in range(3):
        pl.semaphore_signal(
            chip_ready, inc=1, device_id=(me.chip_at(k) * 2 + me.core, me.t), device_id_type=MESH
        )
    pair = 2 * share

    def pair_columns(ref, chip):
        return ref[:, pl.ds(pl.multiple_of(chip * pair, pair), pair)]

    def slots(ref, first, columns):
        return lambda k: ref.at[(first + k) * share : (first + k + 1) * share, 0:columns]

    sum_gate = BlockSum(
        me, lambda m: [(0, hidden_units, dot_tn(pair_columns(norm, m), dg[...]))], [gg_ref],
        lambda k: held_a.at[0, k], slots(wg, 0, hidden_units), slots(wg, 4, hidden_units), rs_sem.at[0],
        [slots(wg, 7, hidden_units)(0)],
    )
    sum_up = BlockSum(
        me, lambda m: [(0, hidden_units, dot_tn(pair_columns(norm, m), du[...]))], [gu_ref],
        lambda k: held_a.at[1, k], slots(wu, 0, hidden_units), slots(wu, 4, hidden_units), rs_sem.at[1],
        [slots(wu, 7, hidden_units)(0)],
    )
    span_a = [(0, hidden_units)]
    pl.semaphore_wait(mate_ready, 1)
    gain[...] = jnp.zeros(gain.shape, F32)

    def middle_grad(c):
        each(back.take, c * per, (c + 1) * per)
        r = chunk_rows(c)
        normed, inverse = norm_rows(mid[r, :])
        grad = a2[r, :].astype(F32)
        scaled = grad * mlp_gain
        gain[1:2, :] += jnp.sum(grad * normed, axis=0, keepdims=True)
        found = og[r, :].astype(F32) + inverse * (
            scaled - normed * jnp.mean(scaled * normed, axis=-1, keepdims=True)
        )
        mid[r, :] = found
        dbr[r, :] = found.astype(BF16)

    def fold_on(lo, hi):
        def one(p, carry):
            back.fold(p)
            back.unfold(p - per)
            return carry

        lax.fori_loop(lo, hi, one, 0)

    def lend_both(k):
        sum_gate.lend(k)
        sum_up.lend(k)

    def merge_both(k):
        sum_gate.merge(k, span_a)
        sum_up.merge(k, span_a)

    lend_both(0)
    fold_on((n_chunks - 2) * per, (n_chunks - 2) * per + per // 2)
    lend_both(1)
    back.drain_outer(n_pieces)
    each(forth.give, 0, forth_pieces)
    fold_on((n_chunks - 2) * per + per // 2, (n_chunks - 1) * per)
    pl.semaphore_wait(chip_ready, 3)
    merge_both(0)
    fold_on((n_chunks - 1) * per, n_pieces - per // 2)
    lend_both(2)
    merge_both(1)
    fold_on(n_pieces - per // 2, n_pieces)
    merge_both(2)
    each(back.unfold, n_pieces - per, n_pieces)
    each(middle_grad, 0, n_chunks - 1)
    each(middle_grad, n_chunks - 1, n_chunks)
    dot_ref[...] = dot_nt(wo[me.t], dbr[...]).astype(BF16)
    delta[...] = jnp.zeros(delta.shape, F32)
    for h in range(q_heads):
        qs, _, _ = heads_of(h, group)
        delta[h : h + 1, :] = jnp.sum(dot_ref[qs, :].astype(F32) * ot[qs, :], axis=0, keepdims=True)
    dq[...] = jnp.zeros(dq.shape, F32)
    back.drain_inner(n_pieces)
    ahead = 3
    each(forth.fold, 0, ahead)

    for s in (1, 2, 4, 6):

        @pl.when(me.slot(s) > me.b)
        def _(s=s):
            kv_copy(me.b, me.slot(s), s).wait_send()

    for s in (2, 4, 6):

        @pl.when(me.slot(s) < me.b)
        def _(s=s):
            kv_copy(me.slot(s), me.mate, s + 1).wait_send()

    def kv_to_mate(k):
        return remote(
            kv.at[me.chip_at(k) * 2 + 1 - me.core], kv_mates.at[k], kvs_sem.at[0, k], kvs_sem.at[1, k],
            me.mate, me.t,
        )

    def kv_to_chip(k):
        return remote(
            kv_mates.at[k], kv_chips.at[k], kvs_sem.at[2, k], kvs_sem.at[3, k],
            me.chip_at(k) * 2 + me.core, me.t,
        )

    def attend_back(u, carry):
        k, own = u // 2, u % 2
        chip = me.chip_at(k)
        slot = chip * 2 + (me.core + 1 - own) % 2

        @pl.when(u + ahead < forth_pieces)
        def _():
            forth.fold(u + ahead)

        @pl.when(u >= 2)
        def _():
            forth.unfold(u - 2)

        @pl.when(slot <= me.b)
        def _():
            fill_bias(bias, starts, slot * rows, me.b * rows)
            for g in range(q_heads // group):
                ks = slice(g * HEAD_SIZE, (g + 1) * HEAD_SIZE)
                vs = slice(kv_width + g * HEAD_SIZE, kv_width + (g + 1) * HEAD_SIZE)
                key_t, value_t = kv[slot, ks, :], kv[slot, vs, :]
                grad_k = grad_v = None
                for h in range(g * group, (g + 1) * group):
                    qs, _, _ = heads_of(h, group)
                    query_t, grad_t = qt[qs, :], dot_ref[qs, :]
                    scores = dot_tn(key_t, query_t) + bias[...]
                    probs = jnp.exp2(scores * scale2 - lse[h : h + 1, :])
                    grad_p = dot_tn(value_t, grad_t)
                    grad_s = (probs * (grad_p - delta[h : h + 1, :])).astype(BF16)
                    one_v = dot_nt(grad_t, probs.astype(BF16))
                    one_k = dot_nt(query_t, grad_s)
                    grad_v = one_v if grad_v is None else grad_v + one_v
                    grad_k = one_k if grad_k is None else grad_k + one_k
                    dq[qs, :] += dot_nn(key_t, grad_s)
                acc[ks, :] = grad_k
                acc[vs, :] = grad_v

        @pl.when(jnp.logical_and(own == 0, slot <= me.b))
        def _():
            kv[slot] = acc[...].astype(BF16)
            kv_to_mate(k).start()

        @pl.when(jnp.logical_and(own == 1, chip < me.chip))
        def _():
            kv_to_mate(k).wait_recv()
            kv_mates[k] = (acc[...] + kv_mates[k].astype(F32)).astype(BF16)
            kv_to_chip(k).start()

        return carry

    lax.fori_loop(0, 8, attend_back, 0)
    low_t[0:q_width, :] = turn(dq[...] * SCORE_SCALE, turns, -1.0).astype(BF16)
    dqr[...] = low_t[0:q_width, :].T

    def first_norm_again(c):
        r = chunk_rows(c)
        normed, _ = norm_rows(hid[r, :].astype(F32))
        norm[r, :] = (normed * attn_gain).astype(BF16)


    @pl.when(me.core == 0)
    def _():
        kv_to_mate(3).wait_recv()
        acc[...] += kv_mates[3].astype(F32)

    for k in range(3):

        @pl.when(me.chip_at(k) > me.chip)
        def _(k=k):
            kv_to_chip(k).wait_recv()
            acc[...] += kv_chips[k].astype(F32)

    low_t[q_width : q_width + kv_width, :] = turn(acc[0:kv_width, :] * SCORE_SCALE, turns, -1.0).astype(BF16)
    low_t[q_width + kv_width :, :] = acc[kv_width : 2 * kv_width, :].astype(BF16)
    dkvr[...] = low_t[q_width:, :].T

    each(forth.take, 0, 2)
    end_sum = LineSum(me, p2, a2, b2, sem4, piece)

    def input_part(c):
        r = chunk_rows(c)
        for n in range(0, width, 512):
            ns = slice(n, n + 512)
            p2[r, ns] = (dot_nt(dqr[r, :], wq[ns, :]) + dot_nn(dkvr[r, :], wkv[:, ns])).astype(BF16)
        each(end_sum.give, c * per, (c + 1) * per)

    each(input_part, 0, n_chunks)
    each(forth.unfold, forth_pieces - 2, forth_pieces)

    def make_b(m):
        yield 0, hidden_units, dot_tn(pair_columns(og, m), act[...])
        yield hidden_units, hidden_units + q_width, dot_tn(pair_columns(dbr, m), attn[me.t])

    def make_c(m):
        columns = pair_columns(norm, m)
        yield 0, q_width, dot_tn(columns, dqr[...])
        yield q_width, q_width + 2 * kv_width, dot_tn(columns, dkvr[...])

    width_b = hidden_units + q_width
    in_wd = slots(wd, 0, width_b)
    sum_b = BlockSum(
        me, make_b, [gd_ref, go_ref], lambda k: held_b.at[k], in_wd,
        lambda k: in_wd(4) if k == 0 else chips_b.at[k - 1], rs_sem.at[2],
        [dg.at[0:share, :], du.at[0:share, 0:q_width]],
    )
    span_b = [(0, hidden_units), (hidden_units, width_b)]
    total_parts = [total_c.at[:, 0:q_width], total_c.at[:, q_width : q_width + 2 * kv_width]]
    sum_c = BlockSum(
        me, make_c, total_parts, lambda k: held_c.at[k], lambda k: mates_c.at[k], lambda k: chips_c.at[k],
        rs_sem.at[3],
        [dg.at[share : 2 * share, 0:q_width], du.at[share : 2 * share, 0 : 2 * kv_width]],
    )
    span_c = [(0, q_width), (q_width, q_width + 2 * kv_width)]
    work = [(functools.partial(lend_both, 3), functools.partial(merge_both, 3))]
    for sums, spans in ((sum_b, span_b), (sum_c, span_c)):
        for k in range(4):
            work.append((functools.partial(sums.lend, k), functools.partial(sums.merge, k, spans)))
    done, late = 0, None
    for i, (lend, merge) in enumerate(work):
        if i == 1:
            each(first_norm_again, 0, n_chunks)
        lend()
        upto = n_pieces * (i + 1) // len(work)
        for p in range(done, upto):
            end_sum.fold(p)
            if p >= 1:
                end_sum.unfold(p - 1)
        done = upto
        if late is not None:
            late()
        late = merge
    end_sum.unfold(n_pieces - 1)
    late()

    each(forth.take, 2, forth_pieces)
    lo_save = pltpu.make_async_copy(a3, lo_out, out_sem.at[0])
    lo_save.start()

    def input_rows(c):
        each(end_sum.take, c * per, (c + 1) * per)
        r = chunk_rows(c)
        normed, inverse = norm_rows(hid[r, :].astype(F32))
        grad = a2[r, :].astype(F32)
        scaled = grad * attn_gain
        gain[0:1, :] += jnp.sum(grad * normed, axis=0, keepdims=True)
        found = inverse * (scaled - normed * jnp.mean(scaled * normed, axis=-1, keepdims=True))
        dbr[r, :] = (mid[r, :] + found).astype(BF16)

    each(input_rows, 0, n_chunks)

    def gain_copy(s):
        return remote(gain, gain_in.at[s], gain_sem.at[0, s], gain_sem.at[1, s], me.slot(s), me.t)

    for s in range(1, 8):
        gain_copy(s).start()
    ig_save = pltpu.make_async_copy(dbr, ig_out, out_sem.at[1])
    ig_save.start()
    sum_gate.finish(span_a)
    sum_up.finish(span_a)
    sum_b.finish(span_b)
    sum_c.finish(span_c)
    gq_ref[...] = total_c[:, 0:q_width]
    gk_ref[...] = total_c[:, q_width : q_width + kv_width]
    gv_ref[...] = total_c[:, q_width + kv_width : q_width + 2 * kv_width]
    for s in range(1, 8):
        gain_copy(s).wait_recv()
    gains = gain[...]
    for s in range(1, 8):
        gains = gains + gain_in[s]
    gain_in[0] = gains
    mine = jnp.zeros((8, share), F32)
    for j in range(8):
        mine = mine + jnp.where(me.b == j, gain_in[0, :, j * share : (j + 1) * share], 0.0)
    gag_ref[...] = mine[0, :]
    gmg_ref[...] = mine[1, :]

    for s in range(1, 8):
        gain_copy(s).wait_send()
    for p in (0, 1):
        whole_wo.drain(p)

    def wo_done(way, hop):
        for p in (0, 1):
            wo_plane(way, hop, p).wait_send()
        wo_to_mate(way, hop).wait_send()

    each_wo((1, 2, 3), wo_done)
    each(line_attn.drain, 0, n_chunks)
    forth.drain(forth_pieces)
    end_sum.drain(n_pieces)
    for sums in (sum_gate, sum_up, sum_b, sum_c):
        sums.drain()
    for k in range(4):
        chip = me.chip_at(k)
        slot = chip * 2 + 1 - me.core

        @pl.when(slot <= me.b)
        def _(k=k):
            kv_to_mate(k).wait_send()

        if k < 3:

            @pl.when(chip < me.chip)
            def _(k=k):
                kv_to_chip(k).wait_send()

    lo_save.wait()
    ig_save.wait()


def hand_over(n, *refs):
    sources, targets, held, sems = refs[:n], refs[n : 2 * n], refs[2 * n : 3 * n], refs[3 * n]
    ins = [pltpu.make_async_copy(a, h, sems.at[0, i]) for i, (a, h) in enumerate(zip(sources, held))]
    outs = [pltpu.make_async_copy(h, b, sems.at[1, i]) for i, (h, b) in enumerate(zip(held, targets))]
    for copy in ins:
        copy.start()
    for first, second in zip(ins, outs):
        first.wait()
        second.start()
    for copy in outs:
        copy.wait()


def kernel_shards(
    hidden_in, out_grad, lengths, attn_gain, w_query, key_projection_weight, value_projection_weight,
    w_out, mlp_gain, w_gate, w_up, w_down,
):
    rows, width = hidden_in.shape
    q_width, kv_width = w_query.shape[1], key_projection_weight.shape[1]
    hidden_units = w_gate.shape[1]
    blocks, line_size = lax.axis_size("blk"), lax.axis_size("tp")
    share = width // blocks
    piece, chunk = rows // 8, rows // 4
    pieces, chunks = rows // piece, rows // chunk
    dims = dict(
        rows=rows, piece=piece, chunk=chunk, share=share, q_heads=q_width // HEAD_SIZE,
        group=q_width // kv_width, kv_width=kv_width, n_docs=lengths.shape[0],
    )
    vmem, hbm = pl.BlockSpec(memory_space=pltpu.VMEM), pl.BlockSpec(memory_space=pl.ANY)
    smem = pl.BlockSpec(memory_space=pltpu.SMEM)
    dma, regular = pltpu.SemaphoreType.DMA, pltpu.SemaphoreType.REGULAR

    def shape(dtype, *dims_):
        return jax.ShapeDtypeStruct(dims_, dtype)

    def low(*dims_):
        return pltpu.VMEM(dims_, BF16)

    def full(*dims_):
        return pltpu.VMEM(dims_, F32)

    line = [low(rows, width)] * 3
    width_b, width_c = hidden_units + q_width, q_width + 2 * kv_width
    shapes = (
        shape(BF16, rows, width), shape(BF16, rows, width), shape(F32, share, q_width),
        shape(F32, share, kv_width), shape(F32, share, kv_width), shape(F32, share, q_width),
        shape(F32, share, hidden_units), shape(F32, share, hidden_units), shape(F32, share, hidden_units),
        shape(F32, share), shape(F32, share),
    )
    outs = pl.pallas_call(
        functools.partial(layer_kernel, dims),
        out_shape=shapes,
        in_specs=[smem, vmem, vmem] + [hbm] * 9,
        out_specs=(hbm, hbm) + (vmem,) * 9,
        scratch_shapes=[
            low(rows, width), low(rows, width), low(width, q_width), low(2 * kv_width, width),
            low(line_size, q_width, width), low(width, hidden_units), low(width, hidden_units),
            low(hidden_units, width), low(blocks, 2 * kv_width, rows), low(rows, width),
            low(line_size, rows, q_width), low(q_width, rows), full(q_width, rows), full(rows, rows),
            full(rows, width), low(rows, hidden_units), low(rows, hidden_units), low(rows, hidden_units),
            *line, *line, low(rows, width), low(q_width, rows), full(q_width, rows), full(2 * kv_width, rows),
            low(width_c, rows), low(rows, q_width), low(rows, 2 * kv_width),
            low(4, 2 * kv_width, rows), low(3, 2 * kv_width, rows),
            low(2, 2, share, hidden_units), low(2, share, width_b), low(2, share, width_b),
            low(2, share, width_c), low(4, share, width_c), low(3, share, width_c), full(share, width_c),
            full(HEAD_SIZE, rows), pltpu.VMEM((8, rows), jnp.int32), full(8, rows), full(8, rows), full(8, rows),
            full(8, rows), full(8, width), full(8, 8, width),
            dma((9,)), dma((2, 8)), dma((2, 2, line_size - 1, 2)), dma((2, 2, 2, line_size - 1)),
            dma((2, 2, line_size - 1)),
            dma((2, 2, line_size - 1, chunks)), dma((6, pieces)), dma((6, pieces)), dma((6, pieces)),
            dma((4, 4)), dma((4, 4, 4)), dma((2, 8)), dma((2,)), regular, regular,
        ],
        compiler_params=pltpu.CompilerParams(
            collective_id=0, has_side_effects=True, vmem_limit_bytes=VMEM_BYTES
        ),
    )(
        lengths, attn_gain, mlp_gain, hidden_in, out_grad, w_query, key_projection_weight.T,
        value_projection_weight.T, w_out, w_gate, w_up, w_down,
    )
    outs = pl.pallas_call(
        functools.partial(hand_over, len(shapes)),
        out_shape=shapes,
        in_specs=[hbm] * len(shapes),
        out_specs=(hbm,) * len(shapes),
        scratch_shapes=[pltpu.VMEM(s.shape, s.dtype) for s in shapes] + [dma((2, len(shapes)))],
    )(*outs)
    layer_out, input_grad, grad_query, grad_key, grad_value, grad_out, grad_gate, grad_up, grad_down, g1, g2 = outs
    return (
        layer_out, input_grad, grad_query, grad_key, grad_value, grad_out.T, grad_gate, grad_up, grad_down.T, g1, g2,
    )


def solution(mesh):
    sizes = dict(mesh.shape)
    small = sizes["blk"] == 8 and sizes["tp"] == 4
    placed = (
        P("blk", None),
        P("blk", None),
        P(),
        P(),
        P(None, "tp"),
        P(None, "tp"),
        P(None, "tp"),
        P("tp", None),
        P(),
        P(None, "tp"),
        P(None, "tp"),
        P("tp", None),
    )
    return jax.shard_map(
        kernel_shards if small else shards,
        mesh=mesh,
        in_specs=placed,
        out_specs=(
            P("blk", None),
            P("blk", None),
            P("blk", "tp"),
            P("blk", "tp"),
            P("blk", "tp"),
            P("tp", "blk"),
            P("blk", "tp"),
            P("blk", "tp"),
            P("tp", "blk"),
            P("blk"),
            P("blk"),
        ),
        check_vma=False,
    )
```

```python
import functools
import math

import jax
import jax.numpy as jnp
from jax import lax
from jax.experimental import pallas as pl
from jax.experimental.pallas import tpu as pltpu
from jax.sharding import PartitionSpec as P

HEAD_SIZE = 96


norm_eps = 1e-05
rope_base = 100000.0
neg_fill = -1e30


def doc_places(lengths, places):
    doc_ends = jnp.cumsum(lengths)
    passed = (places[:, None] >= doc_ends[None, :]).astype(jnp.int32)
    segment = jnp.sum(passed, axis=1)
    preceding = jnp.sum(passed * lengths[None, :], axis=1)
    return (segment, places - preceding)


def apply_rotary(values, token_position, heads, sign_value):
    half_size = HEAD_SIZE // 2
    freqs = rope_base ** (-(2.0 * jnp.arange(half_size, dtype=jnp.float32)) / HEAD_SIZE)
    angle = token_position.astype(jnp.float32)[:, None] * freqs[None, :]
    cosine = jnp.cos(angle)[:, None, :]
    sine = sign_value * jnp.sin(angle)[:, None, :]
    shaped = values.reshape(values.shape[0], heads, HEAD_SIZE)
    first_half = shaped[..., :half_size]
    second_half = shaped[..., half_size:]
    turned = jnp.concatenate(
        [first_half * cosine - second_half * sine, second_half * cosine + first_half * sine],
        axis=-1,
    )
    return turned.reshape(values.shape[0], heads * HEAD_SIZE)


def rms_parts(values):
    inverse = lax.rsqrt(jnp.mean(values * values, axis=-1, keepdims=True) + norm_eps)
    return (values * inverse, inverse)


def norm_back(grad_in, normed, inverse, gain):
    scaled = grad_in * gain
    grad_values = inverse * (scaled - normed * jnp.mean(scaled * normed, axis=-1, keepdims=True))
    return (grad_values, jnp.sum(grad_in * normed, axis=0))


def left_product(left_side, right_side):
    return lax.dot_general(
        left_side, right_side, (((0,), (0,)), ((), ())), preferred_element_type=jnp.float32
    )


def right_product(left_side, weight):
    return lax.dot_general(
        left_side, weight, (((1,), (1,)), ((), ())), preferred_element_type=jnp.float32
    )


def score_block(query_four, key_rows, query_seg, query_place, key_seg, key_place):
    score_scale = HEAD_SIZE ** (-0.5)
    scores = (
        jnp.einsum("igrd,jgd->grij", query_four, key_rows, preferred_element_type=jnp.float32)
        * score_scale
    )
    allowed = (query_seg[:, None] == key_seg[None, :]) & (
        key_place[None, :] <= query_place[:, None]
    )
    return (jnp.where(allowed[None, None], scores, neg_fill), allowed)


def score_grads(
    query_four,
    grad_four,
    log_sum,
    delta,
    query_seg,
    query_place,
    key_rows,
    value_rows,
    key_seg,
    key_place,
):
    scores, allowed = score_block(query_four, key_rows, query_seg, query_place, key_seg, key_place)
    probs = jnp.where(allowed[None, None], jnp.exp(scores - log_sum[..., None]), 0.0)
    grad_probs = jnp.einsum(
        "igrd,jgd->grij", grad_four, value_rows, preferred_element_type=jnp.float32
    )
    grad_scores = (probs * (grad_probs - delta[..., None])).astype(jnp.bfloat16)
    return (grad_scores, probs.astype(jnp.bfloat16))


def keep_same(running):
    return running


def shards(
    hidden_in,
    out_grad,
    lengths,
    attn_gain,
    w_query,
    key_projection_weight,
    value_projection_weight,
    w_out,
    mlp_gain,
    w_gate,
    w_up,
    w_down,
):
    row_count = hidden_in.shape[0]
    cycle_size = lax.axis_size("blk")
    first_row = lax.axis_index("blk") * row_count
    offsets = jnp.arange(row_count, dtype=jnp.int32)
    places = first_row + offsets
    segment, token_position = doc_places(lengths, places)
    q_heads = w_query.shape[1] // HEAD_SIZE
    kv_heads = key_projection_weight.shape[1] // HEAD_SIZE
    query_group_size = q_heads // kv_heads
    kv_width = kv_heads * HEAD_SIZE
    score_scale = HEAD_SIZE ** (-0.5)
    hidden_f = hidden_in.astype(jnp.float32)
    normed_one, inverse_one = rms_parts(hidden_f)
    first_layer_norm = (normed_one * attn_gain).astype(jnp.bfloat16)
    query_raw = jnp.dot(first_layer_norm, w_query, preferred_element_type=jnp.float32)
    key_raw = jnp.dot(first_layer_norm, key_projection_weight, preferred_element_type=jnp.float32)
    value_raw = jnp.dot(
        first_layer_norm, value_projection_weight, preferred_element_type=jnp.float32
    )
    query_low = apply_rotary(query_raw, token_position, q_heads, 1.0).astype(jnp.bfloat16)
    key_low = apply_rotary(key_raw, token_position, kv_heads, 1.0).astype(jnp.bfloat16)
    value_low = value_raw.astype(jnp.bfloat16)
    kv_rows = jnp.concatenate([key_low, value_low], axis=1)
    query_four = query_low.reshape(row_count, kv_heads, query_group_size, HEAD_SIZE)

    def split_kv(piece, block_step):
        block_rows = lax.dynamic_slice_in_dim(piece, block_step * row_count, row_count, 0)
        key_rows = block_rows[:, :kv_width].reshape(row_count, kv_heads, HEAD_SIZE)
        value_rows = block_rows[:, kv_width:].reshape(row_count, kv_heads, HEAD_SIZE)
        return (key_rows, value_rows)

    start_max = jnp.full((kv_heads, query_group_size, row_count), neg_fill, jnp.float32)
    start_sum = jnp.zeros((kv_heads, query_group_size, row_count), jnp.float32)
    start_acc = jnp.zeros((kv_heads, query_group_size, row_count, HEAD_SIZE), jnp.float32)
    piece = lax.all_gather(kv_rows, "blk", axis=0, tiled=True)

    def forward_one_step(block_step, running):
        key_start = block_step * row_count

        def forward_work(running):
            row_max, row_sum, weighted = running
            key_rows, value_rows = split_kv(piece, block_step)
            key_place = key_start + offsets
            key_seg, _ = doc_places(lengths, key_place)
            scores, allowed = score_block(query_four, key_rows, segment, places, key_seg, key_place)
            new_max = jnp.maximum(row_max, jnp.max(scores, axis=-1))
            exp_scores = jnp.where(allowed[None, None], jnp.exp(scores - new_max[..., None]), 0.0)
            rescale = jnp.exp(row_max - new_max)
            row_sum = row_sum * rescale + jnp.sum(exp_scores, axis=-1)
            weighted = weighted * rescale[..., None] + jnp.einsum(
                "grij,jgd->grid",
                exp_scores.astype(jnp.bfloat16),
                value_rows,
                preferred_element_type=jnp.float32,
            )
            return (new_max, row_sum, weighted)

        return lax.cond(key_start <= first_row, forward_work, keep_same, running)

    row_max, row_sum, weighted = lax.fori_loop(
        0, piece.shape[0] // row_count, forward_one_step, (start_max, start_sum, start_acc)
    )
    attn_four = weighted / row_sum[..., None]
    log_sum = row_max + jnp.log(row_sum)
    attn_rows = jnp.transpose(attn_four, (2, 0, 1, 3)).reshape(row_count, q_heads * HEAD_SIZE)
    attn_low = attn_rows.astype(jnp.bfloat16)
    branch = lax.psum(jnp.dot(attn_low, w_out, preferred_element_type=jnp.float32), "tp")
    middle = hidden_f + branch
    normed_two, inverse_two = rms_parts(middle)
    ln_two = (normed_two * mlp_gain).astype(jnp.bfloat16)
    gate = jnp.dot(ln_two, w_gate, preferred_element_type=jnp.float32)
    up_proj = jnp.dot(ln_two, w_up, preferred_element_type=jnp.float32)
    sig_gate = jax.nn.sigmoid(gate)
    act_gate = gate * sig_gate
    hidden = (act_gate * up_proj).astype(jnp.bfloat16)
    mlp_branch = lax.psum(jnp.dot(hidden, w_down, preferred_element_type=jnp.float32), "tp")
    layer_out = (middle + mlp_branch).astype(jnp.bfloat16)
    grad_down = left_product(hidden, out_grad)
    grad_hidden = right_product(out_grad, w_down)
    grad_gate_act = (grad_hidden * up_proj * sig_gate * (1.0 + gate * (1.0 - sig_gate))).astype(
        jnp.bfloat16
    )
    grad_up_act = (grad_hidden * act_gate).astype(jnp.bfloat16)
    grad_gate = left_product(ln_two, grad_gate_act)
    grad_up = left_product(ln_two, grad_up_act)
    grad_ln_two = lax.psum(
        right_product(grad_gate_act, w_gate) + right_product(grad_up_act, w_up), "tp"
    )
    grad_middle_norm, grad_mlp_gain = norm_back(grad_ln_two, normed_two, inverse_two, mlp_gain)
    grad_middle = out_grad.astype(jnp.float32) + grad_middle_norm
    grad_branch = grad_middle.astype(jnp.bfloat16)
    grad_out = left_product(attn_low, grad_branch)
    grad_attn = right_product(grad_branch, w_out).astype(jnp.bfloat16)
    grad_four = grad_attn.reshape(row_count, kv_heads, query_group_size, HEAD_SIZE)
    delta = jnp.sum(jnp.transpose(grad_four.astype(jnp.float32), (1, 2, 0, 3)) * attn_four, axis=-1)

    def query_grads(grad_scores, key_rows):
        return (
            jnp.einsum("grij,jgd->grid", grad_scores, key_rows, preferred_element_type=jnp.float32)
            * score_scale
        )

    def key_value_grads(grad_scores, probs_low, query_rows, grad_rows):
        grad_keys = (
            jnp.einsum(
                "grij,igrd->jgd", grad_scores, query_rows, preferred_element_type=jnp.float32
            )
            * score_scale
        )
        grad_values = jnp.einsum(
            "grij,igrd->jgd", probs_low, grad_rows, preferred_element_type=jnp.float32
        )
        return jnp.concatenate(
            [grad_keys.reshape(row_count, kv_width), grad_values.reshape(row_count, kv_width)],
            axis=1,
        )

    start_dq = jnp.zeros((kv_heads, query_group_size, row_count, HEAD_SIZE), jnp.float32)
    start_kv = jnp.zeros((row_count * cycle_size, 2 * kv_width), jnp.float32)
    back_piece = lax.all_gather(kv_rows, "blk", axis=0, tiled=True)

    def back_one_step(block_step, running):
        key_start = block_step * row_count

        def back_work(running):
            grad_query_acc, grad_kv_acc = running
            key_rows, value_rows = split_kv(back_piece, block_step)
            key_place = key_start + offsets
            key_seg, _ = doc_places(lengths, key_place)
            grad_scores, probs_low = score_grads(
                query_four,
                grad_four,
                log_sum,
                delta,
                segment,
                places,
                key_rows,
                value_rows,
                key_seg,
                key_place,
            )
            grad_query_acc = grad_query_acc + query_grads(grad_scores, key_rows)
            earlier = lax.dynamic_slice_in_dim(grad_kv_acc, key_start, row_count, 0)
            added = earlier + key_value_grads(grad_scores, probs_low, query_four, grad_four)
            return (
                grad_query_acc,
                lax.dynamic_update_slice_in_dim(grad_kv_acc, added, key_start, 0),
            )

        return lax.cond(key_start <= first_row, back_work, keep_same, running)

    grad_query_four, grad_kv_all = lax.fori_loop(
        0, back_piece.shape[0] // row_count, back_one_step, (start_dq, start_kv)
    )
    grad_kv = lax.psum_scatter(grad_kv_all, "blk", scatter_dimension=0, tiled=True)
    grad_query_rows = jnp.transpose(grad_query_four, (2, 0, 1, 3)).reshape(
        row_count, q_heads * HEAD_SIZE
    )
    grad_query_low = apply_rotary(grad_query_rows, token_position, q_heads, -1.0).astype(
        jnp.bfloat16
    )
    grad_key_low = apply_rotary(grad_kv[:, :kv_width], token_position, kv_heads, -1.0).astype(
        jnp.bfloat16
    )
    grad_value_low = grad_kv[:, kv_width:].astype(jnp.bfloat16)
    grad_query = left_product(first_layer_norm, grad_query_low)
    grad_key = left_product(first_layer_norm, grad_key_low)
    grad_value = left_product(first_layer_norm, grad_value_low)
    grad_ln_part = (
        right_product(grad_query_low, w_query)
        + right_product(grad_key_low, key_projection_weight)
        + right_product(grad_value_low, value_projection_weight)
    )
    grad_ln_one = lax.psum(grad_ln_part, "tp")
    grad_input_norm, grad_attn_gain = norm_back(grad_ln_one, normed_one, inverse_one, attn_gain)
    input_grad = (grad_middle + grad_input_norm).astype(jnp.bfloat16)
    summed = (
        lax.psum_scatter(grad_query, "blk", scatter_dimension=0, tiled=True),
        lax.psum_scatter(grad_key, "blk", scatter_dimension=0, tiled=True),
        lax.psum_scatter(grad_value, "blk", scatter_dimension=0, tiled=True),
        lax.psum_scatter(grad_out, "blk", scatter_dimension=1, tiled=True),
        lax.psum_scatter(grad_gate, "blk", scatter_dimension=0, tiled=True),
        lax.psum_scatter(grad_up, "blk", scatter_dimension=0, tiled=True),
        lax.psum_scatter(grad_down, "blk", scatter_dimension=1, tiled=True),
        lax.psum_scatter(grad_attn_gain, "blk", scatter_dimension=0, tiled=True),
        lax.psum_scatter(grad_mlp_gain, "blk", scatter_dimension=0, tiled=True),
    )
    return (
        layer_out,
        input_grad,
        summed[0],
        summed[1],
        summed[2],
        summed[3],
        summed[4],
        summed[5],
        summed[6],
        summed[7],
        summed[8],
    )


MESH = pl.DeviceIdType.MESH
F32, BF16 = jnp.float32, jnp.bfloat16
LOG2E = 1.4426950408889634
SCORE_SCALE = HEAD_SIZE**-0.5
VMEM_BYTES = 64 * 2**20 - 2**19
HALF = HEAD_SIZE // 2


def dot_nn(a, b):
    return lax.dot_general(a, b, (((1,), (0,)), ((), ())), preferred_element_type=F32)


def dot_nt(a, b):
    return lax.dot_general(a, b, (((1,), (1,)), ((), ())), preferred_element_type=F32)


def dot_tn(a, b):
    return lax.dot_general(a, b, (((0,), (0,)), ((), ())), preferred_element_type=F32)


class Place:
    def __init__(self):
        self.b = lax.axis_index("blk")
        self.t = lax.axis_index("tp")
        self.core = self.b % 2
        self.chip = self.b // 2
        self.x = self.chip % 2
        self.y = self.b // 4
        self.mate = self.b + 1 - 2 * self.core
        self.inner = jnp.logical_or(self.t == 1, self.t == 2)
        self.outer = jnp.logical_not(self.inner)
        self.pair = self.t + 1 - 2 * (self.t % 2)
        self.across = 3 - self.t

    def slot(self, s):
        core = (self.core + s % 2) % 2
        x = (self.x + (s // 2) % 2) % 2
        y = (self.y + s // 4) % 2
        return (y * 2 + x) * 2 + core

    def chip_at(self, k):
        x = (self.x + (k + 1) % 2) % 2
        y = (self.y + 1 - k // 2) % 2
        return y * 2 + x


def remote(src, dst, ssem, rsem, b, t):
    return pltpu.make_async_remote_copy(
        src_ref=src, dst_ref=dst, send_sem=ssem, recv_sem=rsem, device_id=(b, t), device_id_type=MESH
    )


def enter(me, blk_steps):
    barrier = pltpu.get_barrier_semaphore()
    for s in blk_steps:
        pl.semaphore_signal(barrier, inc=1, device_id=(me.slot(s), me.t), device_id_type=MESH)
    for z in (me.pair, me.across):
        pl.semaphore_signal(barrier, inc=1, device_id=(me.b, z), device_id_type=MESH)
    pl.semaphore_wait(barrier, len(blk_steps) + 2)


class LineSum:
    def __init__(self, me, part, first, second, sems, rows):
        self.me, self.part, self.first, self.second, self.sems, self.rows = (
            me, part, first, second, sems, rows,
        )

    def at(self, ref, p):
        return ref.at[pl.ds(pl.multiple_of(p * self.rows, self.rows), self.rows), :]

    def copy(self, stage, p):
        me = self.me
        src = (self.part, self.part, self.first)[stage]
        dst = (self.first, self.second, self.first)[stage]
        target = (me.pair, me.across, me.pair)[stage]
        return remote(
            self.at(src, p), self.at(dst, p),
            self.sems.at[2 * stage, p], self.sems.at[2 * stage + 1, p], me.b, target,
        )

    def give(self, p):
        @pl.when(self.me.outer)
        def _():
            self.copy(0, p).start()

    def fold(self, p):
        @pl.when(self.me.inner)
        def _():
            self.copy(0, p).wait_recv()
            mine, got = self.at(self.part, p), self.at(self.first, p)
            mine[...] = (mine[...].astype(F32) + got[...].astype(F32)).astype(BF16)
            self.copy(1, p).start()

    def unfold(self, p):
        @pl.when(self.me.inner)
        def _():
            self.copy(1, p).wait_recv()
            mine, got, out = self.at(self.part, p), self.at(self.second, p), self.at(self.first, p)
            out[...] = (mine[...].astype(F32) + got[...].astype(F32)).astype(BF16)
            self.copy(2, p).start()

    def take(self, p):
        @pl.when(self.me.outer)
        def _():
            self.copy(2, p).wait_recv()

    def drain_outer(self, pieces):
        @pl.when(self.me.outer)
        def _():
            def one(p, carry):
                self.copy(0, p).wait_send()
                return carry

            lax.fori_loop(0, pieces, one, 0)

    def drain_inner(self, pieces):
        @pl.when(self.me.inner)
        def _():
            def one(p, carry):
                self.copy(1, p).wait_send()
                self.copy(2, p).wait_send()
                return carry

            lax.fori_loop(0, pieces, one, 0)

    def drain(self, pieces):
        self.drain_outer(pieces)
        self.drain_inner(pieces)


class LineGather:
    def __init__(self, me, view, ssem, rsem, last):
        self.me, self.view, self.ssem, self.rsem, self.last = me, view, ssem, rsem, last

    def copy(self, way, hop, p):
        t = self.me.t

        def sent():
            slot = t - (hop - 1) if way == 0 else t + (hop - 1)
            ref = self.view(slot, p)
            target = t + 1 if way == 0 else t - 1
            return remote(ref, ref, self.ssem.at[way, hop - 1, p], self.rsem.at[way, hop - 1, p], self.me.b, target)

        def got():
            slot = t - hop if way == 0 else t + hop
            ref = self.view(slot, p)
            target = t - 1 if way == 0 else t + 1
            return remote(ref, ref, self.ssem.at[way, hop - 1, p], self.rsem.at[way, hop - 1, p], self.me.b, target)

        return sent, got

    def sends(self, way, hop):
        t = self.me.t
        if way == 0:
            return jnp.logical_and(t - (hop - 1) >= 0, t + 1 <= self.last)
        return jnp.logical_and(t + (hop - 1) <= self.last, t >= 1)

    def gets(self, way, hop):
        t = self.me.t
        return t - hop >= 0 if way == 0 else t + hop <= self.last

    def send(self, hop, p):
        for way in (0, 1):

            @pl.when(self.sends(way, hop))
            def _(way=way):
                self.copy(way, hop, p)[0]().start()

    def step(self, hop, p, also=None):
        for way in (0, 1):

            @pl.when(self.gets(way, hop))
            def _(way=way):
                self.copy(way, hop, p)[1]().wait_recv()
                if also is not None:
                    also(way, hop).start()

        if hop < self.last:
            self.send(hop + 1, p)

    def drain(self, p):
        for hop in range(1, self.last + 1):
            for way in (0, 1):

                @pl.when(self.sends(way, hop))
                def _(way=way, hop=hop):
                    self.copy(way, hop, p)[0]().wait_send()


class BlockSum:
    def __init__(self, me, make, outs, held, mates, chips, sems, spare):
        self.me, self.make, self.outs, self.spare = me, make, outs, spare
        self.held, self.mates, self.chips, self.sems = held, mates, chips, sems

    def to_mate(self, k):
        me = self.me
        return remote(
            self.held(k % 2), self.mates(k), self.sems.at[0, k], self.sems.at[1, k], me.mate, me.t
        )

    def to_chip(self, k):
        me = self.me
        return remote(
            self.mates(k), self.chips(k), self.sems.at[2, k], self.sems.at[3, k],
            me.chip_at(k) * 2 + me.core, me.t,
        )

    def lend(self, k):
        me = self.me
        if k >= 2:
            self.to_mate(k - 2).wait_send()
        held = self.held(k % 2)
        even = me.core == 0
        for (lo, hi, value), out, spare in zip(self.make(me.chip_at(k)), self.outs, self.spare):
            half = value.shape[0] // 2
            low, high = value[:half], value[half:]
            held[:, lo:hi] = jnp.where(even, high, low).astype(BF16)
            if k % 2 == 0:
                spare[...] = jnp.where(even, low, high).astype(BF16)
            else:
                out[...] = jnp.where(even, low, high)
        self.to_mate(k).start()

    def merge(self, k, spans):
        self.to_mate(k).wait_recv()
        mates = self.mates(k)
        for (lo, hi), out, spare in zip(spans, self.outs, self.spare):
            own = spare[...].astype(F32) if k % 2 == 0 else out[...]
            total = own + mates[:, lo:hi].astype(F32)
            if k < 3:
                mates[:, lo:hi] = total.astype(BF16)
            else:
                out[...] = total
        if k < 3:
            self.to_chip(k).start()

    def finish(self, spans):
        for k in range(3):
            self.to_chip(k).wait_recv()
            chips = self.chips(k)
            for (lo, hi), out in zip(spans, self.outs):
                out[...] += chips[:, lo:hi].astype(F32)

    def drain(self):
        for k in (2, 3):
            self.to_mate(k).wait_send()
        for k in range(3):
            self.to_chip(k).wait_send()


def norm_rows(values):
    inverse = lax.rsqrt(jnp.mean(values * values, axis=-1, keepdims=True) + norm_eps)
    return values * inverse, inverse


def turn(values, cs_ref, sign):
    cosine, sine = cs_ref[0:HALF, :], cs_ref[HALF:HEAD_SIZE, :] * sign
    pieces = []
    for h in range(values.shape[0] // HEAD_SIZE):
        low = values[h * HEAD_SIZE : h * HEAD_SIZE + HALF]
        high = values[h * HEAD_SIZE + HALF : (h + 1) * HEAD_SIZE]
        pieces.append(low * cosine - high * sine)
        pieces.append(high * cosine + low * sine)
    return jnp.concatenate(pieces, axis=0)


def fill_bias(bias, st_ref, key_start, query_start):
    key_place = lax.broadcasted_iota(jnp.int32, bias.shape, 0) + key_start
    query_place = lax.broadcasted_iota(jnp.int32, bias.shape, 1) + query_start
    allowed = jnp.logical_and(key_place >= st_ref[0:1, :], key_place <= query_place)
    bias[...] = jnp.where(allowed, 0.0, neg_fill)


def heads_of(h, group):
    g = h // group
    return slice(h * HEAD_SIZE, (h + 1) * HEAD_SIZE), slice(g * HEAD_SIZE, (g + 1) * HEAD_SIZE), g


def layer_kernel(
    dims,
    len_ref, ag_ref, mg_ref, hid_hbm, og_hbm, wq_hbm, wk_hbm, wv_hbm, wo_hbm, wg_hbm, wu_hbm, wd_hbm,
    lo_out, ig_out, gq_ref, gk_ref, gv_ref, go_ref, gg_ref, gu_ref, gd_ref, gag_ref, gmg_ref,
    hid, og, wq, wkv, wo, wg, wu, wd, kv, norm, attn, qt, ot, bias, mid, act, dg, du,
    p2, a2, b2, p3, a3, b3, dbr, dot_ref, dq, acc, low_t, dqr, dkvr,
    kv_mates, kv_chips, held_a, held_b, chips_b, held_c, mates_c, chips_c, total_c,
    turns, starts, m_ref, l_ref, lse, delta, gain, gain_in,
    load_sem, kv_sem, wo_sem, wo_plane_sem, wo_mate_sem, at_sem, sem2, sem3, sem4, kvs_sem, rs_sem, gain_sem, out_sem,
    mate_ready, chip_ready,
):
    rows, piece, chunk, share = dims["rows"], dims["piece"], dims["chunk"], dims["share"]
    q_heads, group, kv_width, n_docs = dims["q_heads"], dims["group"], dims["kv_width"], dims["n_docs"]
    n_pieces, n_chunks = rows // piece, rows // chunk
    per = chunk // piece
    width, hidden_units = wg.shape
    q_width = q_heads * HEAD_SIZE
    last = wo.shape[0] - 1
    me = Place()
    scale2 = SCORE_SCALE * LOG2E

    def each(f, lo, hi):
        def one(p, carry):
            f(p)
            return carry

        lax.fori_loop(lo, hi, one, 0)

    barrier = pltpu.get_barrier_semaphore()
    for s in range(1, 8):
        pl.semaphore_signal(barrier, inc=1, device_id=(me.slot(s), me.t), device_id_type=MESH)
    for z in (me.pair, me.across):
        pl.semaphore_signal(barrier, inc=1, device_id=(me.b, z), device_id_type=MESH)
    loads = {}
    for i, (name, source, target) in enumerate((
        ("wo", wo_hbm, wo.at[me.t]), ("hid", hid_hbm, hid), ("wk", wk_hbm, wkv.at[0:kv_width]),
        ("wv", wv_hbm, wkv.at[kv_width : 2 * kv_width]), ("wq", wq_hbm, wq), ("wg", wg_hbm, wg),
        ("wu", wu_hbm, wu), ("og", og_hbm, og), ("wd", wd_hbm, wd),
    )):
        loads[name] = pltpu.make_async_copy(source, target, load_sem.at[i])
    for name in ("wo", "hid", "wk", "wv"):
        loads[name].start()

    attn_gain, mlp_gain = ag_ref[...].reshape(1, width), mg_ref[...].reshape(1, width)

    def chunk_rows(c):
        return pl.ds(pl.multiple_of(c * chunk, chunk), chunk)

    def first_norm(c):
        r = chunk_rows(c)
        normed, _ = norm_rows(hid[r, :].astype(F32))
        norm[r, :] = (normed * attn_gain).astype(BF16)

    part = share // 4
    my_half = pl.ds(pl.multiple_of(me.core * share, share), share)

    def wo_rows(slot, p):
        first = me.core * share + p * 2 * part + (me.x, me.y)[p] * part
        return wo.at[slot, pl.ds(pl.multiple_of(first, part), part), :]

    whole_wo = LineGather(me, wo_rows, wo_sem.at[0], wo_sem.at[1], last)

    def wo_plane(way, hop, p):
        ref = wo_rows(me.t - hop if way == 0 else me.t + hop, p)
        return remote(
            ref, ref, wo_plane_sem.at[0, p, way, hop - 1], wo_plane_sem.at[1, p, way, hop - 1],
            me.slot(2 + 2 * p), me.t,
        )

    def wo_to_mate(way, hop):
        ref = wo.at[me.t - hop if way == 0 else me.t + hop, my_half, :]
        return remote(
            ref, ref, wo_mate_sem.at[0, way, hop - 1], wo_mate_sem.at[1, way, hop - 1], me.mate, me.t
        )

    def each_wo(hops, action):
        for hop in hops:
            for way in (0, 1):

                @pl.when(whole_wo.gets(way, hop))
                def _(way=way, hop=hop):
                    action(way, hop)

    def wo_spread(way, hop):
        for p in (0, 1):
            wo_plane(way, hop, p).start()

    def wo_lend(way, hop):
        for p in (0, 1):
            wo_plane(way, hop, p).wait_recv()
        wo_to_mate(way, hop).start()

    def wo_line(hop):
        for p in (0, 1):
            whole_wo.step(hop, p)

    loads["wq"].start()
    places = me.b * rows + lax.broadcasted_iota(jnp.int32, (1, rows), 1)
    start, end = jnp.zeros((1, rows), jnp.int32), jnp.int32(0)
    for k in range(n_docs):
        end = end + len_ref[k]
        start = jnp.where(places >= end, end, start)
    starts[...] = jnp.broadcast_to(start, starts.shape)
    order = lax.broadcasted_iota(jnp.int32, (HALF, 1), 0).astype(F32)
    freqs = jnp.exp(order * (-2.0 / HEAD_SIZE * math.log(rope_base)))
    angle = freqs * (places - start).astype(F32)
    turns[0:HALF, :] = jnp.cos(angle)
    turns[HALF:HEAD_SIZE, :] = jnp.sin(angle)
    loads["hid"].wait()
    each(first_norm, 0, n_chunks)
    loads["wk"].wait()
    loads["wv"].wait()
    both_t = dot_nt(wkv[...], norm[...])
    kv[me.b, 0:kv_width, :] = turn(both_t[0:kv_width], turns, 1.0).astype(BF16)
    kv[me.b, kv_width : 2 * kv_width, :] = both_t[kv_width : 2 * kv_width].astype(BF16)

    loads["wo"].wait()
    pl.semaphore_wait(barrier, 9)
    for p in (0, 1):
        whole_wo.send(1, p)
    def kv_copy(slot, target, n):
        return remote(kv.at[slot], kv.at[slot], kv_sem.at[0, n], kv_sem.at[1, n], target, me.t)

    def share_kv(s):
        @pl.when(me.slot(s) > me.b)
        def _():
            kv_copy(me.b, me.slot(s), s).start()

    for s in (1, 2, 4):
        share_kv(s)
    for name in ("wg", "wu", "og", "wd"):
        loads[name].start()
    loads["wq"].wait()
    qt[...] = turn(dot_nn(norm[...], wq[...]).T, turns, 1.0).astype(BF16)
    m_ref[...] = jnp.full(m_ref.shape, neg_fill, F32)
    l_ref[...] = jnp.zeros(l_ref.shape, F32)
    ot[...] = jnp.zeros(ot.shape, F32)

    def attend(s, carry):
        slot = me.slot(s)
        arrives = jnp.logical_and(s > 0, slot < me.b)

        @pl.when(arrives)
        def _():
            kv_copy(slot, me.mate, s).wait_recv()

        @pl.when(jnp.logical_and(arrives, s % 2 == 0))
        def _():
            kv_copy(slot, me.mate, s + 1).start()

        for hop, turn_at in ((1, 2), (2, 3), (3, 5)):

            @pl.when(s == turn_at)
            def _(hop=hop):
                wo_line(hop)

        @pl.when(s == 6)
        def _():
            each_wo((1, 2, 3), wo_spread)

        @pl.when(slot <= me.b)
        def _():
            fill_bias(bias, starts, slot * rows, me.b * rows)
            for h in range(q_heads):
                qs, ks, g = heads_of(h, group)
                vs = slice(kv_width + g * HEAD_SIZE, kv_width + (g + 1) * HEAD_SIZE)
                scores = dot_tn(kv[slot, ks, :], qt[qs, :]) + bias[...]
                old = m_ref[h : h + 1, :]
                new = jnp.maximum(old, jnp.max(scores, axis=0, keepdims=True))
                probs = jnp.exp2((scores - new) * scale2)
                keep = jnp.exp2((old - new) * scale2)
                m_ref[h : h + 1, :] = new
                l_ref[h : h + 1, :] = l_ref[h : h + 1, :] * keep + jnp.sum(probs, axis=0, keepdims=True)
                ot[qs, :] = ot[qs, :] * keep + dot_nn(kv[slot, vs, :], probs.astype(BF16))

        @pl.when(s == 1)
        def _():
            share_kv(6)

        return carry

    lax.fori_loop(0, 8, attend, 0)

    line_attn = LineGather(
        me, lambda slot, p: attn.at[slot, chunk_rows(p), :], at_sem.at[0], at_sem.at[1], last
    )
    for h in range(q_heads):
        qs, _, _ = heads_of(h, group)
        ot[qs, :] = ot[qs, :] / l_ref[h : h + 1, :]
    for c in range(n_chunks):
        attn[me.t, c * chunk : (c + 1) * chunk, :] = ot[:, c * chunk : (c + 1) * chunk].T.astype(BF16)
        line_attn.send(1, c)
    lse[...] = jnp.zeros(lse.shape, F32)
    lse[0:q_heads, :] = m_ref[0:q_heads, :] * scale2 + jnp.log2(l_ref[0:q_heads, :])
    for name in ("wg", "wu", "og", "wd"):
        loads[name].wait()
    line_attn.step(1, 0)
    each_wo((1, 2, 3), wo_lend)
    line_attn.step(2, 0)
    line_attn.step(3, 0)
    line_attn.step(1, 1)
    each_wo((1, 2, 3), lambda way, hop: wo_to_mate(way, hop).wait_recv())

    back = LineSum(me, p2, a2, b2, sem2, piece)
    forth_rows = rows // 8
    forth = LineSum(me, p3, a3, b3, sem3, forth_rows)
    forth_pieces = 8
    adds_middle = (me.t == 1).astype(F32)

    def feed(c, carry):
        r = chunk_rows(c)

        for n in range(0, width, 512):
            ns = slice(n, n + 512)
            total = hid[r, ns].astype(F32)
            for z in range(last + 1):
                total = total + dot_nn(attn[z, r, :], wo[z, :, ns])
            mid[r, ns] = total
        normed, _ = norm_rows(mid[r, :])
        norm[r, :] = (normed * mlp_gain).astype(BF16)

        @pl.when(c < n_chunks - 1)
        def _():
            line_attn.step(2, c + 1)

        for n in range(0, hidden_units, 512):
            ns = slice(n, n + 512)
            gate = dot_nn(norm[r, :], wg[:, ns])
            up = dot_nn(norm[r, :], wu[:, ns])
            grad = dot_nt(og[r, :], wd[ns, :])
            sig = 1.0 / (1.0 + jnp.exp(-gate))
            silu = gate * sig
            act[r, ns] = (silu * up).astype(BF16)
            dg[r, ns] = (grad * up * sig * (1.0 + gate * (1.0 - sig))).astype(BF16)
            du[r, ns] = (grad * silu).astype(BF16)
            if n == 0:

                @pl.when(c < n_chunks - 2)
                def _():
                    line_attn.step(1, c + 2)

        for n in range(0, width, 512):
            ns = slice(n, n + 512)
            p2[r, ns] = (dot_nt(dg[r, :], wg[ns, :]) + dot_nt(du[r, :], wu[ns, :])).astype(BF16)
        each(back.give, c * per, (c + 1) * per)

        @pl.when(c < n_chunks - 1)
        def _():
            line_attn.step(3, c + 1)

        @pl.when(c >= 2)
        def _():
            each(back.fold, (c - 2) * per, (c - 1) * per)

        @pl.when(c >= 3)
        def _():
            each(back.unfold, (c - 3) * per, (c - 2) * per)

        for n in range(0, width, 512):
            ns = slice(n, n + 512)
            p3[r, ns] = (dot_nn(act[r, :], wd[:, ns]) + mid[r, ns] * adds_middle).astype(BF16)
        return carry

    lax.fori_loop(0, n_chunks, feed, 0)
    pl.semaphore_signal(mate_ready, inc=1, device_id=(me.mate, me.t), device_id_type=MESH)
    for k in range(3):
        pl.semaphore_signal(
            chip_ready, inc=1, device_id=(me.chip_at(k) * 2 + me.core, me.t), device_id_type=MESH
        )
    pair = 2 * share

    def pair_columns(ref, chip):
        return ref[:, pl.ds(pl.multiple_of(chip * pair, pair), pair)]

    def slots(ref, first, columns):
        return lambda k: ref.at[(first + k) * share : (first + k + 1) * share, 0:columns]

    sum_gate = BlockSum(
        me, lambda m: [(0, hidden_units, dot_tn(pair_columns(norm, m), dg[...]))], [gg_ref],
        lambda k: held_a.at[0, k], slots(wg, 0, hidden_units), slots(wg, 4, hidden_units), rs_sem.at[0],
        [slots(wg, 7, hidden_units)(0)],
    )
    sum_up = BlockSum(
        me, lambda m: [(0, hidden_units, dot_tn(pair_columns(norm, m), du[...]))], [gu_ref],
        lambda k: held_a.at[1, k], slots(wu, 0, hidden_units), slots(wu, 4, hidden_units), rs_sem.at[1],
        [slots(wu, 7, hidden_units)(0)],
    )
    span_a = [(0, hidden_units)]
    pl.semaphore_wait(mate_ready, 1)
    gain[...] = jnp.zeros(gain.shape, F32)

    def middle_grad(c):
        each(back.take, c * per, (c + 1) * per)
        r = chunk_rows(c)
        normed, inverse = norm_rows(mid[r, :])
        grad = a2[r, :].astype(F32)
        scaled = grad * mlp_gain
        gain[1:2, :] += jnp.sum(grad * normed, axis=0, keepdims=True)
        found = og[r, :].astype(F32) + inverse * (
            scaled - normed * jnp.mean(scaled * normed, axis=-1, keepdims=True)
        )
        mid[r, :] = found
        dbr[r, :] = found.astype(BF16)

    def fold_on(lo, hi):
        def one(p, carry):
            back.fold(p)
            back.unfold(p - per)
            return carry

        lax.fori_loop(lo, hi, one, 0)

    def lend_both(k):
        sum_gate.lend(k)
        sum_up.lend(k)

    def merge_both(k):
        sum_gate.merge(k, span_a)
        sum_up.merge(k, span_a)

    lend_both(0)
    fold_on((n_chunks - 2) * per, (n_chunks - 2) * per + per // 2)
    lend_both(1)
    back.drain_outer(n_pieces)
    each(forth.give, 0, forth_pieces)
    fold_on((n_chunks - 2) * per + per // 2, (n_chunks - 1) * per)
    pl.semaphore_wait(chip_ready, 3)
    merge_both(0)
    fold_on((n_chunks - 1) * per, n_pieces - per // 2)
    lend_both(2)
    merge_both(1)
    fold_on(n_pieces - per // 2, n_pieces)
    merge_both(2)
    each(back.unfold, n_pieces - per, n_pieces)
    each(middle_grad, 0, n_chunks - 1)
    each(middle_grad, n_chunks - 1, n_chunks)
    dot_ref[...] = dot_nt(wo[me.t], dbr[...]).astype(BF16)
    delta[...] = jnp.zeros(delta.shape, F32)
    for h in range(q_heads):
        qs, _, _ = heads_of(h, group)
        delta[h : h + 1, :] = jnp.sum(dot_ref[qs, :].astype(F32) * ot[qs, :], axis=0, keepdims=True)
    dq[...] = jnp.zeros(dq.shape, F32)
    back.drain_inner(n_pieces)
    ahead = 2
    each(forth.fold, 0, ahead)

    for s in (1, 2, 4, 6):

        @pl.when(me.slot(s) > me.b)
        def _(s=s):
            kv_copy(me.b, me.slot(s), s).wait_send()

    for s in (2, 4, 6):

        @pl.when(me.slot(s) < me.b)
        def _(s=s):
            kv_copy(me.slot(s), me.mate, s + 1).wait_send()

    def kv_to_mate(k):
        return remote(
            kv.at[me.chip_at(k) * 2 + 1 - me.core], kv_mates.at[k], kvs_sem.at[0, k], kvs_sem.at[1, k],
            me.mate, me.t,
        )

    def kv_to_chip(k):
        return remote(
            kv_mates.at[k], kv_chips.at[k], kvs_sem.at[2, k], kvs_sem.at[3, k],
            me.chip_at(k) * 2 + me.core, me.t,
        )

    def attend_back(u, carry):
        k, own = u // 2, u % 2
        chip = me.chip_at(k)
        slot = chip * 2 + (me.core + 1 - own) % 2

        @pl.when(u + ahead < forth_pieces)
        def _():
            forth.fold(u + ahead)

        @pl.when(u >= 2)
        def _():
            forth.unfold(u - 2)

        @pl.when(slot <= me.b)
        def _():
            fill_bias(bias, starts, slot * rows, me.b * rows)
            for g in range(q_heads // group):
                ks = slice(g * HEAD_SIZE, (g + 1) * HEAD_SIZE)
                vs = slice(kv_width + g * HEAD_SIZE, kv_width + (g + 1) * HEAD_SIZE)
                key_t, value_t = kv[slot, ks, :], kv[slot, vs, :]
                grad_k = grad_v = None
                for h in range(g * group, (g + 1) * group):
                    qs, _, _ = heads_of(h, group)
                    query_t, grad_t = qt[qs, :], dot_ref[qs, :]
                    scores = dot_tn(key_t, query_t) + bias[...]
                    probs = jnp.exp2(scores * scale2 - lse[h : h + 1, :])
                    grad_p = dot_tn(value_t, grad_t)
                    grad_s = (probs * (grad_p - delta[h : h + 1, :])).astype(BF16)
                    one_v = dot_nt(grad_t, probs.astype(BF16))
                    one_k = dot_nt(query_t, grad_s)
                    grad_v = one_v if grad_v is None else grad_v + one_v
                    grad_k = one_k if grad_k is None else grad_k + one_k
                    dq[qs, :] += dot_nn(key_t, grad_s)
                acc[ks, :] = grad_k
                acc[vs, :] = grad_v

        @pl.when(jnp.logical_and(own == 0, slot <= me.b))
        def _():
            kv[slot] = acc[...].astype(BF16)
            kv_to_mate(k).start()

        @pl.when(jnp.logical_and(own == 1, chip < me.chip))
        def _():
            kv_to_mate(k).wait_recv()
            kv_mates[k] = (acc[...] + kv_mates[k].astype(F32)).astype(BF16)
            kv_to_chip(k).start()

        return carry

    lax.fori_loop(0, 8, attend_back, 0)
    low_t[0:q_width, :] = turn(dq[...] * SCORE_SCALE, turns, -1.0).astype(BF16)
    dqr[...] = low_t[0:q_width, :].T

    def first_norm_again(c):
        r = chunk_rows(c)
        normed, _ = norm_rows(hid[r, :].astype(F32))
        norm[r, :] = (normed * attn_gain).astype(BF16)


    @pl.when(me.core == 0)
    def _():
        kv_to_mate(3).wait_recv()
        acc[...] += kv_mates[3].astype(F32)

    for k in range(3):

        @pl.when(me.chip_at(k) > me.chip)
        def _(k=k):
            kv_to_chip(k).wait_recv()
            acc[...] += kv_chips[k].astype(F32)

    low_t[q_width : q_width + kv_width, :] = turn(acc[0:kv_width, :] * SCORE_SCALE, turns, -1.0).astype(BF16)
    low_t[q_width + kv_width :, :] = acc[kv_width : 2 * kv_width, :].astype(BF16)
    dkvr[...] = low_t[q_width:, :].T

    each(forth.take, 0, 2)
    end_sum = LineSum(me, p2, a2, b2, sem4, piece)

    def input_part(c):
        r = chunk_rows(c)
        for n in range(0, width, 512):
            ns = slice(n, n + 512)
            p2[r, ns] = (dot_nt(dqr[r, :], wq[ns, :]) + dot_nn(dkvr[r, :], wkv[:, ns])).astype(BF16)
        each(end_sum.give, c * per, (c + 1) * per)

    each(input_part, 0, n_chunks)
    each(forth.unfold, forth_pieces - 2, forth_pieces)

    def make_b(m):
        yield 0, hidden_units, dot_tn(pair_columns(og, m), act[...])
        yield hidden_units, hidden_units + q_width, dot_tn(pair_columns(dbr, m), attn[me.t])

    def make_c(m):
        columns = pair_columns(norm, m)
        yield 0, q_width, dot_tn(columns, dqr[...])
        yield q_width, q_width + 2 * kv_width, dot_tn(columns, dkvr[...])

    width_b = hidden_units + q_width
    in_wd = slots(wd, 0, width_b)
    sum_b = BlockSum(
        me, make_b, [gd_ref, go_ref], lambda k: held_b.at[k], in_wd,
        lambda k: in_wd(4) if k == 0 else chips_b.at[k - 1], rs_sem.at[2],
        [dg.at[0:share, :], du.at[0:share, 0:q_width]],
    )
    span_b = [(0, hidden_units), (hidden_units, width_b)]
    total_parts = [total_c.at[:, 0:q_width], total_c.at[:, q_width : q_width + 2 * kv_width]]
    sum_c = BlockSum(
        me, make_c, total_parts, lambda k: held_c.at[k], lambda k: mates_c.at[k], lambda k: chips_c.at[k],
        rs_sem.at[3],
        [dg.at[share : 2 * share, 0:q_width], du.at[share : 2 * share, 0 : 2 * kv_width]],
    )
    span_c = [(0, q_width), (q_width, q_width + 2 * kv_width)]
    work = [(functools.partial(lend_both, 3), functools.partial(merge_both, 3))]
    for sums, spans in ((sum_b, span_b), (sum_c, span_c)):
        for k in range(4):
            work.append((functools.partial(sums.lend, k), functools.partial(sums.merge, k, spans)))
    done, late = 0, None
    for i, (lend, merge) in enumerate(work):
        if i == 1:
            each(first_norm_again, 0, n_chunks)
        lend()
        upto = n_pieces * (i + 1) // len(work)
        for p in range(done, upto):
            end_sum.fold(p)
            if p >= 1:
                end_sum.unfold(p - 1)
        done = upto
        if late is not None:
            late()
        late = merge
    end_sum.unfold(n_pieces - 1)
    late()

    each(forth.take, 2, forth_pieces)
    lo_save = pltpu.make_async_copy(a3, lo_out, out_sem.at[0])
    lo_save.start()

    def input_rows(c):
        each(end_sum.take, c * per, (c + 1) * per)
        r = chunk_rows(c)
        normed, inverse = norm_rows(hid[r, :].astype(F32))
        grad = a2[r, :].astype(F32)
        scaled = grad * attn_gain
        gain[0:1, :] += jnp.sum(grad * normed, axis=0, keepdims=True)
        found = inverse * (scaled - normed * jnp.mean(scaled * normed, axis=-1, keepdims=True))
        dbr[r, :] = (mid[r, :] + found).astype(BF16)

    each(input_rows, 0, n_chunks)

    def gain_copy(s):
        return remote(gain, gain_in.at[s], gain_sem.at[0, s], gain_sem.at[1, s], me.slot(s), me.t)

    for s in range(1, 8):
        gain_copy(s).start()
    ig_save = pltpu.make_async_copy(dbr, ig_out, out_sem.at[1])
    ig_save.start()
    sum_gate.finish(span_a)
    sum_up.finish(span_a)
    sum_b.finish(span_b)
    sum_c.finish(span_c)
    gq_ref[...] = total_c[:, 0:q_width]
    gk_ref[...] = total_c[:, q_width : q_width + kv_width]
    gv_ref[...] = total_c[:, q_width + kv_width : q_width + 2 * kv_width]
    for s in range(1, 8):
        gain_copy(s).wait_recv()
    gains = gain[...]
    for s in range(1, 8):
        gains = gains + gain_in[s]
    gain_in[0] = gains
    mine = jnp.zeros((8, share), F32)
    for j in range(8):
        mine = mine + jnp.where(me.b == j, gain_in[0, :, j * share : (j + 1) * share], 0.0)
    gag_ref[...] = mine[0, :]
    gmg_ref[...] = mine[1, :]

    for s in range(1, 8):
        gain_copy(s).wait_send()
    for p in (0, 1):
        whole_wo.drain(p)

    def wo_done(way, hop):
        for p in (0, 1):
            wo_plane(way, hop, p).wait_send()
        wo_to_mate(way, hop).wait_send()

    each_wo((1, 2, 3), wo_done)
    each(line_attn.drain, 0, n_chunks)
    forth.drain(forth_pieces)
    end_sum.drain(n_pieces)
    for sums in (sum_gate, sum_up, sum_b, sum_c):
        sums.drain()
    for k in range(4):
        chip = me.chip_at(k)
        slot = chip * 2 + 1 - me.core

        @pl.when(slot <= me.b)
        def _(k=k):
            kv_to_mate(k).wait_send()

        if k < 3:

            @pl.when(chip < me.chip)
            def _(k=k):
                kv_to_chip(k).wait_send()

    lo_save.wait()
    ig_save.wait()


def hand_over(n, *refs):
    sources, targets, held, sems = refs[:n], refs[n : 2 * n], refs[2 * n : 3 * n], refs[3 * n]
    ins = [pltpu.make_async_copy(a, h, sems.at[0, i]) for i, (a, h) in enumerate(zip(sources, held))]
    outs = [pltpu.make_async_copy(h, b, sems.at[1, i]) for i, (h, b) in enumerate(zip(held, targets))]
    for copy in ins:
        copy.start()
    for first, second in zip(ins, outs):
        first.wait()
        second.start()
    for copy in outs:
        copy.wait()


def kernel_shards(
    hidden_in, out_grad, lengths, attn_gain, w_query, key_projection_weight, value_projection_weight,
    w_out, mlp_gain, w_gate, w_up, w_down,
):
    rows, width = hidden_in.shape
    q_width, kv_width = w_query.shape[1], key_projection_weight.shape[1]
    hidden_units = w_gate.shape[1]
    blocks, line_size = lax.axis_size("blk"), lax.axis_size("tp")
    share = width // blocks
    piece, chunk = rows // 8, rows // 4
    pieces, chunks = rows // piece, rows // chunk
    dims = dict(
        rows=rows, piece=piece, chunk=chunk, share=share, q_heads=q_width // HEAD_SIZE,
        group=q_width // kv_width, kv_width=kv_width, n_docs=lengths.shape[0],
    )
    vmem, hbm = pl.BlockSpec(memory_space=pltpu.VMEM), pl.BlockSpec(memory_space=pl.ANY)
    smem = pl.BlockSpec(memory_space=pltpu.SMEM)
    dma, regular = pltpu.SemaphoreType.DMA, pltpu.SemaphoreType.REGULAR

    def shape(dtype, *dims_):
        return jax.ShapeDtypeStruct(dims_, dtype)

    def low(*dims_):
        return pltpu.VMEM(dims_, BF16)

    def full(*dims_):
        return pltpu.VMEM(dims_, F32)

    line = [low(rows, width)] * 3
    width_b, width_c = hidden_units + q_width, q_width + 2 * kv_width
    shapes = (
        shape(BF16, rows, width), shape(BF16, rows, width), shape(F32, share, q_width),
        shape(F32, share, kv_width), shape(F32, share, kv_width), shape(F32, share, q_width),
        shape(F32, share, hidden_units), shape(F32, share, hidden_units), shape(F32, share, hidden_units),
        shape(F32, share), shape(F32, share),
    )
    outs = pl.pallas_call(
        functools.partial(layer_kernel, dims),
        out_shape=shapes,
        in_specs=[smem, vmem, vmem] + [hbm] * 9,
        out_specs=(hbm, hbm) + (vmem,) * 9,
        scratch_shapes=[
            low(rows, width), low(rows, width), low(width, q_width), low(2 * kv_width, width),
            low(line_size, q_width, width), low(width, hidden_units), low(width, hidden_units),
            low(hidden_units, width), low(blocks, 2 * kv_width, rows), low(rows, width),
            low(line_size, rows, q_width), low(q_width, rows), full(q_width, rows), full(rows, rows),
            full(rows, width), low(rows, hidden_units), low(rows, hidden_units), low(rows, hidden_units),
            *line, *line, low(rows, width), low(q_width, rows), full(q_width, rows), full(2 * kv_width, rows),
            low(width_c, rows), low(rows, q_width), low(rows, 2 * kv_width),
            low(4, 2 * kv_width, rows), low(3, 2 * kv_width, rows),
            low(2, 2, share, hidden_units), low(2, share, width_b), low(2, share, width_b),
            low(2, share, width_c), low(4, share, width_c), low(3, share, width_c), full(share, width_c),
            full(HEAD_SIZE, rows), pltpu.VMEM((8, rows), jnp.int32), full(8, rows), full(8, rows), full(8, rows),
            full(8, rows), full(8, width), full(8, 8, width),
            dma((9,)), dma((2, 8)), dma((2, 2, line_size - 1, 2)), dma((2, 2, 2, line_size - 1)),
            dma((2, 2, line_size - 1)),
            dma((2, 2, line_size - 1, chunks)), dma((6, pieces)), dma((6, pieces)), dma((6, pieces)),
            dma((4, 4)), dma((4, 4, 4)), dma((2, 8)), dma((2,)), regular, regular,
        ],
        compiler_params=pltpu.CompilerParams(
            collective_id=0, has_side_effects=True, vmem_limit_bytes=VMEM_BYTES
        ),
    )(
        lengths, attn_gain, mlp_gain, hidden_in, out_grad, w_query, key_projection_weight.T,
        value_projection_weight.T, w_out, w_gate, w_up, w_down,
    )
    outs = pl.pallas_call(
        functools.partial(hand_over, len(shapes)),
        out_shape=shapes,
        in_specs=[hbm] * len(shapes),
        out_specs=(hbm,) * len(shapes),
        scratch_shapes=[pltpu.VMEM(s.shape, s.dtype) for s in shapes] + [dma((2, len(shapes)))],
    )(*outs)
    layer_out, input_grad, grad_query, grad_key, grad_value, grad_out, grad_gate, grad_up, grad_down, g1, g2 = outs
    return (
        layer_out, input_grad, grad_query, grad_key, grad_value, grad_out.T, grad_gate, grad_up, grad_down.T, g1, g2,
    )


def solution(mesh):
    sizes = dict(mesh.shape)
    small = sizes["blk"] == 8 and sizes["tp"] == 4
    placed = (
        P("blk", None),
        P("blk", None),
        P(),
        P(),
        P(None, "tp"),
        P(None, "tp"),
        P(None, "tp"),
        P("tp", None),
        P(),
        P(None, "tp"),
        P(None, "tp"),
        P("tp", None),
    )
    return jax.shard_map(
        kernel_shards if small else shards,
        mesh=mesh,
        in_specs=placed,
        out_specs=(
            P("blk", None),
            P("blk", None),
            P("blk", "tp"),
            P("blk", "tp"),
            P("blk", "tp"),
            P("tp", "blk"),
            P("blk", "tp"),
            P("blk", "tp"),
            P("tp", "blk"),
            P("blk"),
            P("blk"),
        ),
        check_vma=False,
    )
```
